32 devices in a mesh: tracer: 2 (over y), gx: 4 (over x, core), gy: 4 (over z).
Axes of the slice: x: 2, y: 2, z: 4, core: 2. Of those that a mesh axis runs over, the one named last changes fastest.
Arguments:
- tracers: float32 [24, 16, 32, 512], P('tracer', None, 'gx', 'gy'), may hold values from 0.05 to 2
- fluxes: float32 [3, 16, 32, 512], P(None, 'tracer', 'gx', 'gy'), may hold values from -0.15 to 0.15
- diff_east: float32 [32, 512], P('gx', 'gy'), may hold values from 0.01 to 0.1
- diff_north: float32 [32, 512], P('gx', 'gy'), may hold values from 0.01 to 0.1
- column_depth: int32 [32, 512], P('gx', 'gy'), may hold values from 0 to 16
- grazers: float32 [16, 32, 512], P(None, 'gx', 'gy'), may hold values from 0.2 to 0.9
- groups: int32 [24], P('tracer'), may hold values from 0 to 15
- preference: float32 [16], replicated, may hold values from 0.1 to 1
Outputs:
- advanced: float32 [24, 16, 32, 512], P('tracer', None, 'gx', 'gy')
The draws below stay inside these ranges and needn't reach their ends.
Inputs may be any that keep to these rules, and one draw needn't show every extreme that they name: A cell at level k is sea iff k < column_depth of its column.
All inputs are finite; a program needn't handle non-finite values.
Results may differ from the reference program's by a relative error of at most 0.0003.
Values sent between devices are 32-bit elements; how exact they have to be, the bound alone decides.
No kernel may reach another device: no remote copies, remote signals or barrier semaphores. Data moves between devices by JAX's collectives and lax.ppermute only.
A program may use at most 64 MiB of HBM per device.

```python
import math
import jax
import jax.numpy as jnp
from jax import lax

GROUPS = 16
LEV = 16
STEPS = 2
TRACERS = 24
NX = 32
NY = 512


def place_ends(result, stream_key, low, top_value):
    shape = result.shape
    place = [jax.random.randint(jax.random.fold_in(stream_key, axis), (), 0, shape[axis]) for axis in range(len(shape))]
    result = result.at[tuple(place)].set(low)
    longest = shape.index(max(shape))
    place[longest] = (place[longest] + 1) % shape[longest]
    return result.at[tuple(place)].set(top_value)


def block_scale(own_key, shape, shards, low, largest):
    factor_of = 1.0
    for axis_at, shards_of in shards:
        steps = jax.random.uniform(jax.random.fold_in(jax.random.fold_in(own_key, 6), axis_at), (shards_of,), jnp.float32, low / len(shards), largest / len(shards))
        factor_of = factor_of * jnp.repeat(jnp.exp(steps), shape[axis_at] // shards_of).reshape((-1,) + (1,) * (len(shape) - 1 - axis_at))
    return factor_of


def setup_inputs(seed: int = 0) -> dict:
    splits = jax.random.split(jax.random.key(seed), 9)
    return {
        "tracers": jnp.clip(jnp.exp(math.log(2.0) - 3.6888794 * jax.random.uniform(splits[0], (TRACERS, LEV, NX, NY), jnp.float32) ** block_scale(splits[0], (TRACERS, LEV, NX, NY), ((0, 2), (2, 4), (3, 4)), -0.2, 0.2)), 0.05, 2.0),
        "fluxes": jnp.clip(jax.random.uniform(splits[1], (3, LEV, NX, NY), jnp.float32, -0.15, 0.15) * block_scale(splits[1], (3, LEV, NX, NY), ((1, 2), (2, 4), (3, 4)), -0.4, 0.0), -0.15, 0.15),
        "diff_east": jnp.clip(jnp.exp(math.log(0.1) - 2.3025851 * jax.random.uniform(splits[2], (NX, NY), jnp.float32) ** block_scale(splits[2], (NX, NY), ((0, 4), (1, 4)), -0.2, 0.2)), 0.01, 0.1),
        "diff_north": jnp.clip(jnp.exp(math.log(0.1) - 2.3025851 * jax.random.uniform(splits[3], (NX, NY), jnp.float32) ** block_scale(splits[3], (NX, NY), ((0, 4), (1, 4)), -0.2, 0.2)), 0.01, 0.1),
        "column_depth": place_ends(jax.random.randint(splits[4], (NX, NY), 0, LEV + 1), jax.random.fold_in(splits[4], 1), 0, LEV).astype(jnp.int32),
        "grazers": jnp.clip(jnp.exp(math.log(0.9) - 1.50407736 * jax.random.uniform(splits[5], (LEV, NX, NY), jnp.float32) ** block_scale(splits[5], (LEV, NX, NY), ((1, 4), (2, 4)), -0.2, 0.2)), 0.2, 0.9),
        "groups": place_ends(jax.random.randint(splits[6], (TRACERS,), 0, GROUPS), jax.random.fold_in(splits[6], 1), 0, GROUPS - 1).astype(jnp.int32),
        "preference": jnp.clip(jnp.exp(jax.random.uniform(splits[7], (GROUPS,), jnp.float32, math.log(0.1), math.log(1.0))), 0.1, 1.0),
    }


def minmod(jump_low, jump_high):
    return jnp.maximum(0.0, jnp.minimum(jump_low, jump_high)) + jnp.minimum(0.0, jnp.maximum(jump_low, jump_high))


def window(values, low_end, high_end, direction):
    return lax.slice_in_dim(values, low_end, high_end, axis=direction % values.ndim)


def face_terms(tracer_field, open_faces, face_flux, face_kappa, direction):
    length = tracer_field.shape[direction % tracer_field.ndim] - 4
    jump_face = open_faces * (window(tracer_field, 1, length + 4, direction) - window(tracer_field, 0, length + 3, direction))
    slopes = minmod(window(jump_face, 0, length + 2, direction), window(jump_face, 1, length + 3, direction))
    left_value = window(tracer_field, 1, length + 2, direction) + 0.5 * window(slopes, 0, length + 1, direction)
    right_value = window(tracer_field, 2, length + 3, direction) - 0.5 * window(slopes, 1, length + 2, direction)
    carried = face_flux * jnp.where(face_flux > 0.0, left_value, right_value)
    if face_kappa is not None:
        carried = carried - face_kappa * window(jump_face, 1, length + 2, direction)
    return window(carried, 0, length, direction) - window(carried, 1, length + 1, direction)


def reference(tracers, fluxes, diff_east, diff_north, column_depth, grazers, groups, preference):
    level_index = lax.broadcasted_iota(jnp.int32, (LEV, NX, NY), 0)
    wet_cells = (level_index < column_depth[None]).astype(jnp.float32)
    wet_padded = jnp.pad(wet_cells, 2)
    open_x = wet_padded[2:-2, :-1, 2:-2] * wet_padded[2:-2, 1:, 2:-2]
    open_y = wet_padded[2:-2, 2:-2, :-1] * wet_padded[2:-2, 2:-2, 1:]
    open_z = wet_padded[:-1, 2:-2, 2:-2] * wet_padded[1:, 2:-2, 2:-2]
    flux_x = jnp.pad(fluxes[0], ((0, 0), (1, 0), (0, 0))) * open_x[:, 1:NX + 2]
    kappa_x = jnp.pad(diff_east, ((1, 0), (0, 0)))[None] * open_x[:, 1:NX + 2]
    flux_y = jnp.pad(fluxes[1], ((0, 0), (0, 0), (1, 0))) * open_y[:, :, 1:NY + 2]
    kappa_y = jnp.pad(diff_north, ((0, 0), (1, 0)))[None] * open_y[:, :, 1:NY + 2]
    flux_z = jnp.pad(fluxes[2], ((1, 0), (0, 0), (0, 0))) * open_z[1:LEV + 2]
    group_match = (groups[:, None] == lax.broadcasted_iota(jnp.int32, (1, GROUPS), 1)).astype(jnp.float32)
    grazing_pref = jnp.sum(group_match * preference[None, :], axis=1)
    tracer_field = tracers
    for step_index in range(STEPS):
        prey_total = jnp.einsum("t,tlxy->lxy", grazing_pref, tracer_field)
        factor = grazers / (1.0 + 4.0 * prey_total / TRACERS)

        def advance_tracer(items):
            single, pref_one = items
            tendency = face_terms(jnp.pad(single, ((0, 0), (2, 2), (0, 0))), open_x, flux_x, kappa_x, -2)
            tendency = tendency + face_terms(jnp.pad(single, ((0, 0), (0, 0), (2, 2))), open_y, flux_y, kappa_y, -1)
            tendency = tendency + face_terms(jnp.pad(single, ((2, 2), (0, 0), (0, 0))), open_z, flux_z, None, -3)
            return single + tendency - (pref_one * factor) * single

        tracer_field = lax.map(advance_tracer, (tracer_field, grazing_pref))
    return tracer_field
```

```python
import functools

import jax
import jax.numpy as jnp
from jax import lax
from jax.experimental import pallas as pl
from jax.experimental.pallas import tpu as pltpu
from jax.sharding import PartitionSpec as P

STEPS = 2
SUB = 8
LIM = 48 * 1024 * 1024


def with_halo(cells, sides, width):
    for axis, dim in sides:
        count = lax.axis_size(axis)
        ends = count - 1
        head = lax.slice_in_dim(cells, 0, width, axis=dim)
        tail = lax.slice_in_dim(cells, cells.shape[dim] - width, cells.shape[dim], axis=dim)
        cells = jnp.concatenate(
            [
                lax.ppermute(tail, axis, [(i, (i + 1) % count) for i in range(ends)]),
                cells,
                lax.ppermute(head, axis, [((i + 1) % count, i) for i in range(ends)]),
            ],
            axis=dim,
        )
    return cells


def minmod(jump_low, jump_high):
    return jnp.maximum(0.0, jnp.minimum(jump_low, jump_high)) + jnp.minimum(
        0.0, jnp.maximum(jump_low, jump_high)
    )


def window(values, low_end, high_end, direction):
    return lax.slice_in_dim(values, low_end, high_end, axis=direction % values.ndim)


def face_terms(tracer_field, open_faces, face_flux, face_kappa, direction):
    length = tracer_field.shape[direction % tracer_field.ndim] - 4
    jump_face = open_faces * (
        window(tracer_field, 1, length + 4, direction)
        - window(tracer_field, 0, length + 3, direction)
    )
    slopes = minmod(
        window(jump_face, 0, length + 2, direction), window(jump_face, 1, length + 3, direction)
    )
    left_value = window(tracer_field, 1, length + 2, direction) + 0.5 * window(
        slopes, 0, length + 1, direction
    )
    right_value = window(tracer_field, 2, length + 3, direction) - 0.5 * window(
        slopes, 1, length + 2, direction
    )
    carried = face_flux * jnp.where(face_flux > 0.0, left_value, right_value)
    if face_kappa is not None:
        carried = carried - face_kappa * window(jump_face, 1, length + 2, direction)
    return window(carried, 0, length, direction) - window(carried, 1, length + 1, direction)


def plain(tracers, fluxes, diff_east, diff_north, column_depth, grazers, groups, preference):
    tr_dev, levels, rows_dev, cols_dev = tracers.shape
    total_tracers = tr_dev * lax.axis_size("tracer")
    level_index = lax.broadcasted_iota(jnp.int32, (levels, rows_dev, cols_dev), 0)
    wet_cells = (level_index < column_depth[None]).astype(jnp.float32)
    all_fluxes = lax.all_gather(fluxes, "tracer", axis=1, tiled=True)
    stacked = jnp.concatenate(
        [all_fluxes[0], all_fluxes[1], wet_cells, diff_east[None], diff_north[None]], 0
    )
    rimmed = with_halo(stacked, (("gx", 1), ("gy", 2)), 2)
    east_ext = rimmed[:levels]
    north_ext = rimmed[levels : 2 * levels]
    downward = all_fluxes[2]
    wet_ext = rimmed[-(levels + 2) : -2]
    kx_ext = rimmed[-2]
    ky_ext = rimmed[-1]
    open_x = wet_ext[:, :-1, 2:-2] * wet_ext[:, 1:, 2:-2]
    open_y = wet_ext[:, 2:-2, :-1] * wet_ext[:, 2:-2, 1:]
    flux_x = east_ext[:, 1 : rows_dev + 2, 2:-2] * open_x[:, 1 : rows_dev + 2]
    kappa_x = kx_ext[None, 1 : rows_dev + 2, 2:-2] * open_x[:, 1 : rows_dev + 2]
    flux_y = north_ext[:, 2:-2, 1 : cols_dev + 2] * open_y[:, :, 1 : cols_dev + 2]
    kappa_y = ky_ext[None, 2:-2, 1 : cols_dev + 2] * open_y[:, :, 1 : cols_dev + 2]
    wet_z = jnp.pad(wet_cells, ((2, 2), (0, 0), (0, 0)))
    open_z = wet_z[:-1] * wet_z[1:]
    flux_z = jnp.pad(downward, ((1, 0), (0, 0), (0, 0))) * open_z[1 : levels + 2]
    group_match = (
        groups[:, None] == lax.broadcasted_iota(jnp.int32, (1, preference.shape[0]), 1)
    ).astype(jnp.float32)
    grazing_pref = jnp.sum(group_match * preference[None, :], axis=1)
    tracer_field = tracers
    for step_index in range(STEPS):
        prey_local = jnp.sum(grazing_pref[:, None, None, None] * tracer_field, axis=0)
        prey_total = lax.psum(prey_local, "tracer")
        factor = grazers / (1.0 + 4.0 * prey_total / total_tracers)
        extended = with_halo(tracer_field, (("gx", 2), ("gy", 3)), 2)
        tendency = face_terms(extended[:, :, :, 2:-2], open_x, flux_x, kappa_x, -2)
        tendency = tendency + face_terms(extended[:, :, 2:-2, :], open_y, flux_y, kappa_y, -1)
        padded_z = jnp.pad(tracer_field, ((0, 0), (2, 2), (0, 0), (0, 0)))
        tendency = tendency + face_terms(padded_z, open_z, flux_z, None, -3)
        tracer_field = (
            tracer_field + tendency - grazing_pref[:, None, None, None] * factor * tracer_field
        )
    return tracer_field


class Geo:
    def __init__(self, tr_dev, levels, rows, cols):
        self.T, self.L, self.R, self.C = tr_dev, levels, rows, cols
        self.LH = levels // SUB
        self.tile = rows * levels
        self.slots = -(-(tr_dev + 3) // 4) * 4
        self.slots2 = -(-tr_dev // 4) * 4
        at = 0
        self.off = {}
        for name, count in (
            ("hx", (rows + 3) * levels),
            ("px", (rows + 1) * levels),
            ("mx", (rows + 1) * levels),
            ("kx", (rows + 1) * SUB),
            ("hy", self.tile),
            ("py", self.tile),
            ("my", self.tile),
            ("ky", rows * SUB),
            ("hz", self.tile),
            ("pz", self.tile),
            ("mz", self.tile),
            ("hs", SUB),
            ("ps", SUB),
            ("ms", SUB),
            ("ks", SUB),
        ):
            self.off[name] = at
            at += count
        self.coefs = at


def lanes(shape=(SUB, 128)):
    return lax.broadcasted_iota(jnp.int32, shape, 1)


def sublanes(shape=(SUB, 128)):
    return lax.broadcasted_iota(jnp.int32, shape, 0)


def roll(v, by, axis):
    by = by % v.shape[axis]
    return v if by == 0 else pltpu.roll(v, by, axis)


def pack_strips(parts):
    lane = lanes()
    packed = jnp.zeros((SUB, 128), jnp.float32)
    for k, part in enumerate(parts):
        inside = (lane >= 8 * k + 2) & (lane < 8 * k + 6)
        packed = jnp.where(inside, roll(part, 8 * k + 4, 1), packed)
    return packed


def message_strips(packed, low):
    place = lanes() % 8
    out = jnp.zeros((SUB, 128), jnp.float32)
    for m, one in enumerate(packed):
        moved = roll(one, 2 * m - (4 if low else 2), 1)
        out = jnp.where((place == 2 * m) | (place == 2 * m + 1), moved, out)
    return out


def full_strips(own, from_lower, from_upper, m):
    place = lanes() % 8
    out = jnp.where(place < 2, roll(from_lower, -2 * m, 1), roll(from_upper, 6 - 2 * m, 1))
    out = jnp.where((place >= 2) & (place < 4), roll(own, -2, 1), out)
    return jnp.where((place >= 4) & (place < 6), roll(own, 2, 1), out)


def taste_of(groups_ref, pref_ref, t):
    return pref_ref[groups_ref[t]]


def is_even(axis):
    return lax.rem(lax.axis_index(axis), 2) == 0


def edges_kernel(g, fluxes_ref, out_ref):
    base = g.R * SUB
    out_ref[0:SUB, :] = fluxes_ref[pl.ds(g.R - 1, SUB, stride=g.R), :]
    parts = []
    for r in range(g.R):
        row = fluxes_ref[pl.ds(base + r, SUB, stride=g.R), :]
        parts += [row] * g.LH
    out_ref[SUB : 2 * SUB, :] = pack_strips(parts)


def load_kernel(g, tracers_ref, groups_ref, pref_ref, field_ref, strips_ref, prey_ref):
    def one(t, carry):
        taste = taste_of(groups_ref, pref_ref, t)
        base = pl.multiple_of(t * g.tile, g.tile)
        parts = []
        for r in range(g.R):
            for lh in range(g.LH):
                at = (r * g.LH + lh) * SUB
                v = tracers_ref[pl.ds(base + lh * SUB * g.R + r, SUB, stride=g.R), :]
                field_ref[pl.ds(base + at, SUB), :] = v
                parts.append(v)
                prey_ref[at : at + SUB, :] += taste * v
        strips_ref[pl.ds(pl.multiple_of(t * SUB, SUB), SUB), :] = pack_strips(parts)
        return carry

    prey_ref[...] = jnp.zeros_like(prey_ref)
    lax.fori_loop(0, g.T, one, 0)


def first_messages_kernel(
    g, field_ref, strips_ref, mine_ref, other_ref, depth_ref, east_ref, north_ref,
    xev_ref, xod_ref, yev_ref, yod_ref,
):
    x_even, y_even = is_even("gx"), is_even("gy")
    first = lax.axis_index("tracer") == 0
    single = lax.axis_size("tracer") != 2
    zero = jnp.zeros((SUB, 128), jnp.float32)

    def put(ref_ev, ref_od, at, even, low, high):
        ref_ev[at, :] = jnp.where(even, high, low)
        ref_od[at, :] = jnp.where(even, low, high)

    def one(t, carry):
        base = pl.multiple_of(t * g.tile, g.tile)
        for i in range(2 * g.LH):
            low = field_ref[pl.ds(base + i * SUB, SUB), :]
            high = field_ref[pl.ds(base + g.tile - 2 * g.L + i * SUB, SUB), :]
            at = pl.ds(pl.multiple_of(t * 2 * g.L, SUB) + i * SUB, SUB)
            put(xev_ref, xod_ref, at, x_even, low, high)
        return carry

    lax.fori_loop(0, g.T, one, 0)
    mine, other = mine_ref[...], other_ref[...]
    lower = mine if single else jnp.where(first, mine, other)
    upper = other if single else jnp.where(first, other, mine)
    at = g.T * 2 * g.L
    for lh, half in enumerate((lower, upper)):
        put(xev_ref, xod_ref, slice(at, at + SUB), x_even, zero, half[0:SUB])
        at += SUB
    depth = depth_ref[...].astype(jnp.float32)
    put(xev_ref, xod_ref, slice(at, at + SUB), x_even, depth, roll(depth, 2, 0))
    at += SUB
    put(xev_ref, xod_ref, slice(at, at + SUB), x_even, zero, roll(east_ref[...], 1, 0))

    half_of = (lanes() // 8) % g.LH
    packed = [strips_ref[t * SUB : (t + 1) * SUB, :] for t in range(g.T)]
    packed.append(pack_strips(spread_rows(g, depth)))
    packed.append(jnp.where(half_of == 0, lower[SUB : 2 * SUB], upper[SUB : 2 * SUB]))
    packed.append(pack_strips(spread_rows(g, north_ref[...])))
    for v in range(0, len(packed), 4):
        low = message_strips(packed[v : v + 4], True)
        high = message_strips(packed[v : v + 4], False)
        put(yev_ref, yod_ref, slice(v * 2, v * 2 + SUB), y_even, low, high)


def spread_rows(g, rows):
    parts = []
    for r in range(g.R):
        parts += [jnp.broadcast_to(rows[r : r + 1, :], (SUB, 128))] * g.LH
    return parts


def coefficients(
    g, cf, xl, yl, yu, mine_ref, other_ref, fluxes_mine, fluxes_other, depth_ref, east_ref, north_ref
):
    lane, sub = lanes(), sublanes()
    first = lax.axis_index("tracer") == 0
    single = lax.axis_size("tracer") != 2
    depth = depth_ref[...].astype(jnp.float32)
    depth_low, depth_high = xl(g.LH)
    east = east_ref[...]
    east_low, _ = xl(g.LH + 1)
    north = north_ref[...]
    level = [(sub + SUB * lh).astype(jnp.float32) for lh in range(g.LH)]

    def spread(rows, r):
        return jnp.broadcast_to(rows[r : r + 1, :], (SUB, 128))

    depths = [spread(depth_low, 0), spread(depth_low, 1)]
    depths += [spread(depth, r) for r in range(g.R)]
    depths += [spread(depth_high, 0), spread(depth_high, 1)]
    wet = [[level[lh] < d for lh in range(g.LH)] for d in depths]

    def flux(dim, r, lh):
        at = pl.ds(dim * g.R * SUB + r, SUB, stride=g.R)
        a, b = fluxes_mine[at, :], fluxes_other[at, :]
        if single:
            return (a, b)[lh]
        return jnp.where(first, (a, b)[lh], (b, a)[lh])

    def store(name, index, value):
        at = g.off[name] + index * SUB
        cf[at : at + SUB, :] = value

    def put(name, index, opened, h, f):
        f = jnp.where(opened, f, 0.0)
        store("h" + name, h, jnp.where(opened, 0.5, 0.0))
        store("p" + name, index, jnp.maximum(f, 0.0))
        store("m" + name, index, jnp.minimum(f, 0.0))

    for f in range(-1, g.R + 2):
        for lh in range(g.LH):
            opened = wet[f + 1][lh] & wet[f + 2][lh]
            h = (f + 1) * g.LH + lh
            if 0 <= f <= g.R:
                below = xl(lh)[0] if f == 0 else flux(0, f - 1, lh)
                put("x", f * g.LH + lh, opened, h, below)
            else:
                store("hx", h, jnp.where(opened, 0.5, 0.0))
        if 0 <= f <= g.R:
            store("kx", f, 2.0 * (spread(east_low, 0) if f == 0 else spread(east, f - 1)))

    for r in range(g.R):
        before = roll(depths[r + 2], 1, 1)
        store("ky", r, 2.0 * roll(spread(north, r), 1, 1))
        for lh in range(g.LH):
            k = r * g.LH + lh
            here = wet[r + 2][lh]
            opened = here & (level[lh] < before) & (lane > 0)
            put("y", k, opened, k, roll(flux(1, r, lh), 1, 1))
        flux_z = [roll(flux(2, r, lh), 1, 0) for lh in range(g.LH)]
        for lh in range(g.LH):
            k = r * g.LH + lh
            here = wet[r + 2][lh]
            above = flux_z[lh] if lh == 0 else jnp.where(sub == 0, flux_z[lh - 1], flux_z[lh])
            opened = here if lh else here & (sub > 0)
            put("z", k, opened, k, above)

    place = lane % 8
    half_of = (lane // 8) % g.LH
    mine, other = mine_ref[SUB : 2 * SUB, :], other_ref[SUB : 2 * SUB, :]
    lower = mine if single else jnp.where(first, mine, other)
    upper = other if single else jnp.where(first, other, mine)
    own = (
        pack_strips(spread_rows(g, depth)),
        jnp.where(half_of == 0, lower, upper),
        pack_strips(spread_rows(g, north)),
    )
    full = []
    for i, one in enumerate(own):
        slot = g.T + i
        full.append(full_strips(one, yl(slot // 4), yu(slot // 4), slot % 4))
    wet_s = (sub + SUB * half_of).astype(jnp.float32) < full[0]
    opened = jnp.where(wet_s, 1.0, 0.0) * roll(jnp.where(wet_s, 1.0, 0.0), 1, 1)
    opened = (opened > 0.0) & (place != 0) & (place != 4)
    put("s", 0, opened, 0, roll(full[1], 1, 1))
    store("ks", 0, 2.0 * roll(full[2], 1, 1))


def limited(a, b):
    least, most = jnp.minimum(a, b), jnp.maximum(a, b)
    return jnp.maximum(least, jnp.minimum(most, 0.0))


def advance(g, cf, strip_fix, at_row, taste, factor, emit):
    lane, sub = lanes(), sublanes()
    ends = (lane == 0) | (lane == 127)
    top, bottom = sub == 0, sub == SUB - 1

    def coef(name, index):
        at = g.off[name] + index * SUB
        return cf[at : at + SUB, :]

    slope_fix, carried_fix = strip_fix
    before = {}
    cell, jump_next, right, carried = {}, {}, {}, {}
    for lh in range(g.LH):
        c2, c1, c0 = at_row(-2, lh), at_row(-1, lh), at_row(0, lh)
        j1 = coef("hx", lh) * (c1 - c2)
        j0 = coef("hx", g.LH + lh) * (c0 - c1)
        s1 = limited(j1, j0)
        cell[lh], jump_next[lh] = c0, j0
        before[lh] = c1 + s1

    def x_face(f, lh, left, right, jump):
        k = f * g.LH + lh
        return coef("px", k) * left + coef("mx", k) * right - coef("kx", f) * jump

    for r in range(g.R):
        news = []
        here = [cell[lh] for lh in range(g.LH)]
        for lh in range(g.LH):
            k = r * g.LH + lh
            c = cell[lh]
            up = at_row(r + 1, lh)
            j_low = jump_next[lh]
            j_up = coef("hx", (r + 2) * g.LH + lh) * (up - c)
            s = limited(j_low, j_up)
            if r == 0:
                carried[lh] = x_face(0, lh, before[lh], c - s, j_low)
            left = c + s
            up2 = at_row(r + 2, lh)
            j_up2 = coef("hx", (r + 3) * g.LH + lh) * (up2 - up)
            s_up = limited(j_up, j_up2)
            out = x_face(r + 1, lh, left, up - s_up, j_up)
            new = c + (carried[lh] - out)
            carried[lh], cell[lh], jump_next[lh] = out, up, j_up
            j = coef("hy", k) * (c - roll(c, 1, 1))
            s = limited(j, roll(j, -1, 1))
            s = jnp.where(ends, roll(slope_fix, -(8 * k + 2), 1), s)
            flow = coef("py", k) * roll(c + s, 1, 1) + coef("my", k) * (c - s)
            flow = flow - coef("ky", r) * j
            new = new + (flow - roll(flow, -1, 1))
            new = new + jnp.where(ends, roll(carried_fix, -(8 * k + 2), 1), 0.0)
            at = k * SUB
            new = new - (taste * factor[at : at + SUB, :]) * c
            news.append(new)
        def shift_down(v):
            rolled = [roll(x, 1, 0) for x in v]
            return [rolled[0]] + [
                jnp.where(top, rolled[i - 1], rolled[i]) for i in range(1, g.LH)
            ]

        def shift_up(v):
            rolled = [roll(x, -1, 0) for x in v]
            return [
                jnp.where(bottom, rolled[(i + 1) % g.LH], rolled[i]) for i in range(g.LH)
            ]

        index = [r * g.LH + lh for lh in range(g.LH)]
        above = shift_down(here)
        j = [coef("hz", k) * (c - a) for k, c, a in zip(index, here, above)]
        s = [limited(a, b) for a, b in zip(j, shift_up(j))]
        left = shift_down([c + v for c, v in zip(here, s)])
        flow = [
            coef("pz", k) * a + coef("mz", k) * (c - v)
            for k, a, c, v in zip(index, left, here, s)
        ]
        for lh, (a, b, new) in enumerate(zip(flow, shift_up(flow), news)):
            emit(r, lh, new + (a - b))


def strip_fixes(g, cf, full):
    def coef(name):
        return cf[g.off[name] : g.off[name] + SUB, :]

    at_two = lanes() % 8 == 2
    j = coef("hs") * (full - roll(full, 1, 1))
    s = limited(j, roll(j, -1, 1))
    flow = coef("ps") * roll(full + s, 1, 1) + coef("ms") * (full - s) - coef("ks") * j
    return jnp.where(at_two, s, roll(s, -4, 1)), jnp.where(at_two, flow, -roll(flow, -5, 1))


def split_sides(even, ev, od):
    return jnp.where(even, od, ev), jnp.where(even, ev, od)


def set_factor(g, total, factor, grazers_ref, mine_ref, others, scale_rows=0):
    for r in range(g.R):
        for lh in range(g.LH):
            at = (r * g.LH + lh) * SUB
            prey = mine_ref[at : at + SUB, :]
            for ref in others:
                prey = prey + ref[scale_rows + at : scale_rows + at + SUB, :]
            grazers = grazers_ref[pl.ds(lh * SUB * g.R + r, SUB, stride=g.R), :]
            factor[at : at + SUB, :] = grazers / (1.0 + 4.0 * prey / total)


def rows_of(g, field_ref, xev_ref, xod_ref, x_even, t):
    base = pl.multiple_of(t * g.tile, g.tile)
    halo = pl.multiple_of(t * 2 * g.L, 2 * g.L)
    seen = {}

    def at_row(r, lh):
        if (r, lh) not in seen:
            if 0 <= r < g.R:
                seen[r, lh] = field_ref[pl.ds(base + r * g.L + lh * SUB, SUB), :]
            else:
                i = r + 2 if r < 0 else r - g.R
                at = pl.ds(halo + i * g.L + lh * SUB, SUB)
                low, high = split_sides(x_even, xev_ref[at, :], xod_ref[at, :])
                seen[r, lh] = low if r < 0 else high
        return seen[r, lh]

    return at_row


def y_sides(y_even, yev_ref, yod_ref, v):
    at = pl.ds(v * SUB, SUB)
    return split_sides(y_even, yev_ref[at, :], yod_ref[at, :])


def unpack_strips(g, strips_ref, yev_ref, yod_ref, y_even, full_ref):
    for t in range(g.T):
        low, high = y_sides(y_even, yev_ref, yod_ref, t // 4)
        full_ref[t * SUB : (t + 1) * SUB, :] = full_strips(
            strips_ref[t * SUB : (t + 1) * SUB, :], low, high, t % 4
        )


def step_one_kernel(
    g, total, n_other,
    field_ref, strips_ref, xev_ref, xod_ref, yev_ref, yod_ref, mine_ref, other_ref,
    bulk_ref, depth_ref, east_ref, north_ref, grazers_ref, groups_ref, pref_ref, *rest,
):
    others, rest = rest[:n_other], rest[n_other:]
    (out_ref, xev2_ref, xod2_ref, yev2_ref, yod2_ref, strips2_ref, prey2_ref, cf,
     factor, full_ref) = rest
    x_even, y_even = is_even("gx"), is_even("gy")
    prey_rows = 3 * g.R * SUB

    def xl(i):
        at = pl.ds(g.T * 2 * g.L + i * SUB, SUB)
        return split_sides(x_even, xev_ref[at, :], xod_ref[at, :])

    coefficients(
        g, cf, xl,
        lambda v: y_sides(y_even, yev_ref, yod_ref, v)[0],
        lambda v: y_sides(y_even, yev_ref, yod_ref, v)[1],
        mine_ref, other_ref, bulk_ref, others[0], depth_ref, east_ref, north_ref,
    )
    set_factor(
        g, total, factor, grazers_ref, bulk_ref.at[prey_rows : prey_rows + g.tile], others[-1:], prey_rows
    )
    unpack_strips(g, strips_ref, yev_ref, yod_ref, y_even, full_ref)
    prey2_ref[...] = jnp.zeros_like(prey2_ref)

    def one(t, carry):
        taste = taste_of(groups_ref, pref_ref, t)
        base = pl.multiple_of(t * g.tile, g.tile)
        halo = pl.multiple_of(t * 2 * g.L, 2 * g.L)
        strip_at = pl.ds(pl.multiple_of(t * SUB, SUB), SUB)
        news = {}

        def emit(r, lh, new):
            at = (r * g.LH + lh) * SUB
            out_ref[pl.ds(base + at, SUB), :] = new
            prey2_ref[at : at + SUB, :] += taste * new
            news[r, lh] = new

        advance(
            g, cf, strip_fixes(g, cf, full_ref[strip_at, :]),
            rows_of(g, field_ref, xev_ref, xod_ref, x_even, t), taste, factor, emit,
        )
        for i in range(2):
            for lh in range(g.LH):
                at = pl.ds(halo + i * g.L + lh * SUB, SUB)
                low, high = news[i, lh], news[g.R - 2 + i, lh]
                xev2_ref[at, :] = jnp.where(x_even, high, low)
                xod2_ref[at, :] = jnp.where(x_even, low, high)
        strips2_ref[strip_at, :] = pack_strips(
            [news[r, lh] for r in range(g.R) for lh in range(g.LH)]
        )
        return carry

    lax.fori_loop(0, g.T, one, 0)
    packed = [strips2_ref[t * SUB : (t + 1) * SUB, :] for t in range(g.T)]
    for v in range(0, g.T, 4):
        low = message_strips(packed[v : v + 4], True)
        high = message_strips(packed[v : v + 4], False)
        yev2_ref[v * 2 : v * 2 + SUB, :] = jnp.where(y_even, high, low)
        yod2_ref[v * 2 : v * 2 + SUB, :] = jnp.where(y_even, low, high)


def step_two_kernel(
    g, total, n_other,
    field_ref, strips_ref, xev_ref, xod_ref, yev_ref, yod_ref, prey_ref, cf,
    grazers_ref, groups_ref, pref_ref, *rest,
):
    others, (out_ref, factor, full_ref) = rest[:n_other], rest[n_other:]
    x_even, y_even = is_even("gx"), is_even("gy")
    set_factor(g, total, factor, grazers_ref, prey_ref, others)
    unpack_strips(g, strips_ref, yev_ref, yod_ref, y_even, full_ref)

    def one(t, carry):
        taste = taste_of(groups_ref, pref_ref, t)
        base = pl.multiple_of(t * g.tile, g.tile)
        strip_at = pl.ds(pl.multiple_of(t * SUB, SUB), SUB)

        def emit(r, lh, new):
            out_ref[pl.ds(base + lh * SUB * g.R + r, SUB, stride=g.R), :] = new

        advance(
            g, cf, strip_fixes(g, cf, full_ref[strip_at, :]),
            rows_of(g, field_ref, xev_ref, xod_ref, x_even, t), taste, factor, emit,
        )
        return carry

    lax.fori_loop(0, g.T, one, 0)


def call(body, outs, operands, scalars=(), scratch=()):
    vmem, smem = pl.BlockSpec(memory_space=pltpu.VMEM), pl.BlockSpec(memory_space=pltpu.SMEM)
    return pl.pallas_call(
        body,
        out_shape=[jax.ShapeDtypeStruct((rows, 128), jnp.float32) for rows in outs],
        in_specs=[smem if i in scalars else vmem for i in range(len(operands))],
        out_specs=[vmem] * len(outs),
        scratch_shapes=[pltpu.VMEM((rows, 128), jnp.float32) for rows in scratch],
        compiler_params=pltpu.CompilerParams(vmem_limit_bytes=LIM),
    )(*operands)


def pair_swap(values, axis, start):
    pairs = []
    for i in range(start, lax.axis_size(axis) - 1, 2):
        pairs += [(i, i + 1), (i + 1, i)]
    if not pairs:
        return jnp.zeros_like(values)
    return lax.ppermute(values, axis, pairs)


def tracer_swap(values):
    return lax.ppermute(values, "tracer", [(0, 1), (1, 0)])


def neighbours(x_ev, x_od, y_ev, y_od):
    x_od = pair_swap(x_od, "gx", 1)
    y_ev = pair_swap(y_ev, "gy", 0)
    y_od = pair_swap(y_od, "gy", 1)
    x_ev = pair_swap(x_ev, "gx", 0)
    return x_ev, x_od, y_ev, y_od


def on_device(tracers, fluxes, diff_east, diff_north, column_depth, grazers, groups, preference):
    tr_dev, levels, rows, cols = tracers.shape
    parts = lax.axis_size("tracer")
    if not (cols == 128 and rows * levels == cols and levels == 2 * SUB and rows % SUB == 0):
        return plain(
            tracers, fluxes, diff_east, diff_north, column_depth, grazers, groups, preference
        )
    g = Geo(tr_dev, levels, rows, cols)
    total = float(tr_dev * parts)
    pair = parts == 2
    flat = tracers.reshape(-1, cols)
    grazers = grazers.reshape(-1, cols)

    if pair:
        halves = [fluxes.reshape(-1, cols)]
    else:
        gathered = lax.all_gather(fluxes, "tracer", axis=1, tiled=True)
        halves = [gathered[:, i : i + SUB].reshape(-1, cols) for i in (0, SUB)]
    edges = [call(functools.partial(edges_kernel, g), [2 * SUB], [half])[0] for half in halves]
    if pair:
        edges.append(tracer_swap(edges[0]))
    field, strips, prey = call(
        functools.partial(load_kernel, g),
        [g.T * g.tile, g.T * SUB, g.tile],
        [flat, groups, preference],
        scalars=(1, 2),
    )
    if pair:
        bulk = jnp.concatenate([halves[0], prey])
        others = [tracer_swap(bulk)]
    else:
        bulk = jnp.concatenate([halves[0], lax.psum(prey, "tracer")])
        others = [jnp.concatenate([halves[1], jnp.zeros_like(prey)])]

    x_rows = g.T * 2 * g.L + g.L + 2 * SUB
    messages = call(
        functools.partial(first_messages_kernel, g),
        [x_rows, x_rows, g.slots * 2, g.slots * 2],
        [field, strips, *edges, column_depth, diff_east, diff_north],
    )
    messages = neighbours(*messages)
    x_rows = g.T * 2 * g.L
    *results, coefs = call(
        functools.partial(step_one_kernel, g, total, len(others)),
        [g.T * g.tile, x_rows, x_rows, g.slots2 * 2, g.slots2 * 2, g.T * SUB, g.tile, g.coefs],
        [field, strips, *messages, *edges, bulk, column_depth, diff_east, diff_north, grazers,
         groups, preference, *others],
        scalars=(13, 14),
        scratch=[g.tile, g.T * SUB],
    )
    field, *messages, strips, prey = results
    if pair:
        others = [tracer_swap(prey)]
    else:
        prey, others = lax.psum(prey, "tracer"), []
    messages = neighbours(*messages)
    (out,) = call(
        functools.partial(step_two_kernel, g, total, len(others)),
        [g.T * g.tile],
        [field, strips, *messages, prey, coefs, grazers, groups, preference, *others],
        scalars=(9, 10),
        scratch=[g.tile, g.T * SUB],
    )
    return out.reshape(tracers.shape)


def solution(mesh):
    placed = (
        P("tracer", None, "gx", "gy"),
        P(None, "tracer", "gx", "gy"),
        P("gx", "gy"),
        P("gx", "gy"),
        P("gx", "gy"),
        P(None, "gx", "gy"),
        P("tracer"),
        P(),
    )
    return jax.shard_map(
        on_device,
        mesh=mesh,
        in_specs=placed,
        out_specs=P("tracer", None, "gx", "gy"),
        check_vma=False,
    )
```

```python
import functools

import jax
import jax.numpy as jnp
from jax import lax
from jax.experimental import pallas as pl
from jax.experimental.pallas import tpu as pltpu
from jax.sharding import PartitionSpec as P

STEPS = 2
SUB = 8
LIM = 48 * 1024 * 1024
AHEAD = 2


def with_halo(cells, sides, width):
    for axis, dim in sides:
        count = lax.axis_size(axis)
        ends = count - 1
        head = lax.slice_in_dim(cells, 0, width, axis=dim)
        tail = lax.slice_in_dim(cells, cells.shape[dim] - width, cells.shape[dim], axis=dim)
        cells = jnp.concatenate(
            [
                lax.ppermute(tail, axis, [(i, (i + 1) % count) for i in range(ends)]),
                cells,
                lax.ppermute(head, axis, [((i + 1) % count, i) for i in range(ends)]),
            ],
            axis=dim,
        )
    return cells


def minmod(jump_low, jump_high):
    return jnp.maximum(0.0, jnp.minimum(jump_low, jump_high)) + jnp.minimum(
        0.0, jnp.maximum(jump_low, jump_high)
    )


def window(values, low_end, high_end, direction):
    return lax.slice_in_dim(values, low_end, high_end, axis=direction % values.ndim)


def face_terms(tracer_field, open_faces, face_flux, face_kappa, direction):
    length = tracer_field.shape[direction % tracer_field.ndim] - 4
    jump_face = open_faces * (
        window(tracer_field, 1, length + 4, direction)
        - window(tracer_field, 0, length + 3, direction)
    )
    slopes = minmod(
        window(jump_face, 0, length + 2, direction), window(jump_face, 1, length + 3, direction)
    )
    left_value = window(tracer_field, 1, length + 2, direction) + 0.5 * window(
        slopes, 0, length + 1, direction
    )
    right_value = window(tracer_field, 2, length + 3, direction) - 0.5 * window(
        slopes, 1, length + 2, direction
    )
    carried = face_flux * jnp.where(face_flux > 0.0, left_value, right_value)
    if face_kappa is not None:
        carried = carried - face_kappa * window(jump_face, 1, length + 2, direction)
    return window(carried, 0, length, direction) - window(carried, 1, length + 1, direction)


def plain(tracers, fluxes, diff_east, diff_north, column_depth, grazers, groups, preference):
    tr_dev, levels, rows_dev, cols_dev = tracers.shape
    total_tracers = tr_dev * lax.axis_size("tracer")
    level_index = lax.broadcasted_iota(jnp.int32, (levels, rows_dev, cols_dev), 0)
    wet_cells = (level_index < column_depth[None]).astype(jnp.float32)
    all_fluxes = lax.all_gather(fluxes, "tracer", axis=1, tiled=True)
    stacked = jnp.concatenate(
        [all_fluxes[0], all_fluxes[1], wet_cells, diff_east[None], diff_north[None]], 0
    )
    rimmed = with_halo(stacked, (("gx", 1), ("gy", 2)), 2)
    east_ext = rimmed[:levels]
    north_ext = rimmed[levels : 2 * levels]
    downward = all_fluxes[2]
    wet_ext = rimmed[-(levels + 2) : -2]
    kx_ext = rimmed[-2]
    ky_ext = rimmed[-1]
    open_x = wet_ext[:, :-1, 2:-2] * wet_ext[:, 1:, 2:-2]
    open_y = wet_ext[:, 2:-2, :-1] * wet_ext[:, 2:-2, 1:]
    flux_x = east_ext[:, 1 : rows_dev + 2, 2:-2] * open_x[:, 1 : rows_dev + 2]
    kappa_x = kx_ext[None, 1 : rows_dev + 2, 2:-2] * open_x[:, 1 : rows_dev + 2]
    flux_y = north_ext[:, 2:-2, 1 : cols_dev + 2] * open_y[:, :, 1 : cols_dev + 2]
    kappa_y = ky_ext[None, 2:-2, 1 : cols_dev + 2] * open_y[:, :, 1 : cols_dev + 2]
    wet_z = jnp.pad(wet_cells, ((2, 2), (0, 0), (0, 0)))
    open_z = wet_z[:-1] * wet_z[1:]
    flux_z = jnp.pad(downward, ((1, 0), (0, 0), (0, 0))) * open_z[1 : levels + 2]
    group_match = (
        groups[:, None] == lax.broadcasted_iota(jnp.int32, (1, preference.shape[0]), 1)
    ).astype(jnp.float32)
    grazing_pref = jnp.sum(group_match * preference[None, :], axis=1)
    tracer_field = tracers
    for step_index in range(STEPS):
        prey_local = jnp.sum(grazing_pref[:, None, None, None] * tracer_field, axis=0)
        prey_total = lax.psum(prey_local, "tracer")
        factor = grazers / (1.0 + 4.0 * prey_total / total_tracers)
        extended = with_halo(tracer_field, (("gx", 2), ("gy", 3)), 2)
        tendency = face_terms(extended[:, :, :, 2:-2], open_x, flux_x, kappa_x, -2)
        tendency = tendency + face_terms(extended[:, :, 2:-2, :], open_y, flux_y, kappa_y, -1)
        padded_z = jnp.pad(tracer_field, ((0, 0), (2, 2), (0, 0), (0, 0)))
        tendency = tendency + face_terms(padded_z, open_z, flux_z, None, -3)
        tracer_field = (
            tracer_field + tendency - grazing_pref[:, None, None, None] * factor * tracer_field
        )
    return tracer_field


class Geo:
    def __init__(self, tr_dev, levels, rows, cols):
        self.T, self.L, self.R, self.C = tr_dev, levels, rows, cols
        self.LH = levels // SUB
        self.tile = rows * levels
        self.slots = -(-(tr_dev + 3) // 4) * 4
        self.slots2 = -(-tr_dev // 4) * 4
        at = 0
        self.off = {}
        for name, count in (
            ("hx", (rows + 3) * levels),
            ("px", (rows + 1) * levels),
            ("mx", (rows + 1) * levels),
            ("kx", (rows + 1) * SUB),
            ("hy", self.tile),
            ("py", self.tile),
            ("my", self.tile),
            ("ky", rows * SUB),
            ("hz", self.tile),
            ("pz", self.tile),
            ("mz", self.tile),
            ("hs", SUB),
            ("ps", SUB),
            ("ms", SUB),
            ("ks", SUB),
        ):
            self.off[name] = at
            at += count
        self.coefs = at


def lanes(shape=(SUB, 128)):
    return lax.broadcasted_iota(jnp.int32, shape, 1)


def sublanes(shape=(SUB, 128)):
    return lax.broadcasted_iota(jnp.int32, shape, 0)


def roll(v, by, axis):
    by = by % v.shape[axis]
    return v if by == 0 else pltpu.roll(v, by, axis)


def pack_strips(parts):
    lane = lanes()
    packed = jnp.zeros((SUB, 128), jnp.float32)
    for k, part in enumerate(parts):
        inside = (lane >= 8 * k + 2) & (lane < 8 * k + 6)
        packed = jnp.where(inside, roll(part, 8 * k + 4, 1), packed)
    return packed


def message_strips(packed, low):
    place = lanes() % 8
    out = jnp.zeros((SUB, 128), jnp.float32)
    for m, one in enumerate(packed):
        moved = roll(one, 2 * m - (4 if low else 2), 1)
        out = jnp.where((place == 2 * m) | (place == 2 * m + 1), moved, out)
    return out


def full_strips(own, from_lower, from_upper, m):
    place = lanes() % 8
    out = jnp.where(place < 2, roll(from_lower, -2 * m, 1), roll(from_upper, 6 - 2 * m, 1))
    out = jnp.where((place >= 2) & (place < 4), roll(own, -2, 1), out)
    return jnp.where((place >= 4) & (place < 6), roll(own, 2, 1), out)


def taste_of(groups_ref, pref_ref, t):
    return pref_ref[groups_ref[t]]


def is_even(axis):
    return lax.rem(lax.axis_index(axis), 2) == 0


def load_kernel(
    g, tracers_ref, groups_ref, pref_ref, field_ref, strips_ref, prey_ref, landed, sems
):
    def arrival(t):
        at = pl.ds(pl.multiple_of(t * g.tile, g.tile), g.tile)
        return pltpu.make_async_copy(tracers_ref.at[at, :], landed.at[at, :], sems.at[t])

    for t in range(g.T):
        arrival(t).start()
    prey_ref[...] = jnp.zeros_like(prey_ref)

    def one(t):
        arrival(t).wait()
        taste = taste_of(groups_ref, pref_ref, t)
        base = pl.multiple_of(t * g.tile, g.tile)
        parts = []
        for r in range(g.R):
            for lh in range(g.LH):
                at = (r * g.LH + lh) * SUB
                v = landed[pl.ds(base + lh * SUB * g.R + r, SUB, stride=g.R), :]
                field_ref[pl.ds(base + at, SUB), :] = v
                parts.append(v)
                prey_ref[at : at + SUB, :] += taste * v
        strips_ref[pl.ds(pl.multiple_of(t * SUB, SUB), SUB), :] = pack_strips(parts)

    each_tracer(g, one)


def flux_reader(g, mine_ref, other_ref):
    first = lax.axis_index("tracer") == 0
    single = lax.axis_size("tracer") != 2

    def flux(dim, r, lh):
        at = pl.ds(dim * g.R * SUB + r, SUB, stride=g.R)
        a, b = mine_ref[at, :], other_ref[at, :]
        if single:
            return (a, b)[lh]
        return jnp.where(first, (a, b)[lh], (b, a)[lh])

    return flux


def first_messages_kernel(
    g, field_ref, strips_ref, mine_ref, other_ref, depth_ref, east_ref, north_ref,
    xev_ref, xod_ref, yev_ref, yod_ref, extra_ref,
):
    x_even, y_even = is_even("gx"), is_even("gy")
    flux = flux_reader(g, mine_ref, other_ref)
    zero = jnp.zeros((SUB, 128), jnp.float32)

    def put(ref_ev, ref_od, at, even, low, high):
        ref_ev[at, :] = jnp.where(even, high, low)
        ref_od[at, :] = jnp.where(even, low, high)

    def one(t):
        base = pl.multiple_of(t * g.tile, g.tile)
        for i in range(2 * g.LH):
            low = field_ref[pl.ds(base + i * SUB, SUB), :]
            high = field_ref[pl.ds(base + g.tile - 2 * g.L + i * SUB, SUB), :]
            at = pl.ds(pl.multiple_of(t * 2 * g.L, SUB) + i * SUB, SUB)
            put(xev_ref, xod_ref, at, x_even, low, high)

    each_tracer(g, one)
    at = g.T * 2 * g.L
    for lh in range(g.LH):
        put(xev_ref, xod_ref, slice(at, at + SUB), x_even, zero, flux(0, g.R - 1, lh))
        at += SUB
    depth = depth_ref[...].astype(jnp.float32)
    put(xev_ref, xod_ref, slice(at, at + SUB), x_even, depth, roll(depth, 2, 0))
    at += SUB
    put(xev_ref, xod_ref, slice(at, at + SUB), x_even, zero, roll(east_ref[...], 1, 0))

    packed = [strips_ref[t * SUB : (t + 1) * SUB, :] for t in range(g.T)]
    extras = [
        pack_strips(spread_rows(g, depth)),
        pack_strips([flux(1, r, lh) for r in range(g.R) for lh in range(g.LH)]),
        pack_strips(spread_rows(g, north_ref[...])),
    ]
    for i, one_extra in enumerate(extras):
        extra_ref[i * SUB : (i + 1) * SUB, :] = one_extra
    packed += extras
    for v in range(0, len(packed), 4):
        low = message_strips(packed[v : v + 4], True)
        high = message_strips(packed[v : v + 4], False)
        put(yev_ref, yod_ref, slice(v * 2, v * 2 + SUB), y_even, low, high)


def spread_rows(g, rows):
    parts = []
    for r in range(g.R):
        parts += [jnp.broadcast_to(rows[r : r + 1, :], (SUB, 128))] * g.LH
    return parts


def coefficients(g, cf, xl, yl, yu, flux, extra_ref, depth_ref, east_ref, north_ref):
    lane, sub = lanes(), sublanes()
    depth = depth_ref[...].astype(jnp.float32)
    depth_low, depth_high = xl(g.LH)
    east = east_ref[...]
    east_low, _ = xl(g.LH + 1)
    north = north_ref[...]
    level = [(sub + SUB * lh).astype(jnp.float32) for lh in range(g.LH)]

    def spread(rows, r):
        return jnp.broadcast_to(rows[r : r + 1, :], (SUB, 128))

    depths = [spread(depth_low, 0), spread(depth_low, 1)]
    depths += [spread(depth, r) for r in range(g.R)]
    depths += [spread(depth_high, 0), spread(depth_high, 1)]
    wet = [[level[lh] < d for lh in range(g.LH)] for d in depths]

    def store(name, index, value):
        at = g.off[name] + index * SUB
        cf[at : at + SUB, :] = value

    def put(name, index, opened, h, f):
        f = jnp.where(opened, f, 0.0)
        store("h" + name, h, jnp.where(opened, 0.5, 0.0))
        store("p" + name, index, jnp.maximum(f, 0.0))
        store("m" + name, index, jnp.minimum(f, 0.0))

    for f in range(-1, g.R + 2):
        for lh in range(g.LH):
            opened = wet[f + 1][lh] & wet[f + 2][lh]
            h = (f + 1) * g.LH + lh
            if 0 <= f <= g.R:
                below = xl(lh)[0] if f == 0 else flux(0, f - 1, lh)
                put("x", f * g.LH + lh, opened, h, below)
            else:
                store("hx", h, jnp.where(opened, 0.5, 0.0))
        if 0 <= f <= g.R:
            store("kx", f, 2.0 * (spread(east_low, 0) if f == 0 else spread(east, f - 1)))

    for r in range(g.R):
        before = roll(depths[r + 2], 1, 1)
        store("ky", r, 2.0 * roll(spread(north, r), 1, 1))
        for lh in range(g.LH):
            k = r * g.LH + lh
            here = wet[r + 2][lh]
            opened = here & (level[lh] < before) & (lane > 0)
            put("y", k, opened, k, roll(flux(1, r, lh), 1, 1))
        flux_z = [roll(flux(2, r, lh), 1, 0) for lh in range(g.LH)]
        for lh in range(g.LH):
            k = r * g.LH + lh
            here = wet[r + 2][lh]
            above = flux_z[lh] if lh == 0 else jnp.where(sub == 0, flux_z[lh - 1], flux_z[lh])
            opened = here if lh else here & (sub > 0)
            put("z", k, opened, k, above)

    place = lane % 8
    half_of = (lane // 8) % g.LH
    own = [extra_ref[i * SUB : (i + 1) * SUB, :] for i in range(3)]
    full = []
    for i, one in enumerate(own):
        slot = g.T + i
        full.append(full_strips(one, yl(slot // 4), yu(slot // 4), slot % 4))
    wet_s = (sub + SUB * half_of).astype(jnp.float32) < full[0]
    opened = jnp.where(wet_s, 1.0, 0.0) * roll(jnp.where(wet_s, 1.0, 0.0), 1, 1)
    opened = (opened > 0.0) & (place != 0) & (place != 4)
    put("s", 0, opened, 0, roll(full[1], 1, 1))
    store("ks", 0, 2.0 * roll(full[2], 1, 1))


def limited(a, b):
    least, most = jnp.minimum(a, b), jnp.maximum(a, b)
    return jnp.maximum(least, jnp.minimum(most, 0.0))


def advance(g, cf, strip_fix, at_row, taste, factor, emit):
    lane, sub = lanes(), sublanes()
    ends = (lane == 0) | (lane == 127)
    top, bottom = sub == 0, sub == SUB - 1

    def coef(name, index):
        at = g.off[name] + index * SUB
        return cf[at : at + SUB, :]

    slope_fix, carried_fix = strip_fix
    before = {}
    cell, jump_next, right, carried = {}, {}, {}, {}
    for lh in range(g.LH):
        c2, c1, c0 = at_row(-2, lh), at_row(-1, lh), at_row(0, lh)
        j1 = coef("hx", lh) * (c1 - c2)
        j0 = coef("hx", g.LH + lh) * (c0 - c1)
        s1 = limited(j1, j0)
        cell[lh], jump_next[lh] = c0, j0
        before[lh] = c1 + s1

    def x_face(f, lh, left, right, jump):
        k = f * g.LH + lh
        return coef("px", k) * left + coef("mx", k) * right - coef("kx", f) * jump

    for r in range(g.R):
        news = []
        here = [cell[lh] for lh in range(g.LH)]
        for lh in range(g.LH):
            k = r * g.LH + lh
            c = cell[lh]
            up = at_row(r + 1, lh)
            j_low = jump_next[lh]
            j_up = coef("hx", (r + 2) * g.LH + lh) * (up - c)
            s = limited(j_low, j_up)
            if r == 0:
                carried[lh] = x_face(0, lh, before[lh], c - s, j_low)
            left = c + s
            up2 = at_row(r + 2, lh)
            j_up2 = coef("hx", (r + 3) * g.LH + lh) * (up2 - up)
            s_up = limited(j_up, j_up2)
            out = x_face(r + 1, lh, left, up - s_up, j_up)
            new = c + (carried[lh] - out)
            carried[lh], cell[lh], jump_next[lh] = out, up, j_up
            j = coef("hy", k) * (c - roll(c, 1, 1))
            s = limited(j, roll(j, -1, 1))
            s = jnp.where(ends, roll(slope_fix, -(8 * k + 2), 1), s)
            flow = coef("py", k) * roll(c + s, 1, 1) + coef("my", k) * (c - s)
            flow = flow - coef("ky", r) * j
            new = new + (flow - roll(flow, -1, 1))
            new = new + jnp.where(ends, roll(carried_fix, -(8 * k + 2), 1), 0.0)
            at = k * SUB
            new = new - (taste * factor[at : at + SUB, :]) * c
            news.append(new)
        def shift_down(v):
            rolled = [roll(x, 1, 0) for x in v]
            return [rolled[0]] + [
                jnp.where(top, rolled[i - 1], rolled[i]) for i in range(1, g.LH)
            ]

        def shift_up(v):
            rolled = [roll(x, -1, 0) for x in v]
            return [
                jnp.where(bottom, rolled[(i + 1) % g.LH], rolled[i]) for i in range(g.LH)
            ]

        index = [r * g.LH + lh for lh in range(g.LH)]
        above = shift_down(here)
        j = [coef("hz", k) * (c - a) for k, c, a in zip(index, here, above)]
        s = [limited(a, b) for a, b in zip(j, shift_up(j))]
        left = shift_down([c + v for c, v in zip(here, s)])
        flow = [
            coef("pz", k) * a + coef("mz", k) * (c - v)
            for k, a, c, v in zip(index, left, here, s)
        ]
        for lh, (a, b, new) in enumerate(zip(flow, shift_up(flow), news)):
            emit(r, lh, new + (a - b))


def strip_fixes(g, cf, full):
    def coef(name):
        return cf[g.off[name] : g.off[name] + SUB, :]

    at_two = lanes() % 8 == 2
    j = coef("hs") * (full - roll(full, 1, 1))
    s = limited(j, roll(j, -1, 1))
    flow = coef("ps") * roll(full + s, 1, 1) + coef("ms") * (full - s) - coef("ks") * j
    return jnp.where(at_two, s, roll(s, -4, 1)), jnp.where(at_two, flow, -roll(flow, -5, 1))


def split_sides(even, ev, od):
    return jnp.where(even, od, ev), jnp.where(even, ev, od)


def set_factor(g, total, factor, grazers_ref, mine_ref, others):
    for r in range(g.R):
        for lh in range(g.LH):
            at = (r * g.LH + lh) * SUB
            prey = mine_ref[at : at + SUB, :]
            for ref in others:
                prey = prey + ref[at : at + SUB, :]
            grazers = grazers_ref[pl.ds(lh * SUB * g.R + r, SUB, stride=g.R), :]
            factor[at : at + SUB, :] = grazers / (1.0 + 4.0 * prey / total)


def rows_of(g, field_ref, xev_ref, xod_ref, x_even, t):
    base = pl.multiple_of(t * g.tile, g.tile)
    halo = pl.multiple_of(t * 2 * g.L, 2 * g.L)
    seen = {}

    def at_row(r, lh):
        if (r, lh) not in seen:
            if 0 <= r < g.R:
                seen[r, lh] = field_ref[pl.ds(base + r * g.L + lh * SUB, SUB), :]
            else:
                i = r + 2 if r < 0 else r - g.R
                at = pl.ds(halo + i * g.L + lh * SUB, SUB)
                low, high = split_sides(x_even, xev_ref[at, :], xod_ref[at, :])
                seen[r, lh] = low if r < 0 else high
        return seen[r, lh]

    return at_row


def y_sides(y_even, yev_ref, yod_ref, v):
    at = pl.ds(v * SUB, SUB)
    return split_sides(y_even, yev_ref[at, :], yod_ref[at, :])


def all_strip_fixes(g, cf, strips_ref, yev_ref, yod_ref, y_even, slope_ref, carried_ref):
    for t in range(g.T):
        low, high = y_sides(y_even, yev_ref, yod_ref, t // 4)
        at = slice(t * SUB, (t + 1) * SUB)
        full = full_strips(strips_ref[at, :], low, high, t % 4)
        slope_ref[at, :], carried_ref[at, :] = strip_fixes(g, cf, full)


def each_tracer(g, body):
    def some(i, carry):
        for ahead in range(AHEAD):
            body(i * AHEAD + ahead)
        return carry

    lax.fori_loop(0, g.T // AHEAD, some, 0)
    for t in range(g.T - g.T % AHEAD, g.T):
        body(t)


def step_one_kernel(
    g, total, n_other,
    field_ref, strips_ref, xev_ref, xod_ref, yev_ref, yod_ref, extra_ref, mine_ref, other_ref,
    depth_ref, east_ref, north_ref, grazers_ref, groups_ref, pref_ref, prey_ref, *rest,
):
    others, rest = rest[:n_other], rest[n_other:]
    (out_ref, xev2_ref, xod2_ref, yev2_ref, yod2_ref, strips2_ref, prey2_ref, cf,
     factor, slope_ref, carried_ref) = rest
    x_even, y_even = is_even("gx"), is_even("gy")

    def xl(i):
        at = pl.ds(g.T * 2 * g.L + i * SUB, SUB)
        return split_sides(x_even, xev_ref[at, :], xod_ref[at, :])

    coefficients(
        g, cf, xl,
        lambda v: y_sides(y_even, yev_ref, yod_ref, v)[0],
        lambda v: y_sides(y_even, yev_ref, yod_ref, v)[1],
        flux_reader(g, mine_ref, other_ref), extra_ref, depth_ref, east_ref, north_ref,
    )
    set_factor(g, total, factor, grazers_ref, prey_ref, others)
    all_strip_fixes(g, cf, strips_ref, yev_ref, yod_ref, y_even, slope_ref, carried_ref)
    prey2_ref[...] = jnp.zeros_like(prey2_ref)

    def one(t):
        taste = taste_of(groups_ref, pref_ref, t)
        base = pl.multiple_of(t * g.tile, g.tile)
        halo = pl.multiple_of(t * 2 * g.L, 2 * g.L)
        strip_at = pl.ds(pl.multiple_of(t * SUB, SUB), SUB)
        news = {}

        def emit(r, lh, new):
            at = (r * g.LH + lh) * SUB
            out_ref[pl.ds(base + at, SUB), :] = new
            prey2_ref[at : at + SUB, :] += taste * new
            news[r, lh] = new

        advance(
            g, cf, (slope_ref[strip_at, :], carried_ref[strip_at, :]),
            rows_of(g, field_ref, xev_ref, xod_ref, x_even, t), taste, factor, emit,
        )
        for i in range(2):
            for lh in range(g.LH):
                at = pl.ds(halo + i * g.L + lh * SUB, SUB)
                low, high = news[i, lh], news[g.R - 2 + i, lh]
                xev2_ref[at, :] = jnp.where(x_even, high, low)
                xod2_ref[at, :] = jnp.where(x_even, low, high)
        strips2_ref[strip_at, :] = pack_strips(
            [news[r, lh] for r in range(g.R) for lh in range(g.LH)]
        )

    each_tracer(g, one)
    packed = [strips2_ref[t * SUB : (t + 1) * SUB, :] for t in range(g.T)]
    for v in range(0, g.T, 4):
        low = message_strips(packed[v : v + 4], True)
        high = message_strips(packed[v : v + 4], False)
        yev2_ref[v * 2 : v * 2 + SUB, :] = jnp.where(y_even, high, low)
        yod2_ref[v * 2 : v * 2 + SUB, :] = jnp.where(y_even, low, high)


def step_two_kernel(
    g, total, n_other,
    field_ref, strips_ref, xev_ref, xod_ref, yev_ref, yod_ref, cf,
    grazers_ref, groups_ref, pref_ref, prey_ref, *rest,
):
    others, (out_ref, factor, slope_ref, carried_ref, leaving, sems) = rest[:n_other], rest[n_other:]
    x_even, y_even = is_even("gx"), is_even("gy")
    set_factor(g, total, factor, grazers_ref, prey_ref, others)
    all_strip_fixes(g, cf, strips_ref, yev_ref, yod_ref, y_even, slope_ref, carried_ref)

    def departure(t):
        at = pl.ds(pl.multiple_of(t * g.tile, g.tile), g.tile)
        return pltpu.make_async_copy(leaving.at[at, :], out_ref.at[at, :], sems.at[t])

    def one(t):
        taste = taste_of(groups_ref, pref_ref, t)
        base = pl.multiple_of(t * g.tile, g.tile)
        strip_at = pl.ds(pl.multiple_of(t * SUB, SUB), SUB)

        def emit(r, lh, new):
            leaving[pl.ds(base + lh * SUB * g.R + r, SUB, stride=g.R), :] = new

        advance(
            g, cf, (slope_ref[strip_at, :], carried_ref[strip_at, :]),
            rows_of(g, field_ref, xev_ref, xod_ref, x_even, t), taste, factor, emit,
        )
        departure(t).start()

    each_tracer(g, one)
    for t in range(g.T):
        departure(t).wait()


def call(body, outs, operands, scalars=(), far=(), far_out=False, scratch=()):
    spaces = [
        pltpu.SMEM if i in scalars else pltpu.HBM if i in far else pltpu.VMEM
        for i in range(len(operands))
    ]
    return pl.pallas_call(
        body,
        out_shape=[jax.ShapeDtypeStruct((rows, 128), jnp.float32) for rows in outs],
        in_specs=[pl.BlockSpec(memory_space=space) for space in spaces],
        out_specs=[pl.BlockSpec(memory_space=pltpu.HBM if far_out else pltpu.VMEM)] * len(outs),
        scratch_shapes=[
            pltpu.VMEM((rows, 128), jnp.float32) if isinstance(rows, int) else rows
            for rows in scratch
        ],
        compiler_params=pltpu.CompilerParams(vmem_limit_bytes=LIM),
    )(*operands)


def pair_swap(values, axis, start):
    pairs = []
    for i in range(start, lax.axis_size(axis) - 1, 2):
        pairs += [(i, i + 1), (i + 1, i)]
    if not pairs:
        return jnp.zeros_like(values)
    return lax.ppermute(values, axis, pairs)


def tracer_swap(values):
    return lax.ppermute(values, "tracer", [(0, 1), (1, 0)])


def all_prey(values):
    if lax.axis_size("tracer") == 2:
        return [values, tracer_swap(values)]
    return [lax.psum(values, "tracer")]


def neighbours(x_ev, x_od, y_ev, y_od):
    x_od = pair_swap(x_od, "gx", 1)
    y_ev = pair_swap(y_ev, "gy", 0)
    y_od = pair_swap(y_od, "gy", 1)
    x_ev = pair_swap(x_ev, "gx", 0)
    return x_ev, x_od, y_ev, y_od


def on_device(tracers, fluxes, diff_east, diff_north, column_depth, grazers, groups, preference):
    tr_dev, levels, rows, cols = tracers.shape
    parts = lax.axis_size("tracer")
    if not (cols == 128 and rows * levels == cols and levels == 2 * SUB and rows % SUB == 0):
        return plain(
            tracers, fluxes, diff_east, diff_north, column_depth, grazers, groups, preference
        )
    g = Geo(tr_dev, levels, rows, cols)
    total = float(tr_dev * parts)
    pair = parts == 2
    flat = tracers.reshape(-1, cols)
    grazers = grazers.reshape(-1, cols)

    if pair:
        mine = fluxes.reshape(-1, cols)
        other = tracer_swap(mine)
    else:
        gathered = lax.all_gather(fluxes, "tracer", axis=1, tiled=True)
        mine, other = (gathered[:, i : i + SUB].reshape(-1, cols) for i in (0, SUB))
    copies = pltpu.SemaphoreType.DMA((g.T,))
    field, strips, prey = call(
        functools.partial(load_kernel, g),
        [g.T * g.tile, g.T * SUB, g.tile],
        [pltpu.with_memory_space_constraint(flat, pltpu.HBM), groups, preference],
        scalars=(1, 2),
        far=(0,),
        scratch=[g.T * g.tile, copies],
    )
    prey = all_prey(prey)
    x_rows = g.T * 2 * g.L + g.L + 2 * SUB
    *messages, extra = call(
        functools.partial(first_messages_kernel, g),
        [x_rows, x_rows, g.slots * 2, g.slots * 2, 3 * SUB],
        [field, strips, mine, other, column_depth, diff_east, diff_north],
    )
    messages = neighbours(*messages)
    x_rows = g.T * 2 * g.L
    *results, coefs = call(
        functools.partial(step_one_kernel, g, total, len(prey) - 1),
        [g.T * g.tile, x_rows, x_rows, g.slots2 * 2, g.slots2 * 2, g.T * SUB, g.tile, g.coefs],
        [field, strips, *messages, extra, mine, other, column_depth, diff_east, diff_north,
         grazers, groups, preference, *prey],
        scalars=(13, 14),
        scratch=[g.tile, g.T * SUB, g.T * SUB],
    )
    field, *messages, strips, prey = results
    prey = all_prey(prey)
    messages = neighbours(*messages)
    (out,) = call(
        functools.partial(step_two_kernel, g, total, len(prey) - 1),
        [g.T * g.tile],
        [field, strips, *messages, coefs, grazers, groups, preference, *prey],
        scalars=(8, 9),
        far_out=True,
        scratch=[g.tile, g.T * SUB, g.T * SUB, g.T * g.tile, copies],
    )
    return out.reshape(tracers.shape)


def solution(mesh):
    placed = (
        P("tracer", None, "gx", "gy"),
        P(None, "tracer", "gx", "gy"),
        P("gx", "gy"),
        P("gx", "gy"),
        P("gx", "gy"),
        P(None, "gx", "gy"),
        P("tracer"),
        P(),
    )
    return jax.shard_map(
        on_device,
        mesh=mesh,
        in_specs=placed,
        out_specs=P("tracer", None, "gx", "gy"),
        check_vma=False,
    )
```

```python
import functools

import jax
import jax.numpy as jnp
from jax import lax
from jax.experimental import pallas as pl
from jax.experimental.pallas import tpu as pltpu
from jax.sharding import PartitionSpec as P

STEPS = 2
SUB = 8
LIM = 48 * 1024 * 1024
INSIDE, FINISH = 2, 2


def with_halo(cells, sides, width):
    for axis, dim in sides:
        count = lax.axis_size(axis)
        ends = count - 1
        head = lax.slice_in_dim(cells, 0, width, axis=dim)
        tail = lax.slice_in_dim(cells, cells.shape[dim] - width, cells.shape[dim], axis=dim)
        cells = jnp.concatenate(
            [
                lax.ppermute(tail, axis, [(i, (i + 1) % count) for i in range(ends)]),
                cells,
                lax.ppermute(head, axis, [((i + 1) % count, i) for i in range(ends)]),
            ],
            axis=dim,
        )
    return cells


def minmod(jump_low, jump_high):
    return jnp.maximum(0.0, jnp.minimum(jump_low, jump_high)) + jnp.minimum(
        0.0, jnp.maximum(jump_low, jump_high)
    )


def window(values, low_end, high_end, direction):
    return lax.slice_in_dim(values, low_end, high_end, axis=direction % values.ndim)


def face_terms(tracer_field, open_faces, face_flux, face_kappa, direction):
    length = tracer_field.shape[direction % tracer_field.ndim] - 4
    jump_face = open_faces * (
        window(tracer_field, 1, length + 4, direction)
        - window(tracer_field, 0, length + 3, direction)
    )
    slopes = minmod(
        window(jump_face, 0, length + 2, direction), window(jump_face, 1, length + 3, direction)
    )
    left_value = window(tracer_field, 1, length + 2, direction) + 0.5 * window(
        slopes, 0, length + 1, direction
    )
    right_value = window(tracer_field, 2, length + 3, direction) - 0.5 * window(
        slopes, 1, length + 2, direction
    )
    carried = face_flux * jnp.where(face_flux > 0.0, left_value, right_value)
    if face_kappa is not None:
        carried = carried - face_kappa * window(jump_face, 1, length + 2, direction)
    return window(carried, 0, length, direction) - window(carried, 1, length + 1, direction)


def plain(tracers, fluxes, diff_east, diff_north, column_depth, grazers, groups, preference):
    tr_dev, levels, rows_dev, cols_dev = tracers.shape
    total_tracers = tr_dev * lax.axis_size("tracer")
    level_index = lax.broadcasted_iota(jnp.int32, (levels, rows_dev, cols_dev), 0)
    wet_cells = (level_index < column_depth[None]).astype(jnp.float32)
    all_fluxes = lax.all_gather(fluxes, "tracer", axis=1, tiled=True)
    stacked = jnp.concatenate(
        [all_fluxes[0], all_fluxes[1], wet_cells, diff_east[None], diff_north[None]], 0
    )
    rimmed = with_halo(stacked, (("gx", 1), ("gy", 2)), 2)
    east_ext = rimmed[:levels]
    north_ext = rimmed[levels : 2 * levels]
    downward = all_fluxes[2]
    wet_ext = rimmed[-(levels + 2) : -2]
    kx_ext = rimmed[-2]
    ky_ext = rimmed[-1]
    open_x = wet_ext[:, :-1, 2:-2] * wet_ext[:, 1:, 2:-2]
    open_y = wet_ext[:, 2:-2, :-1] * wet_ext[:, 2:-2, 1:]
    flux_x = east_ext[:, 1 : rows_dev + 2, 2:-2] * open_x[:, 1 : rows_dev + 2]
    kappa_x = kx_ext[None, 1 : rows_dev + 2, 2:-2] * open_x[:, 1 : rows_dev + 2]
    flux_y = north_ext[:, 2:-2, 1 : cols_dev + 2] * open_y[:, :, 1 : cols_dev + 2]
    kappa_y = ky_ext[None, 2:-2, 1 : cols_dev + 2] * open_y[:, :, 1 : cols_dev + 2]
    wet_z = jnp.pad(wet_cells, ((2, 2), (0, 0), (0, 0)))
    open_z = wet_z[:-1] * wet_z[1:]
    flux_z = jnp.pad(downward, ((1, 0), (0, 0), (0, 0))) * open_z[1 : levels + 2]
    group_match = (
        groups[:, None] == lax.broadcasted_iota(jnp.int32, (1, preference.shape[0]), 1)
    ).astype(jnp.float32)
    grazing_pref = jnp.sum(group_match * preference[None, :], axis=1)
    tracer_field = tracers
    for step_index in range(STEPS):
        prey_local = jnp.sum(grazing_pref[:, None, None, None] * tracer_field, axis=0)
        prey_total = lax.psum(prey_local, "tracer")
        factor = grazers / (1.0 + 4.0 * prey_total / total_tracers)
        extended = with_halo(tracer_field, (("gx", 2), ("gy", 3)), 2)
        tendency = face_terms(extended[:, :, :, 2:-2], open_x, flux_x, kappa_x, -2)
        tendency = tendency + face_terms(extended[:, :, 2:-2, :], open_y, flux_y, kappa_y, -1)
        padded_z = jnp.pad(tracer_field, ((0, 0), (2, 2), (0, 0), (0, 0)))
        tendency = tendency + face_terms(padded_z, open_z, flux_z, None, -3)
        tracer_field = (
            tracer_field + tendency - grazing_pref[:, None, None, None] * factor * tracer_field
        )
    return tracer_field


WIDE = 16
EACH = 128 // WIDE


class Geo:
    def __init__(self, tr_dev, levels, rows, cols):
        self.T, self.L, self.R, self.C = tr_dev, levels, rows, cols
        self.LH = levels // SUB
        self.tile = rows * levels
        self.K = rows * self.LH
        self.NV = self.K // EACH
        self.SR = self.NV * SUB
        self.my1 = -(-(tr_dev + 3) * self.NV // EACH)
        self.my2 = -(-tr_dev * self.NV // EACH)
        self.inner = Table(
            hx=(rows + 1) * self.LH, px=(rows + 1) * self.LH, mx=(rows + 1) * self.LH,
            kx=rows + 1, hy=self.K, py=self.K, my=self.K, ky=rows,
            hz=self.K, pz=self.K, mz=self.K,
        )
        self.outer = Table(
            hx=4 * self.LH, px=2 * self.LH, mx=2 * self.LH, kx=1,
            hs=self.NV, ps=self.NV, ms=self.NV, ks=self.NV,
        )


class Table:
    def __init__(self, **counts):
        self.at, self.rows = {}, 0
        for name, count in counts.items():
            self.at[name] = self.rows
            self.rows += count * SUB

    def get(self, ref, name, index):
        at = self.at[name] + index * SUB
        return ref[at : at + SUB, :]

    def set(self, ref, name, index, value):
        at = self.at[name] + index * SUB
        ref[at : at + SUB, :] = value

    def set_flux(self, ref, axis, index, opened, flux):
        flux = jnp.where(opened, flux, 0.0)
        self.set(ref, "p" + axis, index, jnp.maximum(flux, 0.0))
        self.set(ref, "m" + axis, index, jnp.minimum(flux, 0.0))

    def set_open(self, ref, axis, index, opened):
        self.set(ref, "h" + axis, index, jnp.where(opened, 0.5, 0.0))


def lanes():
    return lax.broadcasted_iota(jnp.int32, (SUB, 128), 1)


def sublanes():
    return lax.broadcasted_iota(jnp.int32, (SUB, 128), 0)


def roll(v, by, axis):
    by = by % v.shape[axis]
    return v if by == 0 else pltpu.roll(v, by, axis)


def registers(ref):
    return [ref[i : i + SUB, :] for i in range(0, ref.shape[0], SUB)]


def rows8(index):
    return pl.ds(pl.multiple_of(index * SUB, SUB), SUB)


def pack_strips(parts):
    lane = lanes()
    out = []
    for v in range(0, len(parts), EACH):
        packed = jnp.zeros((SUB, 128), jnp.float32)
        for k, part in enumerate(parts[v : v + EACH]):
            inside = (lane >= WIDE * k + 8) & (lane < WIDE * k + 16)
            packed = jnp.where(inside, roll(part, WIDE * k + 12, 1), packed)
        out.append(packed)
    return out


def message_strips(packed, low):
    place = lanes() % WIDE
    out = jnp.zeros((SUB, 128), jnp.float32)
    for m, one in enumerate(packed):
        moved = roll(one, 2 * m - (12 if low else 10), 1)
        out = jnp.where((place == 2 * m) | (place == 2 * m + 1), moved, out)
    return out


def put_messages(packed, even, ev_ref, od_ref):
    for v in range(0, len(packed), EACH):
        low = message_strips(packed[v : v + EACH], True)
        high = message_strips(packed[v : v + EACH], False)
        at = rows8(v // EACH)
        ev_ref[at, :] = jnp.where(even, high, low)
        od_ref[at, :] = jnp.where(even, low, high)


def full_strips(own, from_lower, from_upper, m):
    place = lanes() % WIDE
    out = jnp.where(place < 2, roll(from_lower, -2 * m, 1), 0.0)
    out = jnp.where((place >= 2) & (place < 6), roll(own, -10, 1), out)
    out = jnp.where((place >= 8) & (place < 12), own, out)
    return jnp.where((place >= 12) & (place < 14), roll(from_upper, 12 - 2 * m, 1), out)


def spread(rows, r):
    return jnp.broadcast_to(rows[r : r + 1, :], (SUB, 128))


def spread_rows(g, rows):
    return [spread(rows, r) for r in range(g.R) for _ in range(g.LH)]


def taste_of(groups_ref, pref_ref, t):
    return pref_ref[groups_ref[t]]


def is_even(axis):
    return lax.rem(lax.axis_index(axis), 2) == 0


def split_sides(even, ev, od):
    return jnp.where(even, od, ev), jnp.where(even, ev, od)


def limited(a, b):
    least, most = jnp.minimum(a, b), jnp.maximum(a, b)
    return jnp.maximum(least, jnp.minimum(most, 0.0))


def each_tracer(g, ahead, body):
    def some(i, carry):
        for more in range(ahead):
            body(i * ahead + more)
        return carry

    lax.fori_loop(0, g.T // ahead, some, 0)
    for t in range(g.T - g.T % ahead, g.T):
        body(t)


def flux_reader(g, mine_ref, other_ref):
    first = lax.axis_index("tracer") == 0
    single = lax.axis_size("tracer") != 2

    def flux(dim, r, lh):
        at = pl.ds(dim * g.R * SUB + r, SUB, stride=g.R)
        a, b = mine_ref[at, :], other_ref[at, :]
        if single:
            return (a, b)[lh]
        return jnp.where(first, (a, b)[lh], (b, a)[lh])

    return flux


def load_kernel(
    g, tracers_ref, groups_ref, pref_ref, field_ref, strips_ref, prey_ref, landed, sems
):
    def arrival(t):
        at = pl.ds(pl.multiple_of(t * g.tile, g.tile), g.tile)
        return pltpu.make_async_copy(tracers_ref.at[at, :], landed.at[at, :], sems.at[t])

    for t in range(g.T):
        arrival(t).start()
    prey_ref[...] = jnp.zeros_like(prey_ref)

    def one(t):
        arrival(t).wait()
        taste = taste_of(groups_ref, pref_ref, t)
        base = pl.multiple_of(t * g.tile, g.tile)
        parts = []
        for r in range(g.R):
            for lh in range(g.LH):
                at = (r * g.LH + lh) * SUB
                v = landed[pl.ds(base + lh * SUB * g.R + r, SUB, stride=g.R), :]
                field_ref[pl.ds(base + at, SUB), :] = v
                parts.append(v)
                prey_ref[at : at + SUB, :] += taste * v
        for i, packed in enumerate(pack_strips(parts)):
            strips_ref[rows8(t * g.NV + i), :] = packed

    each_tracer(g, 2, one)


def first_messages_kernel(
    g, field_ref, strips_ref, mine_ref, other_ref, depth_ref, east_ref, north_ref,
    xev_ref, xod_ref, yev_ref, yod_ref, extra_ref,
):
    x_even, y_even = is_even("gx"), is_even("gy")
    flux = flux_reader(g, mine_ref, other_ref)
    zero = jnp.zeros((SUB, 128), jnp.float32)

    def put(at, low, high):
        xev_ref[at, :] = jnp.where(x_even, high, low)
        xod_ref[at, :] = jnp.where(x_even, low, high)

    def one(t):
        base = pl.multiple_of(t * g.tile, g.tile)
        for i in range(2 * g.LH):
            low = field_ref[pl.ds(base + i * SUB, SUB), :]
            high = field_ref[pl.ds(base + g.tile - 2 * g.L + i * SUB, SUB), :]
            put(rows8(t * 2 * g.LH + i), low, high)

    each_tracer(g, 2, one)
    at = g.T * 2 * g.LH
    for lh in range(g.LH):
        put(rows8(at + lh), zero, flux(0, g.R - 1, lh))
    depth = depth_ref[...].astype(jnp.float32)
    put(rows8(at + g.LH), depth, roll(depth, 2, 0))
    put(rows8(at + g.LH + 1), zero, roll(east_ref[...], 1, 0))
    extras = pack_strips(spread_rows(g, depth))
    extras += pack_strips([flux(1, r, lh) for r in range(g.R) for lh in range(g.LH)])
    extras += pack_strips(spread_rows(g, north_ref[...]))
    for i, packed in enumerate(extras):
        extra_ref[rows8(i), :] = packed
    put_messages(registers(strips_ref) + extras, y_even, yev_ref, yod_ref)


def wet_levels(g, depths):
    level = [(sublanes() + SUB * lh).astype(jnp.float32) for lh in range(g.LH)]
    return [[level[lh] < d for lh in range(g.LH)] for d in depths]


def inner_coefficients(g, cf, flux, depth, east, north):
    tab, sub = g.inner, sublanes()
    depths = [spread(depth, r) for r in range(g.R)]
    wet = wet_levels(g, depths)
    wet_before = wet_levels(g, [roll(d, 1, 1) for d in depths])
    for r in range(g.R):
        tab.set(cf, "kx", r + 1, 2.0 * spread(east, r))
        tab.set(cf, "ky", r, 2.0 * roll(spread(north, r), 1, 1))
        flux_z = [roll(flux(2, r, lh), 1, 0) for lh in range(g.LH)]
        for lh in range(g.LH):
            k, here = r * g.LH + lh, wet[r][lh]
            if r:
                opened = here & wet[r - 1][lh]
                tab.set_open(cf, "x", k, opened)
                tab.set_flux(cf, "x", k, opened, flux(0, r - 1, lh))
            opened = here & wet_before[r][lh]
            tab.set_open(cf, "y", k, opened)
            tab.set_flux(cf, "y", k, opened, roll(flux(1, r, lh), 1, 1))
            opened = here if lh else here & (sub > 0)
            above = jnp.where(sub == 0, flux_z[lh - 1], flux_z[lh]) if lh else flux_z[lh]
            tab.set_open(cf, "z", k, opened)
            tab.set_flux(cf, "z", k, opened, above)


def outer_coefficients(g, cf, extra_x, extra_y, flux, extra_ref, depth, east):
    tab, lane = g.outer, lanes()
    depth_low, depth_high = extra_x(g.LH)
    depths = [spread(depth_low, 0), spread(depth_low, 1), spread(depth, 0), spread(depth, g.R - 1)]
    depths += [spread(depth_high, 0), spread(depth_high, 1)]
    wet = wet_levels(g, depths)
    tab.set(cf, "kx", 0, 2.0 * spread(extra_x(g.LH + 1)[0], 0))
    for lh in range(g.LH):
        for face, row in enumerate((0, 1, 3, 4)):
            tab.set_open(cf, "x", face * g.LH + lh, wet[row][lh] & wet[row + 1][lh])
        tab.set_flux(cf, "x", lh, wet[1][lh] & wet[2][lh], extra_x(lh)[0])
        tab.set_flux(cf, "x", g.LH + lh, wet[3][lh] & wet[4][lh], flux(0, g.R - 1, lh))
    place, half = lane % WIDE, (lane // WIDE) % g.LH
    for i in range(g.NV):
        full = []
        for which in range(3):
            own = which * g.NV + i
            slot = g.T * g.NV + own
            full.append(full_strips(extra_ref[rows8(own), :], *extra_y(slot // EACH), slot % EACH))
        wet_s = jnp.where((sublanes() + SUB * half).astype(jnp.float32) < full[0], 1.0, 0.0)
        opened = (wet_s * roll(wet_s, 1, 1) > 0.0) & (place != 0) & (place != 8)
        tab.set_open(cf, "s", i, opened)
        tab.set_flux(cf, "s", i, opened, roll(full[1], 1, 1))
        tab.set(cf, "ks", i, 2.0 * roll(full[2], 1, 1))


def end_lanes():
    lane = lanes()
    return (lane < 2) | (lane >= 126)


def inside_kernel(g, ahead, first, field_ref, *refs):
    if first:
        mine_ref, other_ref, depth_ref, east_ref, north_ref, part_ref, cf = refs
        inner_coefficients(
            g, cf, flux_reader(g, mine_ref, other_ref), depth_ref[...].astype(jnp.float32),
            east_ref[...], north_ref[...],
        )
    else:
        cf, part_ref = refs
    sub = sublanes()
    ends, top, bottom = end_lanes(), sub == 0, sub == SUB - 1

    def coef(name, index):
        return g.inner.get(cf, name, index)

    def shift_down(v):
        rolled = [roll(x, 1, 0) for x in v]
        return rolled[:1] + [
            jnp.where(top, rolled[i - 1], rolled[i]) for i in range(1, g.LH)
        ]

    def shift_up(v):
        rolled = [roll(x, -1, 0) for x in v]
        return [jnp.where(bottom, rolled[(i + 1) % g.LH], rolled[i]) for i in range(g.LH)]

    def one(t):
        base = pl.multiple_of(t * g.tile, g.tile)
        for r in range(g.R):
            index = [r * g.LH + lh for lh in range(g.LH)]
            at = [pl.ds(base + k * SUB, SUB) for k in index]
            cells = [field_ref[a, :] for a in at]
            news = []
            for k, c in zip(index, cells):
                j = coef("hy", k) * (c - roll(c, 1, 1))
                s = limited(j, roll(j, -1, 1))
                flow = coef("py", k) * roll(c + s, 1, 1) + coef("my", k) * (c - s)
                flow = flow - coef("ky", r) * j
                news.append(c + jnp.where(ends, 0.0, flow - roll(flow, -1, 1)))
            j = [coef("hz", k) * (c - a) for k, c, a in zip(index, cells, shift_down(cells))]
            s = [limited(a, b) for a, b in zip(j, shift_up(j))]
            above = shift_down([c + v for c, v in zip(cells, s)])
            flow = [
                coef("pz", k) * a + coef("mz", k) * (c - v)
                for k, a, c, v in zip(index, above, cells, s)
            ]
            for a, new, high, low in zip(at, news, flow, shift_up(flow)):
                part_ref[a, :] = new + (high - low)

    each_tracer(g, ahead, one)


def strip_tendency(g, cf, full, i):
    def coef(name):
        return g.outer.get(cf, name, i)

    j = coef("hs") * (full - roll(full, 1, 1))
    s = limited(j, roll(j, -1, 1))
    flow = coef("ps") * roll(full + s, 1, 1) + coef("ms") * (full - s) - coef("ks") * j
    tend = flow - roll(flow, -1, 1)
    return jnp.where(lanes() % WIDE < 12, tend, roll(tend, 10, 1))


def all_strip_tendencies(g, cf, strips_ref, sides, tend_ref):
    for n in range(g.T * g.NV):
        full = full_strips(strips_ref[rows8(n), :], *sides(n // EACH), n % EACH)
        tend_ref[rows8(n), :] = strip_tendency(g, cf, full, n % g.NV)


def set_factor(g, total, factor, grazers_ref, prey_refs):
    for r in range(g.R):
        for lh in range(g.LH):
            at = rows8(r * g.LH + lh)
            prey = sum(ref[at, :] for ref in prey_refs)
            grazers = grazers_ref[pl.ds(lh * SUB * g.R + r, SUB, stride=g.R), :]
            factor[at, :] = grazers / (1.0 + 4.0 * prey / total)


def finish(g, inner, outer, t, field_ref, part_ref, tend_ref, sides, taste, factor, emit):
    base = pl.multiple_of(t * g.tile, g.tile)
    ends = end_lanes()

    def cell(r, lh):
        if 0 <= r < g.R:
            return field_ref[pl.ds(base + (r * g.LH + lh) * SUB, SUB), :]
        i = r + 2 if r < 0 else r - g.R
        return sides(t * 2 * g.LH + i * g.LH + lh)[0 if r < 0 else 1]

    def coef(name, f, lh):
        if 0 < f < g.R:
            return g.inner.get(inner, name, f * g.LH + lh)
        if name == "hx":
            return g.outer.get(outer, name, {-1: 0, 0: 1, g.R: 2, g.R + 1: 3}[f] * g.LH + lh)
        return g.outer.get(outer, name, (g.LH if f else 0) + lh)

    state = [None] * g.LH
    tends = [tend_ref[rows8(t * g.NV + i), :] for i in range(g.NV)]
    for f in range(-1, g.R + 2):
        kappa = g.inner.get(inner, "kx", f) if f > 0 else g.outer.get(outer, "kx", 0)
        for lh in range(g.LH):
            if f < 0:
                below = cell(-2, lh)
                here = cell(-1, lh)
                state[lh] = (here, coef("hx", f, lh) * (here - below), None, None)
                continue
            c, j, left, carried = state[lh]
            up = cell(f, lh)
            j_up = coef("hx", f, lh) * (up - c)
            s = limited(j, j_up)
            if f > 0:
                kap = g.inner.get(inner, "kx", f - 1) if f > 1 else g.outer.get(outer, "kx", 0)
                flow = coef("px", f - 1, lh) * left + coef("mx", f - 1, lh) * (c - s) - kap * j
                if f > 1:
                    r = f - 2
                    k = r * g.LH + lh
                    v, n = divmod(k, EACH)
                    old = cell(r, lh)
                    new = part_ref[pl.ds(base + k * SUB, SUB), :] + (carried - flow)
                    new = new + jnp.where(ends, roll(tends[v], -(WIDE * n + 12), 1), 0.0)
                    new = new - (taste * factor[rows8(k), :]) * old
                    emit(r, lh, new)
                carried = flow
            state[lh] = (up, j_up, c + s, carried)


def reader(even, ev_ref, od_ref):
    def sides(i):
        at = rows8(i)
        return split_sides(even, ev_ref[at, :], od_ref[at, :])

    return sides


def step_one_kernel(
    g, total, ahead,
    field_ref, part_ref, strips_ref, xev_ref, xod_ref, yev_ref, yod_ref, inner, extra_ref,
    mine_ref, other_ref, depth_ref, east_ref, grazers_ref, groups_ref, pref_ref, *rest,
):
    prey_refs, rest = rest[:-10], rest[-10:]
    (out_ref, xev2_ref, xod2_ref, yev2_ref, yod2_ref, strips2_ref, prey2_ref, outer,
     factor, tend_ref) = rest
    x_even, y_even = is_even("gx"), is_even("gy")
    x_sides, y_sides = reader(x_even, xev_ref, xod_ref), reader(y_even, yev_ref, yod_ref)
    outer_coefficients(
        g, outer, lambda i: x_sides(g.T * 2 * g.LH + i), y_sides,
        flux_reader(g, mine_ref, other_ref), extra_ref,
        depth_ref[...].astype(jnp.float32), east_ref[...],
    )
    set_factor(g, total, factor, grazers_ref, prey_refs)
    all_strip_tendencies(g, outer, strips_ref, y_sides, tend_ref)
    prey2_ref[...] = jnp.zeros_like(prey2_ref)

    def one(t):
        taste = taste_of(groups_ref, pref_ref, t)
        base = pl.multiple_of(t * g.tile, g.tile)
        news = {}

        def emit(r, lh, new):
            at = (r * g.LH + lh) * SUB
            out_ref[pl.ds(base + at, SUB), :] = new
            prey2_ref[at : at + SUB, :] += taste * new
            news[r, lh] = new

        finish(g, inner, outer, t, field_ref, part_ref, tend_ref, x_sides, taste, factor, emit)
        for i in range(2):
            for lh in range(g.LH):
                at = rows8(t * 2 * g.LH + i * g.LH + lh)
                low, high = news[i, lh], news[g.R - 2 + i, lh]
                xev2_ref[at, :] = jnp.where(x_even, high, low)
                xod2_ref[at, :] = jnp.where(x_even, low, high)
        parts = [news[r, lh] for r in range(g.R) for lh in range(g.LH)]
        for i, packed in enumerate(pack_strips(parts)):
            strips2_ref[rows8(t * g.NV + i), :] = packed

    each_tracer(g, ahead, one)
    put_messages(registers(strips2_ref), y_even, yev2_ref, yod2_ref)


def step_two_kernel(
    g, total, ahead,
    field_ref, part_ref, strips_ref, xev_ref, xod_ref, yev_ref, yod_ref, inner, outer,
    grazers_ref, groups_ref, pref_ref, *rest,
):
    prey_refs, (out_ref, factor, tend_ref, leaving, sems) = rest[:-5], rest[-5:]
    x_sides = reader(is_even("gx"), xev_ref, xod_ref)
    y_sides = reader(is_even("gy"), yev_ref, yod_ref)
    set_factor(g, total, factor, grazers_ref, prey_refs)
    all_strip_tendencies(g, outer, strips_ref, y_sides, tend_ref)

    def departure(t):
        at = pl.ds(pl.multiple_of(t * g.tile, g.tile), g.tile)
        return pltpu.make_async_copy(leaving.at[at, :], out_ref.at[at, :], sems.at[t])

    def one(t):
        taste = taste_of(groups_ref, pref_ref, t)
        base = pl.multiple_of(t * g.tile, g.tile)

        def emit(r, lh, new):
            leaving[pl.ds(base + lh * SUB * g.R + r, SUB, stride=g.R), :] = new

        finish(g, inner, outer, t, field_ref, part_ref, tend_ref, x_sides, taste, factor, emit)
        departure(t).start()

    each_tracer(g, ahead, one)
    for t in range(g.T):
        departure(t).wait()


def call(body, outs, operands, scalars=(), far_out=False, scratch=(), cost=0):
    spaces = [pltpu.SMEM if i in scalars else pltpu.VMEM for i in range(len(operands))]
    if far_out is None:
        spaces[0] = pltpu.HBM
        operands = [pltpu.with_memory_space_constraint(operands[0], pltpu.HBM), *operands[1:]]
    return pl.pallas_call(
        body,
        out_shape=[jax.ShapeDtypeStruct((rows, 128), jnp.float32) for rows in outs],
        in_specs=[pl.BlockSpec(memory_space=space) for space in spaces],
        out_specs=[pl.BlockSpec(memory_space=pltpu.HBM if far_out else pltpu.VMEM)] * len(outs),
        scratch_shapes=[
            pltpu.VMEM((rows, 128), jnp.float32) if isinstance(rows, int) else rows
            for rows in scratch
        ],
        compiler_params=pltpu.CompilerParams(vmem_limit_bytes=LIM),
        cost_estimate=pl.CostEstimate(flops=cost, bytes_accessed=0, transcendentals=0)
        if cost
        else None,
    )(*operands)


def pair_swap(values, axis, start):
    pairs = []
    for i in range(start, lax.axis_size(axis) - 1, 2):
        pairs += [(i, i + 1), (i + 1, i)]
    if not pairs:
        return jnp.zeros_like(values)
    return lax.ppermute(values, axis, pairs)


def tracer_swap(values):
    return lax.ppermute(values, "tracer", [(0, 1), (1, 0)])


def all_prey(values):
    if lax.axis_size("tracer") == 2:
        return [values, tracer_swap(values)]
    return [lax.psum(values, "tracer")]


def neighbours(x_ev, x_od, y_ev, y_od):
    x_od = pair_swap(x_od, "gx", 1)
    y_ev = pair_swap(y_ev, "gy", 0)
    y_od = pair_swap(y_od, "gy", 1)
    x_ev = pair_swap(x_ev, "gx", 0)
    return x_ev, x_od, y_ev, y_od


def on_device(tracers, fluxes, diff_east, diff_north, column_depth, grazers, groups, preference):
    tr_dev, levels, rows, cols = tracers.shape
    parts = lax.axis_size("tracer")
    if not (cols == 128 and rows * levels == cols and levels == 2 * SUB and rows % SUB == 0):
        return plain(
            tracers, fluxes, diff_east, diff_north, column_depth, grazers, groups, preference
        )
    g = Geo(tr_dev, levels, rows, cols)
    total = float(tr_dev * parts)
    flat = tracers.reshape(-1, cols)
    grazers = grazers.reshape(-1, cols)
    cells = g.T * g.tile
    copies = pltpu.SemaphoreType.DMA((g.T,))

    if parts == 2:
        mine = fluxes.reshape(-1, cols)
        other = tracer_swap(mine)
    else:
        gathered = lax.all_gather(fluxes, "tracer", axis=1, tiled=True)
        mine, other = (gathered[:, i : i + SUB].reshape(-1, cols) for i in (0, SUB))
    field, strips, prey = call(
        functools.partial(load_kernel, g),
        [cells, g.T * g.SR, g.tile],
        [flat, groups, preference],
        scalars=(1, 2),
        far_out=None,
        scratch=[cells, copies],
    )
    prey = all_prey(prey)
    x_rows = g.T * 2 * g.L
    x_more = x_rows + g.L + 2 * SUB
    *messages, extra = call(
        functools.partial(first_messages_kernel, g),
        [x_more, x_more, g.my1 * SUB, g.my1 * SUB, 3 * g.SR],
        [field, strips, mine, other, column_depth, diff_east, diff_north],
    )
    messages = neighbours(*messages)
    part, inner = call(
        functools.partial(inside_kernel, g, INSIDE, True),
        [cells, g.inner.rows],
        [field, mine, other, column_depth, diff_east, diff_north],
    )
    *results, outer = call(
        functools.partial(step_one_kernel, g, total, FINISH),
        [cells, x_rows, x_rows, g.my2 * SUB, g.my2 * SUB, g.T * g.SR, g.tile, g.outer.rows],
        [field, part, strips, *messages, inner, extra, mine, other, column_depth, diff_east,
         grazers, groups, preference, *prey],
        scalars=(14, 15),
        scratch=[g.tile, g.T * g.SR],
    )
    field, *messages, strips, prey = results
    prey = all_prey(prey)
    messages = neighbours(*messages)
    (part,) = call(functools.partial(inside_kernel, g, INSIDE, False), [cells], [field, inner])
    (out,) = call(
        functools.partial(step_two_kernel, g, total, FINISH),
        [cells],
        [field, part, strips, *messages, inner, outer, grazers, groups, preference, *prey],
        scalars=(10, 11),
        far_out=True,
        scratch=[g.tile, g.T * g.SR, cells, copies],
    )
    return out.reshape(tracers.shape)


def solution(mesh):
    placed = (
        P("tracer", None, "gx", "gy"),
        P(None, "tracer", "gx", "gy"),
        P("gx", "gy"),
        P("gx", "gy"),
        P("gx", "gy"),
        P(None, "gx", "gy"),
        P("tracer"),
        P(),
    )
    return jax.shard_map(
        on_device,
        mesh=mesh,
        in_specs=placed,
        out_specs=P("tracer", None, "gx", "gy"),
        check_vma=False,
    )
```

```python
import functools

import jax
import jax.numpy as jnp
from jax import lax
from jax.experimental import pallas as pl
from jax.experimental.pallas import tpu as pltpu
from jax.sharding import PartitionSpec as P

STEPS = 2
SUB = 8
LIM = 48 * 1024 * 1024
INSIDE, FINISH = 3, 3


def with_halo(cells, sides, width):
    for axis, dim in sides:
        count = lax.axis_size(axis)
        ends = count - 1
        head = lax.slice_in_dim(cells, 0, width, axis=dim)
        tail = lax.slice_in_dim(cells, cells.shape[dim] - width, cells.shape[dim], axis=dim)
        cells = jnp.concatenate(
            [
                lax.ppermute(tail, axis, [(i, (i + 1) % count) for i in range(ends)]),
                cells,
                lax.ppermute(head, axis, [((i + 1) % count, i) for i in range(ends)]),
            ],
            axis=dim,
        )
    return cells


def minmod(jump_low, jump_high):
    return jnp.maximum(0.0, jnp.minimum(jump_low, jump_high)) + jnp.minimum(
        0.0, jnp.maximum(jump_low, jump_high)
    )


def window(values, low_end, high_end, direction):
    return lax.slice_in_dim(values, low_end, high_end, axis=direction % values.ndim)


def face_terms(tracer_field, open_faces, face_flux, face_kappa, direction):
    length = tracer_field.shape[direction % tracer_field.ndim] - 4
    jump_face = open_faces * (
        window(tracer_field, 1, length + 4, direction)
        - window(tracer_field, 0, length + 3, direction)
    )
    slopes = minmod(
        window(jump_face, 0, length + 2, direction), window(jump_face, 1, length + 3, direction)
    )
    left_value = window(tracer_field, 1, length + 2, direction) + 0.5 * window(
        slopes, 0, length + 1, direction
    )
    right_value = window(tracer_field, 2, length + 3, direction) - 0.5 * window(
        slopes, 1, length + 2, direction
    )
    carried = face_flux * jnp.where(face_flux > 0.0, left_value, right_value)
    if face_kappa is not None:
        carried = carried - face_kappa * window(jump_face, 1, length + 2, direction)
    return window(carried, 0, length, direction) - window(carried, 1, length + 1, direction)


def plain(tracers, fluxes, diff_east, diff_north, column_depth, grazers, groups, preference):
    tr_dev, levels, rows_dev, cols_dev = tracers.shape
    total_tracers = tr_dev * lax.axis_size("tracer")
    level_index = lax.broadcasted_iota(jnp.int32, (levels, rows_dev, cols_dev), 0)
    wet_cells = (level_index < column_depth[None]).astype(jnp.float32)
    all_fluxes = lax.all_gather(fluxes, "tracer", axis=1, tiled=True)
    stacked = jnp.concatenate(
        [all_fluxes[0], all_fluxes[1], wet_cells, diff_east[None], diff_north[None]], 0
    )
    rimmed = with_halo(stacked, (("gx", 1), ("gy", 2)), 2)
    east_ext = rimmed[:levels]
    north_ext = rimmed[levels : 2 * levels]
    downward = all_fluxes[2]
    wet_ext = rimmed[-(levels + 2) : -2]
    kx_ext = rimmed[-2]
    ky_ext = rimmed[-1]
    open_x = wet_ext[:, :-1, 2:-2] * wet_ext[:, 1:, 2:-2]
    open_y = wet_ext[:, 2:-2, :-1] * wet_ext[:, 2:-2, 1:]
    flux_x = east_ext[:, 1 : rows_dev + 2, 2:-2] * open_x[:, 1 : rows_dev + 2]
    kappa_x = kx_ext[None, 1 : rows_dev + 2, 2:-2] * open_x[:, 1 : rows_dev + 2]
    flux_y = north_ext[:, 2:-2, 1 : cols_dev + 2] * open_y[:, :, 1 : cols_dev + 2]
    kappa_y = ky_ext[None, 2:-2, 1 : cols_dev + 2] * open_y[:, :, 1 : cols_dev + 2]
    wet_z = jnp.pad(wet_cells, ((2, 2), (0, 0), (0, 0)))
    open_z = wet_z[:-1] * wet_z[1:]
    flux_z = jnp.pad(downward, ((1, 0), (0, 0), (0, 0))) * open_z[1 : levels + 2]
    group_match = (
        groups[:, None] == lax.broadcasted_iota(jnp.int32, (1, preference.shape[0]), 1)
    ).astype(jnp.float32)
    grazing_pref = jnp.sum(group_match * preference[None, :], axis=1)
    tracer_field = tracers
    for step_index in range(STEPS):
        prey_local = jnp.sum(grazing_pref[:, None, None, None] * tracer_field, axis=0)
        prey_total = lax.psum(prey_local, "tracer")
        factor = grazers / (1.0 + 4.0 * prey_total / total_tracers)
        extended = with_halo(tracer_field, (("gx", 2), ("gy", 3)), 2)
        tendency = face_terms(extended[:, :, :, 2:-2], open_x, flux_x, kappa_x, -2)
        tendency = tendency + face_terms(extended[:, :, 2:-2, :], open_y, flux_y, kappa_y, -1)
        padded_z = jnp.pad(tracer_field, ((0, 0), (2, 2), (0, 0), (0, 0)))
        tendency = tendency + face_terms(padded_z, open_z, flux_z, None, -3)
        tracer_field = (
            tracer_field + tendency - grazing_pref[:, None, None, None] * factor * tracer_field
        )
    return tracer_field


WIDE = 16
EACH = 128 // WIDE


class Geo:
    def __init__(self, tr_dev, levels, rows, cols):
        self.T, self.L, self.R, self.C = tr_dev, levels, rows, cols
        self.LH = levels // SUB
        self.tile = rows * levels
        self.K = rows * self.LH
        self.NV = self.K // EACH
        self.SR = self.NV * SUB
        self.my1 = -(-(tr_dev + 3) * self.NV // EACH)
        self.my2 = -(-tr_dev * self.NV // EACH)
        self.inner = Table(
            hx=(rows + 1) * self.LH, px=(rows + 1) * self.LH, mx=(rows + 1) * self.LH,
            kx=rows + 1, hy=self.K, py=self.K, my=self.K, ky=rows,
            hz=self.K, pz=self.K, mz=self.K,
        )
        self.outer = Table(
            hx=4 * self.LH, px=2 * self.LH, mx=2 * self.LH, kx=1,
            hs=self.NV, ps=self.NV, ms=self.NV, ks=self.NV,
        )


class Table:
    def __init__(self, **counts):
        self.at, self.rows = {}, 0
        for name, count in counts.items():
            self.at[name] = self.rows
            self.rows += count * SUB

    def get(self, ref, name, index):
        at = self.at[name] + index * SUB
        return ref[at : at + SUB, :]

    def set(self, ref, name, index, value):
        at = self.at[name] + index * SUB
        ref[at : at + SUB, :] = value

    def set_flux(self, ref, axis, index, opened, flux):
        flux = jnp.where(opened, flux, 0.0)
        self.set(ref, "p" + axis, index, jnp.maximum(flux, 0.0))
        self.set(ref, "m" + axis, index, jnp.minimum(flux, 0.0))

    def set_open(self, ref, axis, index, opened):
        self.set(ref, "h" + axis, index, jnp.where(opened, 0.5, 0.0))


def lanes():
    return lax.broadcasted_iota(jnp.int32, (SUB, 128), 1)


def sublanes():
    return lax.broadcasted_iota(jnp.int32, (SUB, 128), 0)


def roll(v, by, axis):
    by = by % v.shape[axis]
    return v if by == 0 else pltpu.roll(v, by, axis)


def registers(ref):
    return [ref[i : i + SUB, :] for i in range(0, ref.shape[0], SUB)]


def rows8(index):
    return pl.ds(pl.multiple_of(index * SUB, SUB), SUB)


def pack_strips(parts):
    lane = lanes()
    out = []
    for v in range(0, len(parts), EACH):
        packed = jnp.zeros((SUB, 128), jnp.float32)
        for k, part in enumerate(parts[v : v + EACH]):
            inside = (lane >= WIDE * k + 8) & (lane < WIDE * k + 16)
            packed = jnp.where(inside, roll(part, WIDE * k + 12, 1), packed)
        out.append(packed)
    return out


def message_strips(packed, low):
    place = lanes() % WIDE
    out = jnp.zeros((SUB, 128), jnp.float32)
    for m, one in enumerate(packed):
        moved = roll(one, 2 * m - (12 if low else 10), 1)
        out = jnp.where((place == 2 * m) | (place == 2 * m + 1), moved, out)
    return out


def put_messages(packed, even, ev_ref, od_ref):
    for v in range(0, len(packed), EACH):
        low = message_strips(packed[v : v + EACH], True)
        high = message_strips(packed[v : v + EACH], False)
        at = rows8(v // EACH)
        ev_ref[at, :] = jnp.where(even, high, low)
        od_ref[at, :] = jnp.where(even, low, high)


def full_strips(own, from_lower, from_upper, m):
    place = lanes() % WIDE
    out = jnp.where(place < 2, roll(from_lower, -2 * m, 1), 0.0)
    out = jnp.where((place >= 2) & (place < 6), roll(own, -10, 1), out)
    out = jnp.where((place >= 8) & (place < 12), own, out)
    return jnp.where((place >= 12) & (place < 14), roll(from_upper, 12 - 2 * m, 1), out)


def spread(rows, r):
    return jnp.broadcast_to(rows[r : r + 1, :], (SUB, 128))


def spread_rows(g, rows):
    return [spread(rows, r) for r in range(g.R) for _ in range(g.LH)]


def taste_of(groups_ref, pref_ref, t):
    return pref_ref[groups_ref[t]]


def is_even(axis):
    return lax.rem(lax.axis_index(axis), 2) == 0


def split_sides(even, ev, od):
    return jnp.where(even, od, ev), jnp.where(even, ev, od)


def limited(a, b):
    least, most = jnp.minimum(a, b), jnp.maximum(a, b)
    return jnp.maximum(least, jnp.minimum(most, 0.0))


def each_tracer(g, ahead, body):
    def some(i, carry):
        for more in range(ahead):
            body(i * ahead + more)
        return carry

    lax.fori_loop(0, g.T // ahead, some, 0)
    for t in range(g.T - g.T % ahead, g.T):
        body(t)


def flux_reader(g, mine_ref, other_ref):
    first = lax.axis_index("tracer") == 0
    single = lax.axis_size("tracer") != 2

    def flux(dim, r, lh):
        at = pl.ds(dim * g.R * SUB + r, SUB, stride=g.R)
        a, b = mine_ref[at, :], other_ref[at, :]
        if single:
            return (a, b)[lh]
        return jnp.where(first, (a, b)[lh], (b, a)[lh])

    return flux


def load_kernel(
    g, tracers_ref, groups_ref, pref_ref, field_ref, strips_ref, prey_ref, landed, sems
):
    def arrival(t):
        at = pl.ds(pl.multiple_of(t * g.tile, g.tile), g.tile)
        return pltpu.make_async_copy(tracers_ref.at[at, :], landed.at[at, :], sems.at[t])

    for t in range(g.T):
        arrival(t).start()
    prey_ref[...] = jnp.zeros_like(prey_ref)

    def one(t):
        arrival(t).wait()
        taste = taste_of(groups_ref, pref_ref, t)
        base = pl.multiple_of(t * g.tile, g.tile)
        parts = []
        for r in range(g.R):
            for lh in range(g.LH):
                at = (r * g.LH + lh) * SUB
                v = landed[pl.ds(base + lh * SUB * g.R + r, SUB, stride=g.R), :]
                field_ref[pl.ds(base + at, SUB), :] = v
                parts.append(v)
                prey_ref[at : at + SUB, :] += taste * v
        for i, packed in enumerate(pack_strips(parts)):
            strips_ref[rows8(t * g.NV + i), :] = packed

    each_tracer(g, 2, one)


def first_messages_kernel(
    g, field_ref, strips_ref, mine_ref, other_ref, depth_ref, east_ref, north_ref,
    xev_ref, xod_ref, yev_ref, yod_ref, extra_ref,
):
    x_even, y_even = is_even("gx"), is_even("gy")
    flux = flux_reader(g, mine_ref, other_ref)
    zero = jnp.zeros((SUB, 128), jnp.float32)

    def put(at, low, high):
        xev_ref[at, :] = jnp.where(x_even, high, low)
        xod_ref[at, :] = jnp.where(x_even, low, high)

    def one(t):
        base = pl.multiple_of(t * g.tile, g.tile)
        for i in range(2 * g.LH):
            low = field_ref[pl.ds(base + i * SUB, SUB), :]
            high = field_ref[pl.ds(base + g.tile - 2 * g.L + i * SUB, SUB), :]
            put(rows8(t * 2 * g.LH + i), low, high)

    each_tracer(g, 2, one)
    at = g.T * 2 * g.LH
    for lh in range(g.LH):
        put(rows8(at + lh), zero, flux(0, g.R - 1, lh))
    depth = depth_ref[...].astype(jnp.float32)
    put(rows8(at + g.LH), depth, roll(depth, 2, 0))
    put(rows8(at + g.LH + 1), zero, roll(east_ref[...], 1, 0))
    extras = pack_strips(spread_rows(g, depth))
    extras += pack_strips([flux(1, r, lh) for r in range(g.R) for lh in range(g.LH)])
    extras += pack_strips(spread_rows(g, north_ref[...]))
    for i, packed in enumerate(extras):
        extra_ref[rows8(i), :] = packed
    put_messages(registers(strips_ref) + extras, y_even, yev_ref, yod_ref)


def wet_levels(g, depths):
    level = [(sublanes() + SUB * lh).astype(jnp.float32) for lh in range(g.LH)]
    return [[level[lh] < d for lh in range(g.LH)] for d in depths]


def inner_coefficients(g, cf, flux, depth, east, north):
    tab, sub = g.inner, sublanes()
    depths = [spread(depth, r) for r in range(g.R)]
    wet = wet_levels(g, depths)
    wet_before = wet_levels(g, [roll(d, 1, 1) for d in depths])
    for r in range(g.R):
        tab.set(cf, "kx", r + 1, 2.0 * spread(east, r))
        tab.set(cf, "ky", r, 2.0 * roll(spread(north, r), 1, 1))
        flux_z = [roll(flux(2, r, lh), 1, 0) for lh in range(g.LH)]
        for lh in range(g.LH):
            k, here = r * g.LH + lh, wet[r][lh]
            if r:
                opened = here & wet[r - 1][lh]
                tab.set_open(cf, "x", k, opened)
                tab.set_flux(cf, "x", k, opened, flux(0, r - 1, lh))
            opened = here & wet_before[r][lh]
            tab.set_open(cf, "y", k, opened)
            tab.set_flux(cf, "y", k, opened, roll(flux(1, r, lh), 1, 1))
            opened = here if lh else here & (sub > 0)
            above = jnp.where(sub == 0, flux_z[lh - 1], flux_z[lh]) if lh else flux_z[lh]
            tab.set_open(cf, "z", k, opened)
            tab.set_flux(cf, "z", k, opened, above)


def outer_coefficients(g, cf, extra_x, extra_y, flux, extra_ref, depth, east):
    tab, lane = g.outer, lanes()
    depth_low, depth_high = extra_x(g.LH)
    depths = [spread(depth_low, 0), spread(depth_low, 1), spread(depth, 0), spread(depth, g.R - 1)]
    depths += [spread(depth_high, 0), spread(depth_high, 1)]
    wet = wet_levels(g, depths)
    tab.set(cf, "kx", 0, 2.0 * spread(extra_x(g.LH + 1)[0], 0))
    for lh in range(g.LH):
        for face, row in enumerate((0, 1, 3, 4)):
            tab.set_open(cf, "x", face * g.LH + lh, wet[row][lh] & wet[row + 1][lh])
        tab.set_flux(cf, "x", lh, wet[1][lh] & wet[2][lh], extra_x(lh)[0])
        tab.set_flux(cf, "x", g.LH + lh, wet[3][lh] & wet[4][lh], flux(0, g.R - 1, lh))
    place, half = lane % WIDE, (lane // WIDE) % g.LH
    for i in range(g.NV):
        full = []
        for which in range(3):
            own = which * g.NV + i
            slot = g.T * g.NV + own
            full.append(full_strips(extra_ref[rows8(own), :], *extra_y(slot // EACH), slot % EACH))
        wet_s = jnp.where((sublanes() + SUB * half).astype(jnp.float32) < full[0], 1.0, 0.0)
        opened = (wet_s * roll(wet_s, 1, 1) > 0.0) & (place != 0) & (place != 8)
        tab.set_open(cf, "s", i, opened)
        tab.set_flux(cf, "s", i, opened, roll(full[1], 1, 1))
        tab.set(cf, "ks", i, 2.0 * roll(full[2], 1, 1))


def end_lanes():
    lane = lanes()
    return (lane < 2) | (lane >= 126)


def inside_kernel(g, ahead, first, field_ref, *refs):
    if first:
        mine_ref, other_ref, depth_ref, east_ref, north_ref, part_ref, cf = refs
        inner_coefficients(
            g, cf, flux_reader(g, mine_ref, other_ref), depth_ref[...].astype(jnp.float32),
            east_ref[...], north_ref[...],
        )
    else:
        cf, part_ref = refs
    sub = sublanes()
    ends, top, bottom = end_lanes(), sub == 0, sub == SUB - 1

    def coef(name, index):
        return g.inner.get(cf, name, index)

    def shift_down(v):
        rolled = [roll(x, 1, 0) for x in v]
        return rolled[:1] + [
            jnp.where(top, rolled[i - 1], rolled[i]) for i in range(1, g.LH)
        ]

    def shift_up(v):
        rolled = [roll(x, -1, 0) for x in v]
        return [jnp.where(bottom, rolled[(i + 1) % g.LH], rolled[i]) for i in range(g.LH)]

    def one(t):
        base = pl.multiple_of(t * g.tile, g.tile)
        for r in range(g.R):
            index = [r * g.LH + lh for lh in range(g.LH)]
            at = [pl.ds(base + k * SUB, SUB) for k in index]
            cells = [field_ref[a, :] for a in at]
            news = []
            for k, c in zip(index, cells):
                j = coef("hy", k) * (c - roll(c, 1, 1))
                s = limited(j, roll(j, -1, 1))
                flow = coef("py", k) * roll(c + s, 1, 1) + coef("my", k) * (c - s)
                flow = flow - coef("ky", r) * j
                news.append(c + jnp.where(ends, 0.0, flow - roll(flow, -1, 1)))
            j = [coef("hz", k) * (c - a) for k, c, a in zip(index, cells, shift_down(cells))]
            s = [limited(a, b) for a, b in zip(j, shift_up(j))]
            above = shift_down([c + v for c, v in zip(cells, s)])
            flow = [
                coef("pz", k) * a + coef("mz", k) * (c - v)
                for k, a, c, v in zip(index, above, cells, s)
            ]
            for a, new, high, low in zip(at, news, flow, shift_up(flow)):
                part_ref[a, :] = new + (high - low)

    each_tracer(g, ahead, one)


def strip_tendency(g, cf, full, i):
    def coef(name):
        return g.outer.get(cf, name, i)

    j = coef("hs") * (full - roll(full, 1, 1))
    s = limited(j, roll(j, -1, 1))
    flow = coef("ps") * roll(full + s, 1, 1) + coef("ms") * (full - s) - coef("ks") * j
    tend = flow - roll(flow, -1, 1)
    return jnp.where(lanes() % WIDE < 12, tend, roll(tend, 10, 1))


def all_strip_tendencies(g, cf, strips_ref, sides, tend_ref):
    for n in range(g.T * g.NV):
        full = full_strips(strips_ref[rows8(n), :], *sides(n // EACH), n % EACH)
        tend_ref[rows8(n), :] = strip_tendency(g, cf, full, n % g.NV)


def set_factor(g, total, factor, grazers_ref, prey_refs):
    for r in range(g.R):
        for lh in range(g.LH):
            at = rows8(r * g.LH + lh)
            prey = sum(ref[at, :] for ref in prey_refs)
            grazers = grazers_ref[pl.ds(lh * SUB * g.R + r, SUB, stride=g.R), :]
            factor[at, :] = grazers / (1.0 + 4.0 * prey / total)


def finish(g, inner, outer, t, field_ref, part_ref, tend_ref, sides, taste, factor, emit):
    base = pl.multiple_of(t * g.tile, g.tile)
    ends = end_lanes()

    def cell(r, lh):
        if 0 <= r < g.R:
            return field_ref[pl.ds(base + (r * g.LH + lh) * SUB, SUB), :]
        i = r + 2 if r < 0 else r - g.R
        return sides(t * 2 * g.LH + i * g.LH + lh)[0 if r < 0 else 1]

    def coef(name, f, lh):
        if 0 < f < g.R:
            return g.inner.get(inner, name, f * g.LH + lh)
        if name == "hx":
            return g.outer.get(outer, name, {-1: 0, 0: 1, g.R: 2, g.R + 1: 3}[f] * g.LH + lh)
        return g.outer.get(outer, name, (g.LH if f else 0) + lh)

    state = [None] * g.LH
    tends = [tend_ref[rows8(t * g.NV + i), :] for i in range(g.NV)]
    for f in range(-1, g.R + 2):
        kappa = g.inner.get(inner, "kx", f) if f > 0 else g.outer.get(outer, "kx", 0)
        for lh in range(g.LH):
            if f < 0:
                below = cell(-2, lh)
                here = cell(-1, lh)
                state[lh] = (here, coef("hx", f, lh) * (here - below), None, None)
                continue
            c, j, left, carried = state[lh]
            up = cell(f, lh)
            j_up = coef("hx", f, lh) * (up - c)
            s = limited(j, j_up)
            if f > 0:
                kap = g.inner.get(inner, "kx", f - 1) if f > 1 else g.outer.get(outer, "kx", 0)
                flow = coef("px", f - 1, lh) * left + coef("mx", f - 1, lh) * (c - s) - kap * j
                if f > 1:
                    r = f - 2
                    k = r * g.LH + lh
                    v, n = divmod(k, EACH)
                    old = cell(r, lh)
                    new = part_ref[pl.ds(base + k * SUB, SUB), :] + (carried - flow)
                    new = new + jnp.where(ends, roll(tends[v], -(WIDE * n + 12), 1), 0.0)
                    new = new - (taste * factor[rows8(k), :]) * old
                    emit(r, lh, new)
                carried = flow
            state[lh] = (up, j_up, c + s, carried)


def reader(even, ev_ref, od_ref):
    def sides(i):
        at = rows8(i)
        return split_sides(even, ev_ref[at, :], od_ref[at, :])

    return sides


def step_one_kernel(
    g, total, ahead,
    field_ref, part_ref, strips_ref, xev_ref, xod_ref, yod_ref, yev_ref, inner, extra_ref,
    mine_ref, other_ref, depth_ref, east_ref, grazers_ref, groups_ref, pref_ref, *rest,
):
    prey_refs, rest = rest[:-10], rest[-10:]
    (out_ref, xev2_ref, xod2_ref, yev2_ref, yod2_ref, strips2_ref, prey2_ref, outer,
     factor, tend_ref) = rest
    x_even, y_even = is_even("gx"), is_even("gy")
    x_sides, y_sides = reader(x_even, xev_ref, xod_ref), reader(y_even, yev_ref, yod_ref)
    outer_coefficients(
        g, outer, lambda i: x_sides(g.T * 2 * g.LH + i), y_sides,
        flux_reader(g, mine_ref, other_ref), extra_ref,
        depth_ref[...].astype(jnp.float32), east_ref[...],
    )
    set_factor(g, total, factor, grazers_ref, prey_refs)
    all_strip_tendencies(g, outer, strips_ref, y_sides, tend_ref)
    prey2_ref[...] = jnp.zeros_like(prey2_ref)

    def one(t):
        taste = taste_of(groups_ref, pref_ref, t)
        base = pl.multiple_of(t * g.tile, g.tile)
        news = {}

        def emit(r, lh, new):
            at = (r * g.LH + lh) * SUB
            out_ref[pl.ds(base + at, SUB), :] = new
            prey2_ref[at : at + SUB, :] += taste * new
            news[r, lh] = new

        finish(g, inner, outer, t, field_ref, part_ref, tend_ref, x_sides, taste, factor, emit)
        for i in range(2):
            for lh in range(g.LH):
                at = rows8(t * 2 * g.LH + i * g.LH + lh)
                low, high = news[i, lh], news[g.R - 2 + i, lh]
                xev2_ref[at, :] = jnp.where(x_even, high, low)
                xod2_ref[at, :] = jnp.where(x_even, low, high)
        parts = [news[r, lh] for r in range(g.R) for lh in range(g.LH)]
        for i, packed in enumerate(pack_strips(parts)):
            strips2_ref[rows8(t * g.NV + i), :] = packed

    each_tracer(g, ahead, one)
    put_messages(registers(strips2_ref), y_even, yev2_ref, yod2_ref)


def step_two_kernel(
    g, total, ahead,
    field_ref, part_ref, strips_ref, xev_ref, xod_ref, yev_ref, yod_ref, inner, outer,
    grazers_ref, groups_ref, pref_ref, *rest,
):
    prey_refs, (out_ref, factor, tend_ref, leaving, sems) = rest[:-5], rest[-5:]
    x_sides = reader(is_even("gx"), xev_ref, xod_ref)
    y_sides = reader(is_even("gy"), yev_ref, yod_ref)
    set_factor(g, total, factor, grazers_ref, prey_refs)
    all_strip_tendencies(g, outer, strips_ref, y_sides, tend_ref)

    def departure(t):
        at = pl.ds(pl.multiple_of(t * g.tile, g.tile), g.tile)
        return pltpu.make_async_copy(leaving.at[at, :], out_ref.at[at, :], sems.at[t])

    def one(t):
        taste = taste_of(groups_ref, pref_ref, t)
        base = pl.multiple_of(t * g.tile, g.tile)

        def emit(r, lh, new):
            leaving[pl.ds(base + lh * SUB * g.R + r, SUB, stride=g.R), :] = new

        finish(g, inner, outer, t, field_ref, part_ref, tend_ref, x_sides, taste, factor, emit)
        departure(t).start()

    each_tracer(g, ahead, one)
    for t in range(g.T):
        departure(t).wait()


def call(body, outs, operands, scalars=(), far_out=False, scratch=(), cost=0):
    spaces = [pltpu.SMEM if i in scalars else pltpu.VMEM for i in range(len(operands))]
    if far_out is None:
        spaces[0] = pltpu.HBM
        operands = [pltpu.with_memory_space_constraint(operands[0], pltpu.HBM), *operands[1:]]
    return pl.pallas_call(
        body,
        out_shape=[jax.ShapeDtypeStruct((rows, 128), jnp.float32) for rows in outs],
        in_specs=[pl.BlockSpec(memory_space=space) for space in spaces],
        out_specs=[pl.BlockSpec(memory_space=pltpu.HBM if far_out else pltpu.VMEM)] * len(outs),
        scratch_shapes=[
            pltpu.VMEM((rows, 128), jnp.float32) if isinstance(rows, int) else rows
            for rows in scratch
        ],
        compiler_params=pltpu.CompilerParams(vmem_limit_bytes=LIM),
        cost_estimate=pl.CostEstimate(flops=cost, bytes_accessed=0, transcendentals=0)
        if cost
        else None,
    )(*operands)


def pair_swap(values, axis, start):
    pairs = []
    for i in range(start, lax.axis_size(axis) - 1, 2):
        pairs += [(i, i + 1), (i + 1, i)]
    if not pairs:
        return jnp.zeros_like(values)
    return lax.ppermute(values, axis, pairs)


def tracer_swap(values):
    return lax.ppermute(values, "tracer", [(0, 1), (1, 0)])


def all_prey(values):
    if lax.axis_size("tracer") == 2:
        return [values, tracer_swap(values)]
    return [lax.psum(values, "tracer")]


def neighbours(x_ev, x_od, y_ev, y_od):
    x_od = pair_swap(x_od, "gx", 1)
    y_ev = pair_swap(y_ev, "gy", 0)
    y_od = pair_swap(y_od, "gy", 1)
    x_ev = pair_swap(x_ev, "gx", 0)
    return x_ev, x_od, y_ev, y_od


def on_device(tracers, fluxes, diff_east, diff_north, column_depth, grazers, groups, preference):
    tr_dev, levels, rows, cols = tracers.shape
    parts = lax.axis_size("tracer")
    if not (cols == 128 and rows * levels == cols and levels == 2 * SUB and rows % SUB == 0):
        return plain(
            tracers, fluxes, diff_east, diff_north, column_depth, grazers, groups, preference
        )
    g = Geo(tr_dev, levels, rows, cols)
    total = float(tr_dev * parts)
    flat = tracers.reshape(-1, cols)
    grazers = grazers.reshape(-1, cols)
    cells = g.T * g.tile
    copies = pltpu.SemaphoreType.DMA((g.T,))

    if parts == 2:
        mine = fluxes.reshape(-1, cols)
        other = tracer_swap(mine)
    else:
        gathered = lax.all_gather(fluxes, "tracer", axis=1, tiled=True)
        mine, other = (gathered[:, i : i + SUB].reshape(-1, cols) for i in (0, SUB))
    field, strips, prey = call(
        functools.partial(load_kernel, g),
        [cells, g.T * g.SR, g.T * 2 * g.L + g.L + 3 * SUB],
        [flat, groups, preference],
        scalars=(1, 2),
        far_out=None,
        scratch=[cells, copies],
    )
    prey = all_prey(prey)
    x_rows = g.T * 2 * g.L
    x_more = x_rows + g.L + 2 * SUB
    *messages, extra = call(
        functools.partial(first_messages_kernel, g),
        [x_more, x_more, g.my1 * SUB, g.my1 * SUB, 3 * g.SR],
        [field, strips, mine, other, column_depth, diff_east, diff_north],
    )
    messages = neighbours(*messages)
    messages = messages[0], messages[1], messages[3], messages[2]
    part, inner = call(
        functools.partial(inside_kernel, g, INSIDE, True),
        [cells, g.inner.rows],
        [field, mine, other, column_depth, diff_east, diff_north],
    )
    *results, outer = call(
        functools.partial(step_one_kernel, g, total, FINISH),
        [cells, x_rows, x_rows, g.my2 * SUB, g.my2 * SUB, g.T * g.SR, g.tile, g.outer.rows],
        [field, part, strips, *messages, inner, extra, mine, other, column_depth, diff_east,
         grazers, groups, preference, *prey],
        scalars=(14, 15),
        scratch=[g.tile, g.T * g.SR],
    )
    field, *messages, strips, prey = results
    prey = all_prey(prey)
    messages = neighbours(*messages)
    (part,) = call(functools.partial(inside_kernel, g, INSIDE, False), [cells], [field, inner])
    (out,) = call(
        functools.partial(step_two_kernel, g, total, FINISH),
        [cells],
        [field, part, strips, *messages, inner, outer, grazers, groups, preference, *prey],
        scalars=(10, 11),
        far_out=True,
        scratch=[g.tile, g.T * g.SR, cells, copies],
    )
    return out.reshape(tracers.shape)


def solution(mesh):
    placed = (
        P("tracer", None, "gx", "gy"),
        P(None, "tracer", "gx", "gy"),
        P("gx", "gy"),
        P("gx", "gy"),
        P("gx", "gy"),
        P(None, "gx", "gy"),
        P("tracer"),
        P(),
    )
    return jax.shard_map(
        on_device,
        mesh=mesh,
        in_specs=placed,
        out_specs=P("tracer", None, "gx", "gy"),
        check_vma=False,
    )
```

```python
import functools

import jax
import jax.numpy as jnp
from jax import lax
from jax.experimental import pallas as pl
from jax.experimental.pallas import tpu as pltpu
from jax.sharding import PartitionSpec as P

STEPS = 2
SUB = 8
LIM = 48 * 1024 * 1024
INSIDE, FINISH = 3, 3


def with_halo(cells, sides, width):
    for axis, dim in sides:
        count = lax.axis_size(axis)
        ends = count - 1
        head = lax.slice_in_dim(cells, 0, width, axis=dim)
        tail = lax.slice_in_dim(cells, cells.shape[dim] - width, cells.shape[dim], axis=dim)
        cells = jnp.concatenate(
            [
                lax.ppermute(tail, axis, [(i, (i + 1) % count) for i in range(ends)]),
                cells,
                lax.ppermute(head, axis, [((i + 1) % count, i) for i in range(ends)]),
            ],
            axis=dim,
        )
    return cells


def minmod(jump_low, jump_high):
    return jnp.maximum(0.0, jnp.minimum(jump_low, jump_high)) + jnp.minimum(
        0.0, jnp.maximum(jump_low, jump_high)
    )


def window(values, low_end, high_end, direction):
    return lax.slice_in_dim(values, low_end, high_end, axis=direction % values.ndim)


def face_terms(tracer_field, open_faces, face_flux, face_kappa, direction):
    length = tracer_field.shape[direction % tracer_field.ndim] - 4
    jump_face = open_faces * (
        window(tracer_field, 1, length + 4, direction)
        - window(tracer_field, 0, length + 3, direction)
    )
    slopes = minmod(
        window(jump_face, 0, length + 2, direction), window(jump_face, 1, length + 3, direction)
    )
    left_value = window(tracer_field, 1, length + 2, direction) + 0.5 * window(
        slopes, 0, length + 1, direction
    )
    right_value = window(tracer_field, 2, length + 3, direction) - 0.5 * window(
        slopes, 1, length + 2, direction
    )
    carried = face_flux * jnp.where(face_flux > 0.0, left_value, right_value)
    if face_kappa is not None:
        carried = carried - face_kappa * window(jump_face, 1, length + 2, direction)
    return window(carried, 0, length, direction) - window(carried, 1, length + 1, direction)


def plain(tracers, fluxes, diff_east, diff_north, column_depth, grazers, groups, preference):
    tr_dev, levels, rows_dev, cols_dev = tracers.shape
    total_tracers = tr_dev * lax.axis_size("tracer")
    level_index = lax.broadcasted_iota(jnp.int32, (levels, rows_dev, cols_dev), 0)
    wet_cells = (level_index < column_depth[None]).astype(jnp.float32)
    all_fluxes = lax.all_gather(fluxes, "tracer", axis=1, tiled=True)
    stacked = jnp.concatenate(
        [all_fluxes[0], all_fluxes[1], wet_cells, diff_east[None], diff_north[None]], 0
    )
    rimmed = with_halo(stacked, (("gx", 1), ("gy", 2)), 2)
    east_ext = rimmed[:levels]
    north_ext = rimmed[levels : 2 * levels]
    downward = all_fluxes[2]
    wet_ext = rimmed[-(levels + 2) : -2]
    kx_ext = rimmed[-2]
    ky_ext = rimmed[-1]
    open_x = wet_ext[:, :-1, 2:-2] * wet_ext[:, 1:, 2:-2]
    open_y = wet_ext[:, 2:-2, :-1] * wet_ext[:, 2:-2, 1:]
    flux_x = east_ext[:, 1 : rows_dev + 2, 2:-2] * open_x[:, 1 : rows_dev + 2]
    kappa_x = kx_ext[None, 1 : rows_dev + 2, 2:-2] * open_x[:, 1 : rows_dev + 2]
    flux_y = north_ext[:, 2:-2, 1 : cols_dev + 2] * open_y[:, :, 1 : cols_dev + 2]
    kappa_y = ky_ext[None, 2:-2, 1 : cols_dev + 2] * open_y[:, :, 1 : cols_dev + 2]
    wet_z = jnp.pad(wet_cells, ((2, 2), (0, 0), (0, 0)))
    open_z = wet_z[:-1] * wet_z[1:]
    flux_z = jnp.pad(downward, ((1, 0), (0, 0), (0, 0))) * open_z[1 : levels + 2]
    group_match = (
        groups[:, None] == lax.broadcasted_iota(jnp.int32, (1, preference.shape[0]), 1)
    ).astype(jnp.float32)
    grazing_pref = jnp.sum(group_match * preference[None, :], axis=1)
    tracer_field = tracers
    for step_index in range(STEPS):
        prey_local = jnp.sum(grazing_pref[:, None, None, None] * tracer_field, axis=0)
        prey_total = lax.psum(prey_local, "tracer")
        factor = grazers / (1.0 + 4.0 * prey_total / total_tracers)
        extended = with_halo(tracer_field, (("gx", 2), ("gy", 3)), 2)
        tendency = face_terms(extended[:, :, :, 2:-2], open_x, flux_x, kappa_x, -2)
        tendency = tendency + face_terms(extended[:, :, 2:-2, :], open_y, flux_y, kappa_y, -1)
        padded_z = jnp.pad(tracer_field, ((0, 0), (2, 2), (0, 0), (0, 0)))
        tendency = tendency + face_terms(padded_z, open_z, flux_z, None, -3)
        tracer_field = (
            tracer_field + tendency - grazing_pref[:, None, None, None] * factor * tracer_field
        )
    return tracer_field


WIDE = 16
EACH = 128 // WIDE


class Geo:
    def __init__(self, tr_dev, levels, rows, cols):
        self.T, self.L, self.R, self.C = tr_dev, levels, rows, cols
        self.LH = levels // SUB
        self.tile = rows * levels
        self.K = rows * self.LH
        self.NV = self.K // EACH
        self.SR = self.NV * SUB
        self.my1 = -(-(tr_dev + 3) * self.NV // EACH)
        self.my2 = -(-tr_dev * self.NV // EACH)
        self.inner = Table(
            hx=(rows + 1) * self.LH, px=(rows + 1) * self.LH, mx=(rows + 1) * self.LH,
            kx=rows + 1, hy=self.K, py=self.K, my=self.K, ky=rows,
            hz=self.K, pz=self.K, mz=self.K,
        )
        self.outer = Table(
            hx=4 * self.LH, px=2 * self.LH, mx=2 * self.LH, kx=1
        )
        self.ends = Table(
            hs=4 * self.NV, ps=2 * self.NV, ms=2 * self.NV, ks=2 * self.NV
        )


class Table:
    def __init__(self, **counts):
        self.at, self.rows = {}, 0
        for name, count in counts.items():
            self.at[name] = self.rows
            self.rows += count * SUB

    def get(self, ref, name, index):
        at = self.at[name] + index * SUB
        return ref[at : at + SUB, :]

    def set(self, ref, name, index, value):
        at = self.at[name] + index * SUB
        ref[at : at + SUB, :] = value

    def set_flux(self, ref, axis, index, opened, flux):
        flux = jnp.where(opened, flux, 0.0)
        self.set(ref, "p" + axis, index, jnp.maximum(flux, 0.0))
        self.set(ref, "m" + axis, index, jnp.minimum(flux, 0.0))

    def set_open(self, ref, axis, index, opened):
        self.set(ref, "h" + axis, index, jnp.where(opened, 0.5, 0.0))


def lanes():
    return lax.broadcasted_iota(jnp.int32, (SUB, 128), 1)


def sublanes():
    return lax.broadcasted_iota(jnp.int32, (SUB, 128), 0)


def roll(v, by, axis):
    by = by % v.shape[axis]
    return v if by == 0 else pltpu.roll(v, by, axis)


def registers(ref):
    return [ref[i : i + SUB, :] for i in range(0, ref.shape[0], SUB)]


def rows8(index):
    return pl.ds(pl.multiple_of(index * SUB, SUB), SUB)


def pack_strips(parts):
    lane = lanes()
    out = []
    for v in range(0, len(parts), EACH):
        packed = jnp.zeros((SUB, 128), jnp.float32)
        for k, part in enumerate(parts[v : v + EACH]):
            inside = (lane >= WIDE * k + 8) & (lane < WIDE * k + 16)
            packed = jnp.where(inside, roll(part, WIDE * k + 12, 1), packed)
        out.append(packed)
    return out


def message_strips(packed, low):
    place = lanes() % WIDE
    out = jnp.zeros((SUB, 128), jnp.float32)
    for m, one in enumerate(packed):
        moved = roll(one, 2 * m - (12 if low else 10), 1)
        out = jnp.where((place == 2 * m) | (place == 2 * m + 1), moved, out)
    return out


def put_messages(packed, even, ev_ref, od_ref):
    for v in range(0, len(packed), EACH):
        low = message_strips(packed[v : v + EACH], True)
        high = message_strips(packed[v : v + EACH], False)
        at = rows8(v // EACH)
        ev_ref[at, :] = jnp.where(even, high, low)
        od_ref[at, :] = jnp.where(even, low, high)


def full_strips(own, from_lower, from_upper, m):
    place = lanes() % WIDE
    out = jnp.where(place < 2, roll(from_lower, -2 * m, 1), 0.0)
    out = jnp.where((place >= 2) & (place < 6), roll(own, -10, 1), out)
    out = jnp.where((place >= 8) & (place < 12), own, out)
    return jnp.where((place >= 12) & (place < 14), roll(from_upper, 12 - 2 * m, 1), out)


def spread(rows, r):
    return jnp.broadcast_to(rows[r : r + 1, :], (SUB, 128))


def spread_rows(g, rows):
    return [spread(rows, r) for r in range(g.R) for _ in range(g.LH)]


def taste_of(taste_ref, t):
    return taste_ref[rows8(t), :]


def is_even(axis):
    return lax.rem(lax.axis_index(axis), 2) == 0


def split_sides(even, ev, od):
    return jnp.where(even, od, ev), jnp.where(even, ev, od)


def limited(a, b):
    least, most = jnp.minimum(a, b), jnp.maximum(a, b)
    return jnp.maximum(least, jnp.minimum(most, 0.0))


def each_tracer(g, ahead, body):
    def some(i, carry):
        for more in range(ahead):
            body(i * ahead + more)
        return carry

    lax.fori_loop(0, g.T // ahead, some, 0)
    for t in range(g.T - g.T % ahead, g.T):
        body(t)


def flux_reader(g, mine_ref, other_ref):
    first = lax.axis_index("tracer") == 0
    single = lax.axis_size("tracer") != 2

    def flux(dim, r, lh):
        at = pl.ds(dim * g.R * SUB + r, SUB, stride=g.R)
        a, b = mine_ref[at, :], other_ref[at, :]
        if single:
            return (a, b)[lh]
        return jnp.where(first, (a, b)[lh], (b, a)[lh])

    return flux


def load_kernel(
    g, tracers_ref, groups_far, pref_far, field_ref, strips_ref, prey_ref, taste_ref,
    landed, sems, groups_ref, pref_ref, small_sems,
):
    def arrival(t):
        at = pl.ds(pl.multiple_of(t * g.tile, g.tile), g.tile)
        return pltpu.make_async_copy(tracers_ref.at[at, :], landed.at[at, :], sems.at[t])

    small = [
        pltpu.make_async_copy(a, b, small_sems.at[i])
        for i, (a, b) in enumerate(((groups_far, groups_ref), (pref_far, pref_ref)))
    ]
    for copy in small:
        copy.start()
    for t in range(g.T):
        arrival(t).start()
    prey_ref[...] = jnp.zeros_like(prey_ref)

    for copy in small:
        copy.wait()
    for t in range(g.T):
        taste_ref[rows8(t), :] = jnp.full((SUB, 128), pref_ref[groups_ref[t]], jnp.float32)

    def one(t):
        arrival(t).wait()
        taste = taste_of(taste_ref, t)
        base = pl.multiple_of(t * g.tile, g.tile)
        parts = []
        for r in range(g.R):
            for lh in range(g.LH):
                at = (r * g.LH + lh) * SUB
                v = landed[pl.ds(base + lh * SUB * g.R + r, SUB, stride=g.R), :]
                field_ref[pl.ds(base + at, SUB), :] = v
                parts.append(v)
                prey_ref[at : at + SUB, :] += taste * v
        for i, packed in enumerate(pack_strips(parts)):
            strips_ref[rows8(t * g.NV + i), :] = packed

    each_tracer(g, 2, one)


def first_messages_kernel(
    g, field_ref, strips_ref, mine_ref, other_ref, depth_ref, east_ref, north_ref,
    xev_ref, xod_ref, yev_ref, yod_ref, extra_ref,
):
    x_even, y_even = is_even("gx"), is_even("gy")
    flux = flux_reader(g, mine_ref, other_ref)
    zero = jnp.zeros((SUB, 128), jnp.float32)

    def put(at, low, high):
        xev_ref[at, :] = jnp.where(x_even, high, low)
        xod_ref[at, :] = jnp.where(x_even, low, high)

    def one(t):
        base = pl.multiple_of(t * g.tile, g.tile)
        for i in range(2 * g.LH):
            low = field_ref[pl.ds(base + i * SUB, SUB), :]
            high = field_ref[pl.ds(base + g.tile - 2 * g.L + i * SUB, SUB), :]
            put(rows8(t * 2 * g.LH + i), low, high)

    each_tracer(g, 2, one)
    at = g.T * 2 * g.LH
    for lh in range(g.LH):
        put(rows8(at + lh), zero, flux(0, g.R - 1, lh))
    depth = depth_ref[...].astype(jnp.float32)
    put(rows8(at + g.LH), depth, roll(depth, 2, 0))
    put(rows8(at + g.LH + 1), zero, roll(east_ref[...], 1, 0))
    extras = pack_strips(spread_rows(g, depth))
    extras += pack_strips([flux(1, r, lh) for r in range(g.R) for lh in range(g.LH)])
    extras += pack_strips(spread_rows(g, north_ref[...]))
    for i, packed in enumerate(extras):
        extra_ref[rows8(i), :] = packed
    put_messages(registers(strips_ref) + extras, y_even, yev_ref, yod_ref)


def wet_levels(g, depths):
    level = [(sublanes() + SUB * lh).astype(jnp.float32) for lh in range(g.LH)]
    return [[level[lh] < d for lh in range(g.LH)] for d in depths]


def inner_coefficients(g, cf, flux, depth, east, north):
    tab, sub = g.inner, sublanes()
    depths = [spread(depth, r) for r in range(g.R)]
    wet = wet_levels(g, depths)
    wet_before = wet_levels(g, [roll(d, 1, 1) for d in depths])
    for r in range(g.R):
        tab.set(cf, "kx", r + 1, 2.0 * spread(east, r))
        tab.set(cf, "ky", r, 2.0 * roll(spread(north, r), 1, 1))
        flux_z = [roll(flux(2, r, lh), 1, 0) for lh in range(g.LH)]
        for lh in range(g.LH):
            k, here = r * g.LH + lh, wet[r][lh]
            if r:
                opened = here & wet[r - 1][lh]
                tab.set_open(cf, "x", k, opened)
                tab.set_flux(cf, "x", k, opened, flux(0, r - 1, lh))
            opened = here & wet_before[r][lh]
            tab.set_open(cf, "y", k, opened)
            tab.set_flux(cf, "y", k, opened, roll(flux(1, r, lh), 1, 1))
            opened = here if lh else here & (sub > 0)
            above = jnp.where(sub == 0, flux_z[lh - 1], flux_z[lh]) if lh else flux_z[lh]
            tab.set_open(cf, "z", k, opened)
            tab.set_flux(cf, "z", k, opened, above)


def outer_coefficients(g, cf, extra_x, flux, depth, east):
    tab = g.outer
    depth_low, depth_high = extra_x(g.LH)
    depths = [spread(depth_low, 0), spread(depth_low, 1), spread(depth, 0), spread(depth, g.R - 1)]
    depths += [spread(depth_high, 0), spread(depth_high, 1)]
    wet = wet_levels(g, depths)
    tab.set(cf, "kx", 0, 2.0 * spread(extra_x(g.LH + 1)[0], 0))
    for lh in range(g.LH):
        for face, row in enumerate((0, 1, 3, 4)):
            tab.set_open(cf, "x", face * g.LH + lh, wet[row][lh] & wet[row + 1][lh])
        tab.set_flux(cf, "x", lh, wet[1][lh] & wet[2][lh], extra_x(lh)[0])
        tab.set_flux(cf, "x", g.LH + lh, wet[3][lh] & wet[4][lh], flux(0, g.R - 1, lh))


def strip_coefficients(g, cf, extra_y, extra_ref):
    tab, lane = g.ends, lanes()
    half = (lane // WIDE) % g.LH
    level = (sublanes() + SUB * half).astype(jnp.float32)
    for i in range(g.NV):
        full = []
        for which in range(3):
            own = which * g.NV + i
            slot = g.T * g.NV + own
            full.append(full_strips(extra_ref[rows8(own), :], *extra_y(slot // EACH), slot % EACH))
        wet = [level < roll(full[0], -away, 1) for away in (-2, -1, 0, 1, 2)]
        opened = [a & b for a, b in zip(wet, wet[1:])]
        for face in range(4):
            tab.set_open(cf, "s", face * g.NV + i, opened[face])
        for face in range(2):
            flux, kappa = (roll(v, 1 - face, 1) for v in full[1:])
            tab.set_flux(cf, "s", face * g.NV + i, opened[1 + face], flux)
            tab.set(cf, "ks", face * g.NV + i, 2.0 * kappa)


def end_lanes():
    lane = lanes()
    return (lane < 2) | (lane >= 126)


def inside_kernel(g, ahead, first, field_ref, *refs):
    if first:
        mine_ref, other_ref, depth_ref, east_ref, north_ref, part_ref, cf = refs
        inner_coefficients(
            g, cf, flux_reader(g, mine_ref, other_ref), depth_ref[...].astype(jnp.float32),
            east_ref[...], north_ref[...],
        )
    else:
        tend_ref, cf, whole_ref, part_ref = refs
    sub = sublanes()
    ends, top, bottom = end_lanes(), sub == 0, sub == SUB - 1

    def coef(name, index):
        return g.inner.get(cf, name, index)

    def shift_down(v):
        rolled = [roll(x, 1, 0) for x in v]
        return rolled[:1] + [
            jnp.where(top, rolled[i - 1], rolled[i]) for i in range(1, g.LH)
        ]

    def shift_up(v):
        rolled = [roll(x, -1, 0) for x in v]
        return [jnp.where(bottom, rolled[(i + 1) % g.LH], rolled[i]) for i in range(g.LH)]

    def one(t):
        base = pl.multiple_of(t * g.tile, g.tile)
        for r in range(g.R):
            index = [r * g.LH + lh for lh in range(g.LH)]
            at = [pl.ds(base + k * SUB, SUB) for k in index]
            cells = [field_ref[a, :] for a in at]
            if not first:
                cells = [c + end_columns(g, tend_ref, t, k) for k, c in zip(index, cells)]
                for a, c in zip(at, cells):
                    whole_ref[a, :] = c
            news = []
            for k, c in zip(index, cells):
                j = coef("hy", k) * (c - roll(c, 1, 1))
                s = limited(j, roll(j, -1, 1))
                flow = coef("py", k) * roll(c + s, 1, 1) + coef("my", k) * (c - s)
                flow = flow - coef("ky", r) * j
                news.append(c + jnp.where(ends, 0.0, flow - roll(flow, -1, 1)))
            j = [coef("hz", k) * (c - a) for k, c, a in zip(index, cells, shift_down(cells))]
            s = [limited(a, b) for a, b in zip(j, shift_up(j))]
            above = shift_down([c + v for c, v in zip(cells, s)])
            flow = [
                coef("pz", k) * a + coef("mz", k) * (c - v)
                for k, a, c, v in zip(index, above, cells, s)
            ]
            for a, new, high, low in zip(at, news, flow, shift_up(flow)):
                part_ref[a, :] = new + (high - low)

    each_tracer(g, ahead, one)


def strip_tendency(g, cf, full, i):
    def coef(name, face):
        return g.ends.get(cf, name, face * g.NV + i)

    cell = [roll(full, -away, 1) for away in (-2, -1, 0, 1, 2)]
    j = [coef("hs", face) * (cell[face + 1] - cell[face]) for face in range(4)]
    s = [limited(a, b) for a, b in zip(j, j[1:])]
    flow = [
        coef("ps", f) * (cell[f + 1] + s[f])
        + coef("ms", f) * (cell[f + 2] - s[f + 1])
        - coef("ks", f) * j[f + 1]
        for f in range(2)
    ]
    tend = flow[0] - flow[1]
    place = lanes() % WIDE
    tend = jnp.where(place < 12, tend, roll(tend, 10, 1))
    return jnp.where((place >= 10) & (place < 14), tend, 0.0)


def all_strip_tendencies(g, cf, strips_ref, sides, tend_ref):
    for n in range(g.T * g.NV):
        full = full_strips(strips_ref[rows8(n), :], *sides(n // EACH), n % EACH)
        tend_ref[rows8(n), :] = strip_tendency(g, cf, full, n % g.NV)


def end_columns(g, tend_ref, t, k):
    v, n = divmod(k, EACH)
    return jnp.where(end_lanes(), roll(tend_ref[rows8(t * g.NV + v), :], -(WIDE * n + 12), 1), 0.0)


def set_factor(g, total, factor, grazers_ref, prey_refs):
    for r in range(g.R):
        for lh in range(g.LH):
            at = rows8(r * g.LH + lh)
            prey = sum(ref[at, :] for ref in prey_refs)
            grazers = grazers_ref[pl.ds(lh * SUB * g.R + r, SUB, stride=g.R), :]
            factor[at, :] = grazers / (1.0 + 4.0 * prey / total)


def finish(g, inner, outer, t, field_ref, part_ref, sides, taste, factor, emit):
    base = pl.multiple_of(t * g.tile, g.tile)

    def cell(r, lh):
        if 0 <= r < g.R:
            return field_ref[pl.ds(base + (r * g.LH + lh) * SUB, SUB), :]
        i = r + 2 if r < 0 else r - g.R
        return sides(t * 2 * g.LH + i * g.LH + lh)[0 if r < 0 else 1]

    def coef(name, f, lh):
        if 0 < f < g.R:
            return g.inner.get(inner, name, f * g.LH + lh)
        if name == "hx":
            return g.outer.get(outer, name, {-1: 0, 0: 1, g.R: 2, g.R + 1: 3}[f] * g.LH + lh)
        return g.outer.get(outer, name, (g.LH if f else 0) + lh)

    state = [None] * g.LH
    for f in range(-1, g.R + 2):
        for lh in range(g.LH):
            if f < 0:
                below = cell(-2, lh)
                here = cell(-1, lh)
                state[lh] = (here, coef("hx", f, lh) * (here - below), None, None)
                continue
            c, j, left, carried = state[lh]
            up = cell(f, lh)
            j_up = coef("hx", f, lh) * (up - c)
            s = limited(j, j_up)
            if f > 0:
                kap = g.inner.get(inner, "kx", f - 1) if f > 1 else g.outer.get(outer, "kx", 0)
                flow = coef("px", f - 1, lh) * left + coef("mx", f - 1, lh) * (c - s) - kap * j
                if f > 1:
                    r = f - 2
                    k = r * g.LH + lh
                    old = cell(r, lh)
                    new = part_ref[pl.ds(base + k * SUB, SUB), :] + (carried - flow)
                    new = new - (taste * factor[rows8(k), :]) * old
                    emit(r, lh, new)
                carried = flow
            state[lh] = (up, j_up, c + s, carried)


def reader(even, ev_ref, od_ref):
    def sides(i):
        at = rows8(i)
        return split_sides(even, ev_ref[at, :], od_ref[at, :])

    return sides


def border_kernel(
    g, total, ahead,
    field_ref, part_ref, xev_ref, xod_ref, inner, mine_ref, other_ref, depth_ref, east_ref,
    grazers_ref, taste_ref, *rest,
):
    prey_refs, (out_ref, strips_ref, prey_ref, outer, factor) = rest[:-5], rest[-5:]
    x_sides = reader(is_even("gx"), xev_ref, xod_ref)
    outer_coefficients(
        g, outer, lambda i: x_sides(g.T * 2 * g.LH + i), flux_reader(g, mine_ref, other_ref),
        depth_ref[...].astype(jnp.float32), east_ref[...],
    )
    set_factor(g, total, factor, grazers_ref, prey_refs)
    prey_ref[...] = jnp.zeros_like(prey_ref)

    def one(t):
        taste = taste_of(taste_ref, t)
        base = pl.multiple_of(t * g.tile, g.tile)
        news = {}

        def emit(r, lh, new):
            at = (r * g.LH + lh) * SUB
            out_ref[pl.ds(base + at, SUB), :] = new
            prey_ref[at : at + SUB, :] += taste * new
            news[r, lh] = new

        finish(g, inner, outer, t, field_ref, part_ref, x_sides, taste, factor, emit)
        parts = [news[r, lh] for r in range(g.R) for lh in range(g.LH)]
        for i, packed in enumerate(pack_strips(parts)):
            strips_ref[rows8(t * g.NV + i), :] = packed

    each_tracer(g, ahead, one)


def second_messages_kernel(
    g, field_ref, strips_ref, next_ref, prey_ref, extra_ref, yod_ref, yev_ref, taste_ref,
    xev2_ref, xod2_ref, yev2_ref, yod2_ref, strips2_ref, prey2_ref, tend_ref, ends, grazed,
):
    x_even, y_even = is_even("gx"), is_even("gy")
    y_sides = reader(y_even, yev_ref, yod_ref)
    strip_coefficients(g, ends, y_sides, extra_ref)
    all_strip_tendencies(g, ends, strips_ref, y_sides, tend_ref)
    packed = [next_ref[rows8(n), :] + tend_ref[rows8(n), :] for n in range(g.T * g.NV)]
    for n, one_packed in enumerate(packed):
        strips2_ref[rows8(n), :] = one_packed
    put_messages(packed, y_even, yev2_ref, yod2_ref)
    for i in range(g.NV):
        grazed[rows8(i), :] = sum(
            taste_of(taste_ref, t) * tend_ref[rows8(t * g.NV + i), :] for t in range(g.T)
        )
    for k in range(g.K):
        prey2_ref[rows8(k), :] = prey_ref[rows8(k), :] + end_columns(g, grazed, 0, k)

    def one(t):
        for i in range(2 * g.LH):
            j = i + (g.R - 2) * g.LH
            low, high = (
                field_ref[rows8(t * g.K + k), :] + end_columns(g, tend_ref, t, k) for k in (i, j)
            )
            at = rows8(t * 2 * g.LH + i)
            xev2_ref[at, :] = jnp.where(x_even, high, low)
            xod2_ref[at, :] = jnp.where(x_even, low, high)

    each_tracer(g, 4, one)


def border_two_kernel(
    g, total, ahead,
    field_ref, part_ref, xev_ref, xod_ref, inner, outer, grazers_ref, taste_ref, *rest,
):
    prey_refs, (out_ref, factor) = rest[:-2], rest[-2:]
    x_sides = reader(is_even("gx"), xev_ref, xod_ref)
    set_factor(g, total, factor, grazers_ref, prey_refs)

    def one(t):
        base = pl.multiple_of(t * g.tile, g.tile)

        def emit(r, lh, new):
            out_ref[pl.ds(base + (r * g.LH + lh) * SUB, SUB), :] = new

        taste = taste_of(taste_ref, t)
        finish(g, inner, outer, t, field_ref, part_ref, x_sides, taste, factor, emit)

    each_tracer(g, ahead, one)


def result_kernel(
    g, ahead, field_ref, strips_ref, yev_ref, yod_ref, ends, out_ref, tend_ref, leaving, sems
):
    y_sides = reader(is_even("gy"), yev_ref, yod_ref)
    all_strip_tendencies(g, ends, strips_ref, y_sides, tend_ref)

    def departure(t):
        at = pl.ds(pl.multiple_of(t * g.tile, g.tile), g.tile)
        return pltpu.make_async_copy(leaving.at[at, :], out_ref.at[at, :], sems.at[t])

    def one(t):
        base = pl.multiple_of(t * g.tile, g.tile)
        for r in range(g.R):
            for lh in range(g.LH):
                k = r * g.LH + lh
                new = field_ref[rows8(t * g.K + k), :] + end_columns(g, tend_ref, t, k)
                leaving[pl.ds(base + lh * SUB * g.R + r, SUB, stride=g.R), :] = new
        departure(t).start()

    each_tracer(g, ahead, one)
    for t in range(g.T):
        departure(t).wait()


def call(body, outs, operands, far=0, far_out=False, scratch=()):
    spaces = [pltpu.HBM if i < far else pltpu.VMEM for i in range(len(operands))]
    operands = [
        pltpu.with_memory_space_constraint(a, space) if space == pltpu.HBM else a
        for a, space in zip(operands, spaces)
    ]
    return pl.pallas_call(
        body,
        out_shape=[jax.ShapeDtypeStruct((rows, 128), jnp.float32) for rows in outs],
        in_specs=[pl.BlockSpec(memory_space=space) for space in spaces],
        out_specs=[pl.BlockSpec(memory_space=pltpu.HBM if far_out else pltpu.VMEM)] * len(outs),
        scratch_shapes=[
            pltpu.VMEM((rows, 128), jnp.float32) if isinstance(rows, int) else rows
            for rows in scratch
        ],
        compiler_params=pltpu.CompilerParams(vmem_limit_bytes=LIM),
    )(*operands)


def pair_swap(values, axis, start):
    pairs = []
    for i in range(start, lax.axis_size(axis) - 1, 2):
        pairs += [(i, i + 1), (i + 1, i)]
    if not pairs:
        return jnp.zeros_like(values)
    return lax.ppermute(values, axis, pairs)


def tracer_swap(values):
    return lax.ppermute(values, "tracer", [(0, 1), (1, 0)])


def all_prey(values):
    if lax.axis_size("tracer") == 2:
        return [values, tracer_swap(values)]
    return [lax.psum(values, "tracer")]


def neighbours(x_ev, x_od, y_ev, y_od):
    x_od = pair_swap(x_od, "gx", 1)
    y_ev = pair_swap(y_ev, "gy", 0)
    y_od = pair_swap(y_od, "gy", 1)
    x_ev = pair_swap(x_ev, "gx", 0)
    return x_ev, x_od, y_ev, y_od


def on_device(tracers, fluxes, diff_east, diff_north, column_depth, grazers, groups, preference):
    tr_dev, levels, rows, cols = tracers.shape
    parts = lax.axis_size("tracer")
    if not (cols == 128 and rows * levels == cols and levels == 2 * SUB and rows % SUB == 0):
        return plain(
            tracers, fluxes, diff_east, diff_north, column_depth, grazers, groups, preference
        )
    g = Geo(tr_dev, levels, rows, cols)
    total = float(tr_dev * parts)
    flat = tracers.reshape(-1, cols)
    grazers = grazers.reshape(-1, cols)
    cells = g.T * g.tile
    copies = pltpu.SemaphoreType.DMA((g.T,))

    if parts == 2:
        mine = fluxes.reshape(-1, cols)
        other = tracer_swap(mine)
    else:
        gathered = lax.all_gather(fluxes, "tracer", axis=1, tiled=True)
        mine, other = (gathered[:, i : i + SUB].reshape(-1, cols) for i in (0, SUB))
    field, strips, prey, taste = call(
        functools.partial(load_kernel, g),
        [cells, g.T * g.SR, g.T * 2 * g.L + g.L + 3 * SUB, g.T * SUB],
        [flat, groups, preference],
        far=3,
        scratch=[cells, copies, pltpu.SMEM(groups.shape, groups.dtype),
                 pltpu.SMEM(preference.shape, preference.dtype), pltpu.SemaphoreType.DMA((2,))],
    )
    prey = all_prey(prey)
    x_rows = g.T * 2 * g.L
    x_more = x_rows + g.L + 2 * SUB
    *messages, extra = call(
        functools.partial(first_messages_kernel, g),
        [x_more, x_more, g.my1 * SUB, g.my1 * SUB, 3 * g.SR],
        [field, strips, mine, other, column_depth, diff_east, diff_north],
    )
    messages = neighbours(*messages)
    messages = messages[0], messages[1], messages[3], messages[2]
    part, inner = call(
        functools.partial(inside_kernel, g, INSIDE, True),
        [cells, g.inner.rows],
        [field, mine, other, column_depth, diff_east, diff_north],
    )
    field, next_strips, next_prey, outer = call(
        functools.partial(border_kernel, g, total, FINISH),
        [cells, g.T * g.SR, g.tile, g.outer.rows],
        [field, part, *messages[:2], inner, mine, other, column_depth, diff_east, grazers, taste,
         *prey],
        scratch=[g.tile],
    )
    *messages, strips, prey, tend, ends = call(
        functools.partial(second_messages_kernel, g),
        [x_rows, x_rows, g.my2 * SUB, g.my2 * SUB, g.T * g.SR, g.tile, g.T * g.SR, g.ends.rows],
        [field, strips, next_strips, next_prey, extra, *messages[2:], taste],
        scratch=[g.SR],
    )
    prey = all_prey(prey)
    messages = neighbours(*messages)
    field, part = call(
        functools.partial(inside_kernel, g, INSIDE, False), [cells, cells], [field, tend, inner]
    )
    (field,) = call(
        functools.partial(border_two_kernel, g, total, FINISH),
        [cells],
        [field, part, *messages[:2], inner, outer, grazers, taste, *prey],
        scratch=[g.tile],
    )
    (out,) = call(
        functools.partial(result_kernel, g, FINISH),
        [cells],
        [field, strips, *messages[2:], ends],
        far_out=True,
        scratch=[g.T * g.SR, cells, copies],
    )
    return out.reshape(tracers.shape)


def solution(mesh):
    placed = (
        P("tracer", None, "gx", "gy"),
        P(None, "tracer", "gx", "gy"),
        P("gx", "gy"),
        P("gx", "gy"),
        P("gx", "gy"),
        P(None, "gx", "gy"),
        P("tracer"),
        P(),
    )
    return jax.shard_map(
        on_device,
        mesh=mesh,
        in_specs=placed,
        out_specs=P("tracer", None, "gx", "gy"),
        check_vma=False,
    )
```

```python
import functools

import jax
import jax.numpy as jnp
from jax import lax
from jax.experimental import pallas as pl
from jax.experimental.pallas import tpu as pltpu
from jax.sharding import PartitionSpec as P

STEPS = 2
LONG = pl.CostEstimate(flops=2_000_000_000, bytes_accessed=400_000_000, transcendentals=0)
SUB = 8
LIM = 48 * 1024 * 1024
INSIDE, FINISH, LAST = 3, 3, 3


def with_halo(cells, sides, width):
    for axis, dim in sides:
        count = lax.axis_size(axis)
        ends = count - 1
        head = lax.slice_in_dim(cells, 0, width, axis=dim)
        tail = lax.slice_in_dim(cells, cells.shape[dim] - width, cells.shape[dim], axis=dim)
        cells = jnp.concatenate(
            [
                lax.ppermute(tail, axis, [(i, (i + 1) % count) for i in range(ends)]),
                cells,
                lax.ppermute(head, axis, [((i + 1) % count, i) for i in range(ends)]),
            ],
            axis=dim,
        )
    return cells


def minmod(jump_low, jump_high):
    return jnp.maximum(0.0, jnp.minimum(jump_low, jump_high)) + jnp.minimum(
        0.0, jnp.maximum(jump_low, jump_high)
    )


def window(values, low_end, high_end, direction):
    return lax.slice_in_dim(values, low_end, high_end, axis=direction % values.ndim)


def face_terms(tracer_field, open_faces, face_flux, face_kappa, direction):
    length = tracer_field.shape[direction % tracer_field.ndim] - 4
    jump_face = open_faces * (
        window(tracer_field, 1, length + 4, direction)
        - window(tracer_field, 0, length + 3, direction)
    )
    slopes = minmod(
        window(jump_face, 0, length + 2, direction), window(jump_face, 1, length + 3, direction)
    )
    left_value = window(tracer_field, 1, length + 2, direction) + 0.5 * window(
        slopes, 0, length + 1, direction
    )
    right_value = window(tracer_field, 2, length + 3, direction) - 0.5 * window(
        slopes, 1, length + 2, direction
    )
    carried = face_flux * jnp.where(face_flux > 0.0, left_value, right_value)
    if face_kappa is not None:
        carried = carried - face_kappa * window(jump_face, 1, length + 2, direction)
    return window(carried, 0, length, direction) - window(carried, 1, length + 1, direction)


def plain(tracers, fluxes, diff_east, diff_north, column_depth, grazers, groups, preference):
    tr_dev, levels, rows_dev, cols_dev = tracers.shape
    total_tracers = tr_dev * lax.axis_size("tracer")
    level_index = lax.broadcasted_iota(jnp.int32, (levels, rows_dev, cols_dev), 0)
    wet_cells = (level_index < column_depth[None]).astype(jnp.float32)
    all_fluxes = lax.all_gather(fluxes, "tracer", axis=1, tiled=True)
    stacked = jnp.concatenate(
        [all_fluxes[0], all_fluxes[1], wet_cells, diff_east[None], diff_north[None]], 0
    )
    rimmed = with_halo(stacked, (("gx", 1), ("gy", 2)), 2)
    east_ext = rimmed[:levels]
    north_ext = rimmed[levels : 2 * levels]
    downward = all_fluxes[2]
    wet_ext = rimmed[-(levels + 2) : -2]
    kx_ext = rimmed[-2]
    ky_ext = rimmed[-1]
    open_x = wet_ext[:, :-1, 2:-2] * wet_ext[:, 1:, 2:-2]
    open_y = wet_ext[:, 2:-2, :-1] * wet_ext[:, 2:-2, 1:]
    flux_x = east_ext[:, 1 : rows_dev + 2, 2:-2] * open_x[:, 1 : rows_dev + 2]
    kappa_x = kx_ext[None, 1 : rows_dev + 2, 2:-2] * open_x[:, 1 : rows_dev + 2]
    flux_y = north_ext[:, 2:-2, 1 : cols_dev + 2] * open_y[:, :, 1 : cols_dev + 2]
    kappa_y = ky_ext[None, 2:-2, 1 : cols_dev + 2] * open_y[:, :, 1 : cols_dev + 2]
    wet_z = jnp.pad(wet_cells, ((2, 2), (0, 0), (0, 0)))
    open_z = wet_z[:-1] * wet_z[1:]
    flux_z = jnp.pad(downward, ((1, 0), (0, 0), (0, 0))) * open_z[1 : levels + 2]
    group_match = (
        groups[:, None] == lax.broadcasted_iota(jnp.int32, (1, preference.shape[0]), 1)
    ).astype(jnp.float32)
    grazing_pref = jnp.sum(group_match * preference[None, :], axis=1)
    tracer_field = tracers
    for step_index in range(STEPS):
        prey_local = jnp.sum(grazing_pref[:, None, None, None] * tracer_field, axis=0)
        prey_total = lax.psum(prey_local, "tracer")
        factor = grazers / (1.0 + 4.0 * prey_total / total_tracers)
        extended = with_halo(tracer_field, (("gx", 2), ("gy", 3)), 2)
        tendency = face_terms(extended[:, :, :, 2:-2], open_x, flux_x, kappa_x, -2)
        tendency = tendency + face_terms(extended[:, :, 2:-2, :], open_y, flux_y, kappa_y, -1)
        padded_z = jnp.pad(tracer_field, ((0, 0), (2, 2), (0, 0), (0, 0)))
        tendency = tendency + face_terms(padded_z, open_z, flux_z, None, -3)
        tracer_field = (
            tracer_field + tendency - grazing_pref[:, None, None, None] * factor * tracer_field
        )
    return tracer_field


WIDE = 16
EACH = 128 // WIDE
SLOTS = WIDE // 4


class Geo:
    def __init__(self, tr_dev, levels, rows, cols):
        self.T, self.L, self.R, self.C = tr_dev, levels, rows, cols
        self.LH = levels // SUB
        self.tile = rows * levels
        self.K = rows * self.LH
        self.NV = self.K // EACH
        self.SR = self.NV * SUB
        self.my1 = -(-(tr_dev + 3) * self.NV // SLOTS)
        self.my2 = -(-tr_dev * self.NV // SLOTS)
        self.inner = Table(
            hx=(rows + 1) * self.LH, px=(rows + 1) * self.LH, mx=(rows + 1) * self.LH,
            kx=rows + 1, hy=self.K, py=self.K, my=self.K, ky=rows,
            hz=self.K, pz=self.K, mz=self.K,
        )
        self.outer = Table(
            hx=4 * self.LH, px=2 * self.LH, mx=2 * self.LH, kx=1
        )
        self.ends = Table(
            hs=4 * self.NV, ps=2 * self.NV, ms=2 * self.NV, ks=2 * self.NV
        )


class Table:
    def __init__(self, **counts):
        self.at, self.rows = {}, 0
        for name, count in counts.items():
            self.at[name] = self.rows
            self.rows += count * SUB

    def get(self, ref, name, index):
        at = self.at[name] + index * SUB
        return ref[at : at + SUB, :]

    def set(self, ref, name, index, value):
        at = self.at[name] + index * SUB
        ref[at : at + SUB, :] = value

    def set_flux(self, ref, axis, index, opened, flux):
        flux = jnp.where(opened, flux, 0.0)
        self.set(ref, "p" + axis, index, jnp.maximum(flux, 0.0))
        self.set(ref, "m" + axis, index, jnp.minimum(flux, 0.0))

    def set_open(self, ref, axis, index, opened):
        self.set(ref, "h" + axis, index, jnp.where(opened, 0.5, 0.0))


def lanes():
    return lax.broadcasted_iota(jnp.int32, (SUB, 128), 1)


def sublanes():
    return lax.broadcasted_iota(jnp.int32, (SUB, 128), 0)


def roll(v, by, axis):
    by = by % v.shape[axis]
    return v if by == 0 else pltpu.roll(v, by, axis)


def registers(ref):
    return [ref[i : i + SUB, :] for i in range(0, ref.shape[0], SUB)]


def rows8(index):
    return pl.ds(pl.multiple_of(index * SUB, SUB), SUB)


def pack_strips(parts):
    lane = lanes()
    out = []
    for v in range(0, len(parts), EACH):
        packed = jnp.zeros((SUB, 128), jnp.float32)
        for k, part in enumerate(parts[v : v + EACH]):
            inside = (lane >= WIDE * k + 6) & (lane < WIDE * k + 14)
            packed = jnp.where(inside, roll(part, WIDE * k + 10, 1), packed)
        out.append(packed)
    return out


def put_messages(packed, out_ref):
    slot = (lanes() % WIDE) // 4
    for v in range(0, len(packed), SLOTS):
        out = jnp.zeros((SUB, 128), jnp.float32)
        for m, one in enumerate(packed[v : v + SLOTS]):
            out = jnp.where(slot == m, roll(one, 4 * m - 8, 1), out)
        out_ref[rows8(v // SLOTS), :] = out


def full_strips(own, from_lower, from_upper, m):
    place = lanes() % WIDE
    out = jnp.where(place < 2, roll(from_lower, -4 * m, 1), roll(own, -8, 1))
    out = jnp.where(place < 6, out, own)
    out = jnp.where(place < 10, out, roll(from_upper, 8 - 4 * m, 1))
    return jnp.where(place < 12, out, 0.0)


def spread(rows, r):
    return jnp.broadcast_to(rows[r : r + 1, :], (SUB, 128))


def spread_rows(g, rows):
    return [spread(rows, r) for r in range(g.R) for _ in range(g.LH)]


def taste_of(taste_ref, t):
    return taste_ref[rows8(t), :]


def is_even(axis):
    return lax.rem(lax.axis_index(axis), 2) == 0


def split_sides(even, ev, od):
    return jnp.where(even, od, ev), jnp.where(even, ev, od)


def limited(a, b):
    least, most = jnp.minimum(a, b), jnp.maximum(a, b)
    return jnp.maximum(least, jnp.minimum(most, 0.0))


def each_tracer(g, ahead, body):
    def some(i, carry):
        for more in range(ahead):
            body(i * ahead + more)
        return carry

    lax.fori_loop(0, g.T // ahead, some, 0)
    for t in range(g.T - g.T % ahead, g.T):
        body(t)


def flux_reader(g, mine_ref, other_ref):
    first = lax.axis_index("tracer") == 0
    single = lax.axis_size("tracer") != 2

    def flux(dim, r, lh):
        at = pl.ds(dim * g.R * SUB + r, SUB, stride=g.R)
        a, b = mine_ref[at, :], other_ref[at, :]
        if single:
            return (a, b)[lh]
        return jnp.where(first, (a, b)[lh], (b, a)[lh])

    return flux


def load_kernel(
    g, tracers_ref, groups_far, pref_far, field_ref, strips_ref, prey_ref, taste_ref,
    landed, sems, groups_ref, pref_ref, small_sems,
):
    def arrival(t):
        at = pl.ds(pl.multiple_of(t * g.tile, g.tile), g.tile)
        return pltpu.make_async_copy(tracers_ref.at[at, :], landed.at[at, :], sems.at[t])

    small = [
        pltpu.make_async_copy(a, b, small_sems.at[i])
        for i, (a, b) in enumerate(((groups_far, groups_ref), (pref_far, pref_ref)))
    ]
    for copy in small:
        copy.start()
    for t in range(g.T):
        arrival(t).start()
    prey_ref[...] = jnp.zeros_like(prey_ref)

    for copy in small:
        copy.wait()
    for t in range(g.T):
        taste_ref[rows8(t), :] = jnp.full((SUB, 128), pref_ref[groups_ref[t]], jnp.float32)

    def one(t):
        arrival(t).wait()
        taste = taste_of(taste_ref, t)
        base = pl.multiple_of(t * g.tile, g.tile)
        parts = []
        for r in range(g.R):
            for lh in range(g.LH):
                at = (r * g.LH + lh) * SUB
                v = landed[pl.ds(base + lh * SUB * g.R + r, SUB, stride=g.R), :]
                field_ref[pl.ds(base + at, SUB), :] = v
                parts.append(v)
                prey_ref[at : at + SUB, :] += taste * v
        for i, packed in enumerate(pack_strips(parts)):
            strips_ref[rows8(t * g.NV + i), :] = packed

    each_tracer(g, 2, one)


def first_messages_kernel(
    g, field_ref, strips_ref, mine_ref, other_ref, depth_ref, east_ref, north_ref,
    xev_ref, xod_ref, y_ref, extra_ref,
):
    x_even = is_even("gx")
    flux = flux_reader(g, mine_ref, other_ref)
    zero = jnp.zeros((SUB, 128), jnp.float32)

    def put(at, low, high):
        xev_ref[at, :] = jnp.where(x_even, high, low)
        xod_ref[at, :] = jnp.where(x_even, low, high)

    def one(t):
        base = pl.multiple_of(t * g.tile, g.tile)
        for i in range(2 * g.LH):
            low = field_ref[pl.ds(base + i * SUB, SUB), :]
            high = field_ref[pl.ds(base + g.tile - 2 * g.L + i * SUB, SUB), :]
            put(rows8(t * 2 * g.LH + i), low, high)

    each_tracer(g, 2, one)
    at = g.T * 2 * g.LH
    for lh in range(g.LH):
        put(rows8(at + lh), zero, flux(0, g.R - 1, lh))
    depth = depth_ref[...].astype(jnp.float32)
    put(rows8(at + g.LH), depth, roll(depth, 2, 0))
    put(rows8(at + g.LH + 1), zero, roll(east_ref[...], 1, 0))
    extras = pack_strips(spread_rows(g, depth))
    extras += pack_strips([flux(1, r, lh) for r in range(g.R) for lh in range(g.LH)])
    extras += pack_strips(spread_rows(g, north_ref[...]))
    for i, packed in enumerate(extras):
        extra_ref[rows8(i), :] = packed
    put_messages(registers(strips_ref) + extras, y_ref)


def wet_levels(g, depths):
    level = [(sublanes() + SUB * lh).astype(jnp.float32) for lh in range(g.LH)]
    return [[level[lh] < d for lh in range(g.LH)] for d in depths]


def inner_coefficients(g, cf, flux, depth, east, north):
    tab, sub = g.inner, sublanes()
    depths = [spread(depth, r) for r in range(g.R)]
    wet = wet_levels(g, depths)
    wet_before = wet_levels(g, [roll(d, 1, 1) for d in depths])
    for r in range(g.R):
        tab.set(cf, "kx", r + 1, 2.0 * spread(east, r))
        tab.set(cf, "ky", r, 2.0 * roll(spread(north, r), 1, 1))
        flux_z = [roll(flux(2, r, lh), 1, 0) for lh in range(g.LH)]
        for lh in range(g.LH):
            k, here = r * g.LH + lh, wet[r][lh]
            if r:
                opened = here & wet[r - 1][lh]
                tab.set_open(cf, "x", k, opened)
                tab.set_flux(cf, "x", k, opened, flux(0, r - 1, lh))
            opened = here & wet_before[r][lh]
            tab.set_open(cf, "y", k, opened)
            tab.set_flux(cf, "y", k, opened, roll(flux(1, r, lh), 1, 1))
            opened = here if lh else here & (sub > 0)
            above = jnp.where(sub == 0, flux_z[lh - 1], flux_z[lh]) if lh else flux_z[lh]
            tab.set_open(cf, "z", k, opened)
            tab.set_flux(cf, "z", k, opened, above)


def outer_coefficients(g, cf, extra_x, flux, depth, east):
    tab = g.outer
    depth_low, depth_high = extra_x(g.LH)
    depths = [spread(depth_low, 0), spread(depth_low, 1), spread(depth, 0), spread(depth, g.R - 1)]
    depths += [spread(depth_high, 0), spread(depth_high, 1)]
    wet = wet_levels(g, depths)
    tab.set(cf, "kx", 0, 2.0 * spread(extra_x(g.LH + 1)[0], 0))
    for lh in range(g.LH):
        for face, row in enumerate((0, 1, 3, 4)):
            tab.set_open(cf, "x", face * g.LH + lh, wet[row][lh] & wet[row + 1][lh])
        tab.set_flux(cf, "x", lh, wet[1][lh] & wet[2][lh], extra_x(lh)[0])
        tab.set_flux(cf, "x", g.LH + lh, wet[3][lh] & wet[4][lh], flux(0, g.R - 1, lh))


def strip_coefficients(g, cf, extra_y, extra_ref):
    tab, lane = g.ends, lanes()
    half = (lane // WIDE) % g.LH
    level = (sublanes() + SUB * half).astype(jnp.float32)
    for i in range(g.NV):
        full = []
        for which in range(3):
            own = which * g.NV + i
            slot = g.T * g.NV + own
            full.append(full_strips(extra_ref[rows8(own), :], *extra_y(slot // SLOTS), slot % SLOTS))
        wet = [level < roll(full[0], -away, 1) for away in (-2, -1, 0, 1, 2)]
        opened = [a & b for a, b in zip(wet, wet[1:])]
        for face in range(4):
            tab.set_open(cf, "s", face * g.NV + i, opened[face])
        for face in range(2):
            flux, kappa = (roll(v, 1 - face, 1) for v in full[1:])
            tab.set_flux(cf, "s", face * g.NV + i, opened[1 + face], flux)
            tab.set(cf, "ks", face * g.NV + i, 2.0 * kappa)


def end_lanes():
    lane = lanes()
    return (lane < 2) | (lane >= 126)


def inside_kernel(g, ahead, first, field_ref, *refs):
    if first:
        mine_ref, other_ref, depth_ref, east_ref, north_ref, part_ref, cf = refs
        inner_coefficients(
            g, cf, flux_reader(g, mine_ref, other_ref), depth_ref[...].astype(jnp.float32),
            east_ref[...], north_ref[...],
        )
    else:
        tend_ref, cf, whole_ref, part_ref = refs
    sub = sublanes()
    ends, top, bottom = end_lanes(), sub == 0, sub == SUB - 1

    def coef(name, index):
        return g.inner.get(cf, name, index)

    def shift_down(v):
        rolled = [roll(x, 1, 0) for x in v]
        return rolled[:1] + [
            jnp.where(top, rolled[i - 1], rolled[i]) for i in range(1, g.LH)
        ]

    def shift_up(v):
        rolled = [roll(x, -1, 0) for x in v]
        return [jnp.where(bottom, rolled[(i + 1) % g.LH], rolled[i]) for i in range(g.LH)]

    def one(t):
        base = pl.multiple_of(t * g.tile, g.tile)
        for r in range(g.R):
            index = [r * g.LH + lh for lh in range(g.LH)]
            at = [pl.ds(base + k * SUB, SUB) for k in index]
            cells = [field_ref[a, :] for a in at]
            if not first:
                cells = [c + end_columns(g, tend_ref, t, k) for k, c in zip(index, cells)]
                for a, c in zip(at, cells):
                    whole_ref[a, :] = c
            news = []
            for k, c in zip(index, cells):
                j = coef("hy", k) * (c - roll(c, 1, 1))
                s = limited(j, roll(j, -1, 1))
                flow = coef("py", k) * roll(c + s, 1, 1) + coef("my", k) * (c - s)
                flow = flow - coef("ky", r) * j
                news.append(c + jnp.where(ends, 0.0, flow - roll(flow, -1, 1)))
            j = [coef("hz", k) * (c - a) for k, c, a in zip(index, cells, shift_down(cells))]
            s = [limited(a, b) for a, b in zip(j, shift_up(j))]
            above = shift_down([c + v for c, v in zip(cells, s)])
            flow = [
                coef("pz", k) * a + coef("mz", k) * (c - v)
                for k, a, c, v in zip(index, above, cells, s)
            ]
            for a, new, high, low in zip(at, news, flow, shift_up(flow)):
                part_ref[a, :] = new + (high - low)

    each_tracer(g, ahead, one)


def strip_tendency(g, cf, full, i):
    def coef(name, face):
        return g.ends.get(cf, name, face * g.NV + i)

    cell = [roll(full, -away, 1) for away in (-2, -1, 0, 1, 2)]
    j = [coef("hs", face) * (cell[face + 1] - cell[face]) for face in range(4)]
    s = [limited(a, b) for a, b in zip(j, j[1:])]
    flow = [
        coef("ps", f) * (cell[f + 1] + s[f])
        + coef("ms", f) * (cell[f + 2] - s[f + 1])
        - coef("ks", f) * j[f + 1]
        for f in range(2)
    ]
    tend = flow[0] - flow[1]
    place = lanes() % WIDE
    tend = jnp.where(place < 10, tend, roll(tend, 8, 1))
    return jnp.where((place >= 8) & (place < 12), tend, 0.0)


def all_strip_tendencies(g, cf, strips_ref, sides, tend_ref):
    for n in range(g.T * g.NV):
        full = full_strips(strips_ref[rows8(n), :], *sides(n // SLOTS), n % SLOTS)
        tend_ref[rows8(n), :] = strip_tendency(g, cf, full, n % g.NV)


def end_columns(g, tend_ref, t, k):
    v, n = divmod(k, EACH)
    return jnp.where(end_lanes(), roll(tend_ref[rows8(t * g.NV + v), :], -(WIDE * n + 10), 1), 0.0)


def set_factor(g, total, factor, grazers_ref, prey_refs):
    for r in range(g.R):
        for lh in range(g.LH):
            at = rows8(r * g.LH + lh)
            prey = sum(ref[at, :] for ref in prey_refs)
            grazers = grazers_ref[pl.ds(lh * SUB * g.R + r, SUB, stride=g.R), :]
            factor[at, :] = grazers / (1.0 + 4.0 * prey / total)


def finish(g, inner, outer, t, field_ref, part_ref, sides, emit):
    base = pl.multiple_of(t * g.tile, g.tile)

    def cell(r, lh):
        if 0 <= r < g.R:
            return field_ref[pl.ds(base + (r * g.LH + lh) * SUB, SUB), :]
        i = r + 2 if r < 0 else r - g.R
        return sides(t * 2 * g.LH + i * g.LH + lh)[0 if r < 0 else 1]

    def coef(name, f, lh):
        if 0 < f < g.R:
            return g.inner.get(inner, name, f * g.LH + lh)
        if name == "hx":
            return g.outer.get(outer, name, {-1: 0, 0: 1, g.R: 2, g.R + 1: 3}[f] * g.LH + lh)
        return g.outer.get(outer, name, (g.LH if f else 0) + lh)

    state = [None] * g.LH
    for f in range(-1, g.R + 2):
        for lh in range(g.LH):
            if f < 0:
                below = cell(-2, lh)
                here = cell(-1, lh)
                state[lh] = (here, coef("hx", f, lh) * (here - below), None, None)
                continue
            c, j, left, carried = state[lh]
            up = cell(f, lh)
            j_up = coef("hx", f, lh) * (up - c)
            s = limited(j, j_up)
            if f > 0:
                kap = g.inner.get(inner, "kx", f - 1) if f > 1 else g.outer.get(outer, "kx", 0)
                flow = coef("px", f - 1, lh) * left + coef("mx", f - 1, lh) * (c - s) - kap * j
                if f > 1:
                    r = f - 2
                    k = r * g.LH + lh
                    old = cell(r, lh)
                    new = part_ref[pl.ds(base + k * SUB, SUB), :] + (carried - flow)
                    emit(r, lh, old, new)
                carried = flow
            state[lh] = (up, j_up, c + s, carried)


def reader(even, ev_ref, od_ref):
    def sides(i):
        at = rows8(i)
        return split_sides(even, ev_ref[at, :], od_ref[at, :])

    return sides


def border_kernel(
    g, total, ahead,
    field_ref, part_ref, xev_ref, xod_ref, inner, mine_ref, other_ref, depth_ref, east_ref,
    grazers_ref, taste_ref, *rest,
):
    prey_refs, (out_ref, strips_ref, prey_ref, outer, factor) = rest[:-5], rest[-5:]
    x_sides = reader(is_even("gx"), xev_ref, xod_ref)
    outer_coefficients(
        g, outer, lambda i: x_sides(g.T * 2 * g.LH + i), flux_reader(g, mine_ref, other_ref),
        depth_ref[...].astype(jnp.float32), east_ref[...],
    )
    set_factor(g, total, factor, grazers_ref, prey_refs)
    prey_ref[...] = jnp.zeros_like(prey_ref)

    def one(t):
        taste = taste_of(taste_ref, t)
        base = pl.multiple_of(t * g.tile, g.tile)
        news = {}

        def emit(r, lh, old, new):
            at = (r * g.LH + lh) * SUB
            new = new - (taste * factor[at : at + SUB, :]) * old
            out_ref[pl.ds(base + at, SUB), :] = new
            prey_ref[at : at + SUB, :] += taste * new
            news[r, lh] = new

        finish(g, inner, outer, t, field_ref, part_ref, x_sides, emit)
        parts = [news[r, lh] for r in range(g.R) for lh in range(g.LH)]
        for i, packed in enumerate(pack_strips(parts)):
            strips_ref[rows8(t * g.NV + i), :] = packed

    each_tracer(g, ahead, one)


def second_messages_kernel(
    g, field_ref, strips_ref, next_ref, prey_ref, extra_ref, yod_ref, yev_ref, taste_ref,
    xev2_ref, xod2_ref, y2_ref, strips2_ref, prey2_ref, tend_ref, ends, grazed,
):
    x_even = is_even("gx")
    y_sides = reader(is_even("gy"), yev_ref, yod_ref)
    strip_coefficients(g, ends, y_sides, extra_ref)
    all_strip_tendencies(g, ends, strips_ref, y_sides, tend_ref)
    packed = [next_ref[rows8(n), :] + tend_ref[rows8(n), :] for n in range(g.T * g.NV)]
    for n, one_packed in enumerate(packed):
        strips2_ref[rows8(n), :] = one_packed
    put_messages(packed, y2_ref)
    for i in range(g.NV):
        grazed[rows8(i), :] = sum(
            taste_of(taste_ref, t) * tend_ref[rows8(t * g.NV + i), :] for t in range(g.T)
        )
    for k in range(g.K):
        prey2_ref[rows8(k), :] = prey_ref[rows8(k), :] + end_columns(g, grazed, 0, k)

    def one(t):
        for i in range(2 * g.LH):
            j = i + (g.R - 2) * g.LH
            low, high = (
                field_ref[rows8(t * g.K + k), :] + end_columns(g, tend_ref, t, k) for k in (i, j)
            )
            at = rows8(t * 2 * g.LH + i)
            xev2_ref[at, :] = jnp.where(x_even, high, low)
            xod2_ref[at, :] = jnp.where(x_even, low, high)

    each_tracer(g, 6, one)


def border_two_kernel(g, ahead, field_ref, part_ref, xev_ref, xod_ref, inner, outer, out_ref):
    x_sides = reader(is_even("gx"), xev_ref, xod_ref)

    def one(t):
        base = pl.multiple_of(t * g.tile, g.tile)

        def emit(r, lh, old, new):
            out_ref[pl.ds(base + (r * g.LH + lh) * SUB, SUB), :] = new

        finish(g, inner, outer, t, field_ref, part_ref, x_sides, emit)

    each_tracer(g, ahead, one)


def result_kernel(
    g, total, ahead, field_ref, part_ref, strips_ref, yev_ref, yod_ref, ends, grazers_ref, taste_ref,
    *rest,
):
    prey_refs, (out_ref, factor, tend_ref, leaving, sems) = rest[:-5], rest[-5:]
    y_sides = reader(is_even("gy"), yev_ref, yod_ref)
    all_strip_tendencies(g, ends, strips_ref, y_sides, tend_ref)
    set_factor(g, total, factor, grazers_ref, prey_refs)

    def departure(t):
        at = pl.ds(pl.multiple_of(t * g.tile, g.tile), g.tile)
        return pltpu.make_async_copy(leaving.at[at, :], out_ref.at[at, :], sems.at[t])

    def one(t):
        base = pl.multiple_of(t * g.tile, g.tile)
        taste = taste_of(taste_ref, t)
        for r in range(g.R):
            for lh in range(g.LH):
                k = r * g.LH + lh
                at = rows8(t * g.K + k)
                new = part_ref[at, :] + end_columns(g, tend_ref, t, k)
                new = new - (taste * factor[rows8(k), :]) * field_ref[at, :]
                leaving[pl.ds(base + lh * SUB * g.R + r, SUB, stride=g.R), :] = new
        departure(t).start()

    each_tracer(g, ahead, one)
    for t in range(g.T):
        departure(t).wait()


def call(body, outs, operands, far=0, far_out=False, scratch=(), cost=None):
    spaces = [pltpu.HBM if i < far else pltpu.VMEM for i in range(len(operands))]
    operands = [
        pltpu.with_memory_space_constraint(a, space) if space == pltpu.HBM else a
        for a, space in zip(operands, spaces)
    ]
    return pl.pallas_call(
        body,
        out_shape=[jax.ShapeDtypeStruct((rows, 128), jnp.float32) for rows in outs],
        in_specs=[pl.BlockSpec(memory_space=space) for space in spaces],
        out_specs=[pl.BlockSpec(memory_space=pltpu.HBM if far_out else pltpu.VMEM)] * len(outs),
        scratch_shapes=[
            pltpu.VMEM((rows, 128), jnp.float32) if isinstance(rows, int) else rows
            for rows in scratch
        ],
        compiler_params=pltpu.CompilerParams(vmem_limit_bytes=LIM),
        cost_estimate=cost,
    )(*operands)


def pair_swap(values, axis, start):
    pairs = []
    for i in range(start, lax.axis_size(axis) - 1, 2):
        pairs += [(i, i + 1), (i + 1, i)]
    if not pairs:
        return jnp.zeros_like(values)
    return lax.ppermute(values, axis, pairs)


def tracer_swap(values):
    return lax.ppermute(values, "tracer", [(0, 1), (1, 0)])


def all_prey(values):
    if lax.axis_size("tracer") == 2:
        return [values, tracer_swap(values)]
    return [lax.psum(values, "tracer")]


def neighbours(x_ev, x_od, y):
    y_ev, y_od = pair_swap(y, "gy", 0), pair_swap(y, "gy", 1)
    return pair_swap(x_ev, "gx", 0), pair_swap(x_od, "gx", 1), y_ev, y_od


def on_device(tracers, fluxes, diff_east, diff_north, column_depth, grazers, groups, preference):
    tr_dev, levels, rows, cols = tracers.shape
    parts = lax.axis_size("tracer")
    if not (cols == 128 and rows * levels == cols and levels == 2 * SUB and rows % SUB == 0):
        return plain(
            tracers, fluxes, diff_east, diff_north, column_depth, grazers, groups, preference
        )
    g = Geo(tr_dev, levels, rows, cols)
    total = float(tr_dev * parts)
    flat = tracers.reshape(-1, cols)
    grazers = grazers.reshape(-1, cols)
    cells = g.T * g.tile
    copies = pltpu.SemaphoreType.DMA((g.T,))

    if parts == 2:
        mine = fluxes.reshape(-1, cols)
        other = tracer_swap(mine)
    else:
        gathered = lax.all_gather(fluxes, "tracer", axis=1, tiled=True)
        mine, other = (gathered[:, i : i + SUB].reshape(-1, cols) for i in (0, SUB))
    field, strips, prey, taste = call(
        functools.partial(load_kernel, g),
        [cells, g.T * g.SR, g.T * 2 * g.L + g.L + 3 * SUB, g.T * SUB],
        [flat, groups, preference],
        far=3,
        scratch=[cells, copies, pltpu.SMEM(groups.shape, groups.dtype),
                 pltpu.SMEM(preference.shape, preference.dtype), pltpu.SemaphoreType.DMA((2,))],
    )
    prey = all_prey(prey)
    x_rows = g.T * 2 * g.L
    x_more = x_rows + g.L + 2 * SUB
    *messages, extra = call(
        functools.partial(first_messages_kernel, g),
        [x_more, x_more, g.my1 * SUB, 3 * g.SR],
        [field, strips, mine, other, column_depth, diff_east, diff_north],
    )
    messages = neighbours(*messages)
    messages = messages[0], messages[1], messages[3], messages[2]
    part, inner = call(
        functools.partial(inside_kernel, g, INSIDE, True),
        [cells, g.inner.rows],
        [field, mine, other, column_depth, diff_east, diff_north],
    )
    field, next_strips, next_prey, outer = call(
        functools.partial(border_kernel, g, total, FINISH),
        [cells, g.T * g.SR, g.tile, g.outer.rows],
        [field, part, *messages[:2], inner, mine, other, column_depth, diff_east, grazers, taste,
         *prey],
        scratch=[g.tile],
    )
    *messages, strips, prey, tend, ends = call(
        functools.partial(second_messages_kernel, g),
        [x_rows, x_rows, g.my2 * SUB, g.T * g.SR, g.tile, g.T * g.SR, g.ends.rows],
        [field, strips, next_strips, next_prey, extra, *messages[2:], taste],
        scratch=[g.SR],
    )
    prey = all_prey(prey)
    messages = neighbours(*messages)
    field, part = call(
        functools.partial(inside_kernel, g, INSIDE, False), [cells, cells], [field, tend, inner],
        cost=LONG,
    )
    (part,) = call(
        functools.partial(border_two_kernel, g, FINISH),
        [cells],
        [field, part, *messages[:2], inner, outer],
        cost=LONG,
    )
    (out,) = call(
        functools.partial(result_kernel, g, total, LAST),
        [cells],
        [field, part, strips, *messages[2:], ends, grazers, taste, *prey],
        far_out=True,
        scratch=[g.tile, g.T * g.SR, cells, copies],
    )
    return out.reshape(tracers.shape)


def solution(mesh):
    placed = (
        P("tracer", None, "gx", "gy"),
        P(None, "tracer", "gx", "gy"),
        P("gx", "gy"),
        P("gx", "gy"),
        P("gx", "gy"),
        P(None, "gx", "gy"),
        P("tracer"),
        P(),
    )
    return jax.shard_map(
        on_device,
        mesh=mesh,
        in_specs=placed,
        out_specs=P("tracer", None, "gx", "gy"),
        check_vma=False,
    )
```

```python
import functools

import jax
import jax.numpy as jnp
from jax import lax
from jax.experimental import pallas as pl
from jax.experimental.pallas import tpu as pltpu
from jax.sharding import PartitionSpec as P

STEPS = 2
SUB = 8
LIM = 48 * 1024 * 1024
INSIDE, FINISH, BOTH, LAST = 3, 3, 3, 3


def with_halo(cells, sides, width):
    for axis, dim in sides:
        count = lax.axis_size(axis)
        ends = count - 1
        head = lax.slice_in_dim(cells, 0, width, axis=dim)
        tail = lax.slice_in_dim(cells, cells.shape[dim] - width, cells.shape[dim], axis=dim)
        cells = jnp.concatenate(
            [
                lax.ppermute(tail, axis, [(i, (i + 1) % count) for i in range(ends)]),
                cells,
                lax.ppermute(head, axis, [((i + 1) % count, i) for i in range(ends)]),
            ],
            axis=dim,
        )
    return cells


def minmod(jump_low, jump_high):
    return jnp.maximum(0.0, jnp.minimum(jump_low, jump_high)) + jnp.minimum(
        0.0, jnp.maximum(jump_low, jump_high)
    )


def window(values, low_end, high_end, direction):
    return lax.slice_in_dim(values, low_end, high_end, axis=direction % values.ndim)


def face_terms(tracer_field, open_faces, face_flux, face_kappa, direction):
    length = tracer_field.shape[direction % tracer_field.ndim] - 4
    jump_face = open_faces * (
        window(tracer_field, 1, length + 4, direction)
        - window(tracer_field, 0, length + 3, direction)
    )
    slopes = minmod(
        window(jump_face, 0, length + 2, direction), window(jump_face, 1, length + 3, direction)
    )
    left_value = window(tracer_field, 1, length + 2, direction) + 0.5 * window(
        slopes, 0, length + 1, direction
    )
    right_value = window(tracer_field, 2, length + 3, direction) - 0.5 * window(
        slopes, 1, length + 2, direction
    )
    carried = face_flux * jnp.where(face_flux > 0.0, left_value, right_value)
    if face_kappa is not None:
        carried = carried - face_kappa * window(jump_face, 1, length + 2, direction)
    return window(carried, 0, length, direction) - window(carried, 1, length + 1, direction)


def plain(tracers, fluxes, diff_east, diff_north, column_depth, grazers, groups, preference):
    tr_dev, levels, rows_dev, cols_dev = tracers.shape
    total_tracers = tr_dev * lax.axis_size("tracer")
    level_index = lax.broadcasted_iota(jnp.int32, (levels, rows_dev, cols_dev), 0)
    wet_cells = (level_index < column_depth[None]).astype(jnp.float32)
    all_fluxes = lax.all_gather(fluxes, "tracer", axis=1, tiled=True)
    stacked = jnp.concatenate(
        [all_fluxes[0], all_fluxes[1], wet_cells, diff_east[None], diff_north[None]], 0
    )
    rimmed = with_halo(stacked, (("gx", 1), ("gy", 2)), 2)
    east_ext = rimmed[:levels]
    north_ext = rimmed[levels : 2 * levels]
    downward = all_fluxes[2]
    wet_ext = rimmed[-(levels + 2) : -2]
    kx_ext = rimmed[-2]
    ky_ext = rimmed[-1]
    open_x = wet_ext[:, :-1, 2:-2] * wet_ext[:, 1:, 2:-2]
    open_y = wet_ext[:, 2:-2, :-1] * wet_ext[:, 2:-2, 1:]
    flux_x = east_ext[:, 1 : rows_dev + 2, 2:-2] * open_x[:, 1 : rows_dev + 2]
    kappa_x = kx_ext[None, 1 : rows_dev + 2, 2:-2] * open_x[:, 1 : rows_dev + 2]
    flux_y = north_ext[:, 2:-2, 1 : cols_dev + 2] * open_y[:, :, 1 : cols_dev + 2]
    kappa_y = ky_ext[None, 2:-2, 1 : cols_dev + 2] * open_y[:, :, 1 : cols_dev + 2]
    wet_z = jnp.pad(wet_cells, ((2, 2), (0, 0), (0, 0)))
    open_z = wet_z[:-1] * wet_z[1:]
    flux_z = jnp.pad(downward, ((1, 0), (0, 0), (0, 0))) * open_z[1 : levels + 2]
    group_match = (
        groups[:, None] == lax.broadcasted_iota(jnp.int32, (1, preference.shape[0]), 1)
    ).astype(jnp.float32)
    grazing_pref = jnp.sum(group_match * preference[None, :], axis=1)
    tracer_field = tracers
    for step_index in range(STEPS):
        prey_local = jnp.sum(grazing_pref[:, None, None, None] * tracer_field, axis=0)
        prey_total = lax.psum(prey_local, "tracer")
        factor = grazers / (1.0 + 4.0 * prey_total / total_tracers)
        extended = with_halo(tracer_field, (("gx", 2), ("gy", 3)), 2)
        tendency = face_terms(extended[:, :, :, 2:-2], open_x, flux_x, kappa_x, -2)
        tendency = tendency + face_terms(extended[:, :, 2:-2, :], open_y, flux_y, kappa_y, -1)
        padded_z = jnp.pad(tracer_field, ((0, 0), (2, 2), (0, 0), (0, 0)))
        tendency = tendency + face_terms(padded_z, open_z, flux_z, None, -3)
        tracer_field = (
            tracer_field + tendency - grazing_pref[:, None, None, None] * factor * tracer_field
        )
    return tracer_field


WIDE = 16
EACH = 128 // WIDE
SLOTS = WIDE // 4


class Geo:
    def __init__(self, tr_dev, levels, rows, cols):
        self.T, self.L, self.R, self.C = tr_dev, levels, rows, cols
        self.LH = levels // SUB
        self.tile = rows * levels
        self.K = rows * self.LH
        self.NV = self.K // EACH
        self.SR = self.NV * SUB
        self.my1 = -(-(tr_dev + 3) * self.NV // SLOTS)
        self.my2 = -(-tr_dev * self.NV // SLOTS)
        self.inner = Table(
            hx=(rows + 1) * self.LH, px=(rows + 1) * self.LH, mx=(rows + 1) * self.LH,
            kx=rows + 1, hy=self.K, py=self.K, my=self.K, ky=rows,
            hz=self.K, pz=self.K, mz=self.K,
        )
        self.outer = Table(
            hx=4 * self.LH, px=2 * self.LH, mx=2 * self.LH, kx=1
        )
        self.ends = Table(
            hs=4 * self.NV, ps=2 * self.NV, ms=2 * self.NV, ks=2 * self.NV
        )


class Table:
    def __init__(self, **counts):
        self.at, self.rows = {}, 0
        for name, count in counts.items():
            self.at[name] = self.rows
            self.rows += count * SUB

    def get(self, ref, name, index):
        at = self.at[name] + index * SUB
        return ref[at : at + SUB, :]

    def set(self, ref, name, index, value):
        at = self.at[name] + index * SUB
        ref[at : at + SUB, :] = value

    def set_flux(self, ref, axis, index, opened, flux):
        flux = jnp.where(opened, flux, 0.0)
        self.set(ref, "p" + axis, index, jnp.maximum(flux, 0.0))
        self.set(ref, "m" + axis, index, jnp.minimum(flux, 0.0))

    def set_open(self, ref, axis, index, opened):
        self.set(ref, "h" + axis, index, jnp.where(opened, 0.5, 0.0))


def lanes():
    return lax.broadcasted_iota(jnp.int32, (SUB, 128), 1)


def sublanes():
    return lax.broadcasted_iota(jnp.int32, (SUB, 128), 0)


def roll(v, by, axis):
    by = by % v.shape[axis]
    return v if by == 0 else pltpu.roll(v, by, axis)


def registers(ref):
    return [ref[i : i + SUB, :] for i in range(0, ref.shape[0], SUB)]


def rows8(index):
    return pl.ds(pl.multiple_of(index * SUB, SUB), SUB)


def pack_strips(parts):
    lane = lanes()
    out = []
    for v in range(0, len(parts), EACH):
        packed = jnp.zeros((SUB, 128), jnp.float32)
        for k, part in enumerate(parts[v : v + EACH]):
            inside = (lane >= WIDE * k + 6) & (lane < WIDE * k + 14)
            packed = jnp.where(inside, roll(part, WIDE * k + 10, 1), packed)
        out.append(packed)
    return out


def put_messages(packed, out_ref):
    slot = (lanes() % WIDE) // 4
    for v in range(0, len(packed), SLOTS):
        out = jnp.zeros((SUB, 128), jnp.float32)
        for m, one in enumerate(packed[v : v + SLOTS]):
            out = jnp.where(slot == m, roll(one, 4 * m - 8, 1), out)
        out_ref[rows8(v // SLOTS), :] = out


def full_strips(own, from_lower, from_upper, m):
    place = lanes() % WIDE
    out = jnp.where(place < 2, roll(from_lower, -4 * m, 1), roll(own, -8, 1))
    out = jnp.where(place < 6, out, own)
    out = jnp.where(place < 10, out, roll(from_upper, 8 - 4 * m, 1))
    return jnp.where(place < 12, out, 0.0)


def spread(rows, r):
    return jnp.broadcast_to(rows[r : r + 1, :], (SUB, 128))


def spread_rows(g, rows):
    return [spread(rows, r) for r in range(g.R) for _ in range(g.LH)]


def taste_of(taste_ref, t):
    return taste_ref[rows8(t), :]


def is_even(axis):
    return lax.rem(lax.axis_index(axis), 2) == 0


def split_sides(even, ev, od):
    return jnp.where(even, od, ev), jnp.where(even, ev, od)


def limited(a, b):
    least, most = jnp.minimum(a, b), jnp.maximum(a, b)
    return jnp.maximum(least, jnp.minimum(most, 0.0))


def each_tracer(g, ahead, body):
    def some(i, carry):
        for more in range(ahead):
            body(i * ahead + more)
        return carry

    lax.fori_loop(0, g.T // ahead, some, 0)
    for t in range(g.T - g.T % ahead, g.T):
        body(t)


def flux_reader(g, mine_ref, other_ref):
    first = lax.axis_index("tracer") == 0
    single = lax.axis_size("tracer") != 2

    def flux(dim, r, lh):
        at = pl.ds(dim * g.R * SUB + r, SUB, stride=g.R)
        a, b = mine_ref[at, :], other_ref[at, :]
        if single:
            return (a, b)[lh]
        return jnp.where(first, (a, b)[lh], (b, a)[lh])

    return flux


def load_kernel(
    g, tracers_ref, groups_far, pref_far, field_ref, strips_ref, prey_ref, taste_ref,
    landed, sems, groups_ref, pref_ref, small_sems,
):
    def arrival(t):
        at = pl.ds(pl.multiple_of(t * g.tile, g.tile), g.tile)
        return pltpu.make_async_copy(tracers_ref.at[at, :], landed.at[at, :], sems.at[t])

    small = [
        pltpu.make_async_copy(a, b, small_sems.at[i])
        for i, (a, b) in enumerate(((groups_far, groups_ref), (pref_far, pref_ref)))
    ]
    for copy in small:
        copy.start()
    for t in range(g.T):
        arrival(t).start()
    prey_ref[...] = jnp.zeros_like(prey_ref)

    for copy in small:
        copy.wait()
    for t in range(g.T):
        taste_ref[rows8(t), :] = jnp.full((SUB, 128), pref_ref[groups_ref[t]], jnp.float32)

    def one(t):
        arrival(t).wait()
        taste = taste_of(taste_ref, t)
        base = pl.multiple_of(t * g.tile, g.tile)
        parts = []
        for r in range(g.R):
            for lh in range(g.LH):
                at = (r * g.LH + lh) * SUB
                v = landed[pl.ds(base + lh * SUB * g.R + r, SUB, stride=g.R), :]
                field_ref[pl.ds(base + at, SUB), :] = v
                parts.append(v)
                prey_ref[at : at + SUB, :] += taste * v
        for i, packed in enumerate(pack_strips(parts)):
            strips_ref[rows8(t * g.NV + i), :] = packed

    each_tracer(g, 2, one)


def first_messages_kernel(
    g, field_ref, strips_ref, mine_ref, other_ref, depth_ref, east_ref, north_ref,
    xev_ref, xod_ref, y_ref, extra_ref,
):
    x_even = is_even("gx")
    flux = flux_reader(g, mine_ref, other_ref)
    zero = jnp.zeros((SUB, 128), jnp.float32)

    def put(at, low, high):
        xev_ref[at, :] = jnp.where(x_even, high, low)
        xod_ref[at, :] = jnp.where(x_even, low, high)

    def one(t):
        base = pl.multiple_of(t * g.tile, g.tile)
        for i in range(2 * g.LH):
            low = field_ref[pl.ds(base + i * SUB, SUB), :]
            high = field_ref[pl.ds(base + g.tile - 2 * g.L + i * SUB, SUB), :]
            put(rows8(t * 2 * g.LH + i), low, high)

    each_tracer(g, 2, one)
    at = g.T * 2 * g.LH
    for lh in range(g.LH):
        put(rows8(at + lh), zero, flux(0, g.R - 1, lh))
    depth = depth_ref[...].astype(jnp.float32)
    put(rows8(at + g.LH), depth, roll(depth, 2, 0))
    put(rows8(at + g.LH + 1), zero, roll(east_ref[...], 1, 0))
    extras = pack_strips(spread_rows(g, depth))
    extras += pack_strips([flux(1, r, lh) for r in range(g.R) for lh in range(g.LH)])
    extras += pack_strips(spread_rows(g, north_ref[...]))
    for i, packed in enumerate(extras):
        extra_ref[rows8(i), :] = packed
    put_messages(registers(strips_ref) + extras, y_ref)


def wet_levels(g, depths):
    level = [(sublanes() + SUB * lh).astype(jnp.float32) for lh in range(g.LH)]
    return [[level[lh] < d for lh in range(g.LH)] for d in depths]


def inner_coefficients(g, cf, flux, depth, east, north):
    tab, sub = g.inner, sublanes()
    depths = [spread(depth, r) for r in range(g.R)]
    wet = wet_levels(g, depths)
    wet_before = wet_levels(g, [roll(d, 1, 1) for d in depths])
    for r in range(g.R):
        tab.set(cf, "kx", r + 1, 2.0 * spread(east, r))
        tab.set(cf, "ky", r, 2.0 * roll(spread(north, r), 1, 1))
        flux_z = [roll(flux(2, r, lh), 1, 0) for lh in range(g.LH)]
        for lh in range(g.LH):
            k, here = r * g.LH + lh, wet[r][lh]
            if r:
                opened = here & wet[r - 1][lh]
                tab.set_open(cf, "x", k, opened)
                tab.set_flux(cf, "x", k, opened, flux(0, r - 1, lh))
            opened = here & wet_before[r][lh]
            tab.set_open(cf, "y", k, opened)
            tab.set_flux(cf, "y", k, opened, roll(flux(1, r, lh), 1, 1))
            opened = here if lh else here & (sub > 0)
            above = jnp.where(sub == 0, flux_z[lh - 1], flux_z[lh]) if lh else flux_z[lh]
            tab.set_open(cf, "z", k, opened)
            tab.set_flux(cf, "z", k, opened, above)


def outer_coefficients(g, cf, extra_x, flux, depth, east):
    tab = g.outer
    depth_low, depth_high = extra_x(g.LH)
    depths = [spread(depth_low, 0), spread(depth_low, 1), spread(depth, 0), spread(depth, g.R - 1)]
    depths += [spread(depth_high, 0), spread(depth_high, 1)]
    wet = wet_levels(g, depths)
    tab.set(cf, "kx", 0, 2.0 * spread(extra_x(g.LH + 1)[0], 0))
    for lh in range(g.LH):
        for face, row in enumerate((0, 1, 3, 4)):
            tab.set_open(cf, "x", face * g.LH + lh, wet[row][lh] & wet[row + 1][lh])
        tab.set_flux(cf, "x", lh, wet[1][lh] & wet[2][lh], extra_x(lh)[0])
        tab.set_flux(cf, "x", g.LH + lh, wet[3][lh] & wet[4][lh], flux(0, g.R - 1, lh))


def strip_coefficients(g, cf, extra_y, extra_ref):
    tab, lane = g.ends, lanes()
    half = (lane // WIDE) % g.LH
    level = (sublanes() + SUB * half).astype(jnp.float32)
    for i in range(g.NV):
        full = []
        for which in range(3):
            own = which * g.NV + i
            slot = g.T * g.NV + own
            full.append(full_strips(extra_ref[rows8(own), :], *extra_y(slot // SLOTS), slot % SLOTS))
        wet = [level < roll(full[0], -away, 1) for away in (-2, -1, 0, 1, 2)]
        opened = [a & b for a, b in zip(wet, wet[1:])]
        for face in range(4):
            tab.set_open(cf, "s", face * g.NV + i, opened[face])
        for face in range(2):
            flux, kappa = (roll(v, 1 - face, 1) for v in full[1:])
            tab.set_flux(cf, "s", face * g.NV + i, opened[1 + face], flux)
            tab.set(cf, "ks", face * g.NV + i, 2.0 * kappa)


def end_lanes():
    lane = lanes()
    return (lane < 2) | (lane >= 126)


def inside(g, cf, field_ref, part_ref, tend_ref=None, whole_ref=None):
    sub = sublanes()
    ends, top, bottom = end_lanes(), sub == 0, sub == SUB - 1

    def coef(name, index):
        return g.inner.get(cf, name, index)

    def shift_down(v):
        rolled = [roll(x, 1, 0) for x in v]
        return rolled[:1] + [
            jnp.where(top, rolled[i - 1], rolled[i]) for i in range(1, g.LH)
        ]

    def shift_up(v):
        rolled = [roll(x, -1, 0) for x in v]
        return [jnp.where(bottom, rolled[(i + 1) % g.LH], rolled[i]) for i in range(g.LH)]

    def one(t):
        base = pl.multiple_of(t * g.tile, g.tile)
        for r in range(g.R):
            index = [r * g.LH + lh for lh in range(g.LH)]
            at = [pl.ds(base + k * SUB, SUB) for k in index]
            cells = [field_ref[a, :] for a in at]
            if whole_ref is not None:
                cells = [c + end_columns(g, tend_ref, t, k) for k, c in zip(index, cells)]
                for a, c in zip(at, cells):
                    whole_ref[a, :] = c
            news = []
            for k, c in zip(index, cells):
                j = coef("hy", k) * (c - roll(c, 1, 1))
                s = limited(j, roll(j, -1, 1))
                flow = coef("py", k) * roll(c + s, 1, 1) + coef("my", k) * (c - s)
                flow = flow - coef("ky", r) * j
                news.append(c + jnp.where(ends, 0.0, flow - roll(flow, -1, 1)))
            j = [coef("hz", k) * (c - a) for k, c, a in zip(index, cells, shift_down(cells))]
            s = [limited(a, b) for a, b in zip(j, shift_up(j))]
            above = shift_down([c + v for c, v in zip(cells, s)])
            flow = [
                coef("pz", k) * a + coef("mz", k) * (c - v)
                for k, a, c, v in zip(index, above, cells, s)
            ]
            for a, new, high, low in zip(at, news, flow, shift_up(flow)):
                part_ref[a, :] = new + (high - low)

    return one


def inside_kernel(
    g, ahead, field_ref, mine_ref, other_ref, depth_ref, east_ref, north_ref, part_ref, cf
):
    inner_coefficients(
        g, cf, flux_reader(g, mine_ref, other_ref), depth_ref[...].astype(jnp.float32),
        east_ref[...], north_ref[...],
    )
    each_tracer(g, ahead, inside(g, cf, field_ref, part_ref))


def strip_tendency(g, cf, full, i):
    def coef(name, face):
        return g.ends.get(cf, name, face * g.NV + i)

    cell = [roll(full, -away, 1) for away in (-2, -1, 0, 1, 2)]
    j = [coef("hs", face) * (cell[face + 1] - cell[face]) for face in range(4)]
    s = [limited(a, b) for a, b in zip(j, j[1:])]
    flow = [
        coef("ps", f) * (cell[f + 1] + s[f])
        + coef("ms", f) * (cell[f + 2] - s[f + 1])
        - coef("ks", f) * j[f + 1]
        for f in range(2)
    ]
    tend = flow[0] - flow[1]
    place = lanes() % WIDE
    tend = jnp.where(place < 10, tend, roll(tend, 8, 1))
    return jnp.where((place >= 8) & (place < 12), tend, 0.0)


def all_strip_tendencies(g, cf, strips_ref, sides, tend_ref):
    for n in range(g.T * g.NV):
        full = full_strips(strips_ref[rows8(n), :], *sides(n // SLOTS), n % SLOTS)
        tend_ref[rows8(n), :] = strip_tendency(g, cf, full, n % g.NV)


def end_columns(g, tend_ref, t, k):
    v, n = divmod(k, EACH)
    return jnp.where(end_lanes(), roll(tend_ref[rows8(t * g.NV + v), :], -(WIDE * n + 10), 1), 0.0)


def set_factor(g, total, factor, grazers_ref, prey_refs):
    for r in range(g.R):
        for lh in range(g.LH):
            at = rows8(r * g.LH + lh)
            prey = sum(ref[at, :] for ref in prey_refs)
            grazers = grazers_ref[pl.ds(lh * SUB * g.R + r, SUB, stride=g.R), :]
            factor[at, :] = grazers / (1.0 + 4.0 * prey / total)


def finish(g, inner, outer, t, field_ref, part_ref, sides, emit):
    base = pl.multiple_of(t * g.tile, g.tile)

    def cell(r, lh):
        if 0 <= r < g.R:
            return field_ref[pl.ds(base + (r * g.LH + lh) * SUB, SUB), :]
        i = r + 2 if r < 0 else r - g.R
        return sides(t * 2 * g.LH + i * g.LH + lh)[0 if r < 0 else 1]

    def coef(name, f, lh):
        if 0 < f < g.R:
            return g.inner.get(inner, name, f * g.LH + lh)
        if name == "hx":
            return g.outer.get(outer, name, {-1: 0, 0: 1, g.R: 2, g.R + 1: 3}[f] * g.LH + lh)
        return g.outer.get(outer, name, (g.LH if f else 0) + lh)

    state = [None] * g.LH
    for f in range(-1, g.R + 2):
        for lh in range(g.LH):
            if f < 0:
                below = cell(-2, lh)
                here = cell(-1, lh)
                state[lh] = (here, coef("hx", f, lh) * (here - below), None, None)
                continue
            c, j, left, carried = state[lh]
            up = cell(f, lh)
            j_up = coef("hx", f, lh) * (up - c)
            s = limited(j, j_up)
            if f > 0:
                kap = g.inner.get(inner, "kx", f - 1) if f > 1 else g.outer.get(outer, "kx", 0)
                flow = coef("px", f - 1, lh) * left + coef("mx", f - 1, lh) * (c - s) - kap * j
                if f > 1:
                    r = f - 2
                    k = r * g.LH + lh
                    old = cell(r, lh)
                    new = part_ref[pl.ds(base + k * SUB, SUB), :] + (carried - flow)
                    emit(r, lh, old, new)
                carried = flow
            state[lh] = (up, j_up, c + s, carried)


def reader(even, ev_ref, od_ref):
    def sides(i):
        at = rows8(i)
        return split_sides(even, ev_ref[at, :], od_ref[at, :])

    return sides


def border_kernel(
    g, total, ahead,
    field_ref, part_ref, xev_ref, xod_ref, inner, mine_ref, other_ref, depth_ref, east_ref,
    grazers_ref, taste_ref, *rest,
):
    prey_refs, (out_ref, strips_ref, prey_ref, outer, factor) = rest[:-5], rest[-5:]
    x_sides = reader(is_even("gx"), xev_ref, xod_ref)
    outer_coefficients(
        g, outer, lambda i: x_sides(g.T * 2 * g.LH + i), flux_reader(g, mine_ref, other_ref),
        depth_ref[...].astype(jnp.float32), east_ref[...],
    )
    set_factor(g, total, factor, grazers_ref, prey_refs)
    prey_ref[...] = jnp.zeros_like(prey_ref)

    def one(t):
        taste = taste_of(taste_ref, t)
        base = pl.multiple_of(t * g.tile, g.tile)
        news = {}

        def emit(r, lh, old, new):
            at = (r * g.LH + lh) * SUB
            new = new - (taste * factor[at : at + SUB, :]) * old
            out_ref[pl.ds(base + at, SUB), :] = new
            prey_ref[at : at + SUB, :] += taste * new
            news[r, lh] = new

        finish(g, inner, outer, t, field_ref, part_ref, x_sides, emit)
        parts = [news[r, lh] for r in range(g.R) for lh in range(g.LH)]
        for i, packed in enumerate(pack_strips(parts)):
            strips_ref[rows8(t * g.NV + i), :] = packed

    each_tracer(g, ahead, one)


def second_messages_kernel(
    g, field_ref, strips_ref, next_ref, prey_ref, extra_ref, yev_ref, yod_ref, taste_ref,
    xev2_ref, xod2_ref, y2_ref, strips2_ref, prey2_ref, tend_ref, ends, grazed,
):
    x_even = is_even("gx")
    y_sides = reader(is_even("gy"), yev_ref, yod_ref)
    strip_coefficients(g, ends, y_sides, extra_ref)
    all_strip_tendencies(g, ends, strips_ref, y_sides, tend_ref)
    packed = [next_ref[rows8(n), :] + tend_ref[rows8(n), :] for n in range(g.T * g.NV)]
    for n, one_packed in enumerate(packed):
        strips2_ref[rows8(n), :] = one_packed
    put_messages(packed, y2_ref)
    for i in range(g.NV):
        grazed[rows8(i), :] = sum(
            taste_of(taste_ref, t) * tend_ref[rows8(t * g.NV + i), :] for t in range(g.T)
        )
    for k in range(g.K):
        prey2_ref[rows8(k), :] = prey_ref[rows8(k), :] + end_columns(g, grazed, 0, k)

    def one(t):
        for i in range(2 * g.LH):
            j = i + (g.R - 2) * g.LH
            low, high = (
                field_ref[rows8(t * g.K + k), :] + end_columns(g, tend_ref, t, k) for k in (i, j)
            )
            at = rows8(t * 2 * g.LH + i)
            xev2_ref[at, :] = jnp.where(x_even, high, low)
            xod2_ref[at, :] = jnp.where(x_even, low, high)

    each_tracer(g, 6, one)


def transport_two_kernel(
    g, total, ahead, field_ref, tend_ref, xev_ref, xod_ref, inner, outer, grazers_ref, taste_ref, *rest
):
    prey_refs, (out_ref, whole_ref, part_ref, factor) = rest[:-4], rest[-4:]
    set_factor(g, total, factor, grazers_ref, prey_refs)
    x_sides = reader(is_even("gx"), xev_ref, xod_ref)
    early = inside(g, inner, field_ref, part_ref, tend_ref, whole_ref)

    def late(t):
        taste = taste_of(taste_ref, t)

        def emit(r, lh, old, new):
            k = r * g.LH + lh
            out_ref[rows8(t * g.K + k), :] = new - (taste * factor[rows8(k), :]) * old

        finish(g, inner, outer, t, whole_ref, part_ref, x_sides, emit)

    def group(body, i):
        for more in range(ahead):
            body(i * ahead + more)

    def both(i, carry):
        group(late, i - 1)
        group(early, i)
        return carry

    groups = g.T // ahead
    group(early, 0)
    lax.fori_loop(1, groups, both, 0)
    group(late, groups - 1)
    for t in range(groups * ahead, g.T):
        early(t)
        late(t)


def result_kernel(
    g, ahead, field_ref, strips_ref, yod_ref, yev_ref, ends, out_ref, tend_ref, leaving, sems
):
    y_sides = reader(is_even("gy"), yev_ref, yod_ref)
    all_strip_tendencies(g, ends, strips_ref, y_sides, tend_ref)

    def departure(t):
        at = pl.ds(pl.multiple_of(t * g.tile, g.tile), g.tile)
        return pltpu.make_async_copy(leaving.at[at, :], out_ref.at[at, :], sems.at[t])

    def one(t):
        base = pl.multiple_of(t * g.tile, g.tile)
        for r in range(g.R):
            for lh in range(g.LH):
                k = r * g.LH + lh
                new = field_ref[rows8(t * g.K + k), :] + end_columns(g, tend_ref, t, k)
                leaving[pl.ds(base + lh * SUB * g.R + r, SUB, stride=g.R), :] = new
        departure(t).start()

    each_tracer(g, ahead, one)
    for t in range(g.T):
        departure(t).wait()


def call(body, outs, operands, far=0, far_out=False, scratch=()):
    spaces = [pltpu.HBM if i < far else pltpu.VMEM for i in range(len(operands))]
    operands = [
        pltpu.with_memory_space_constraint(a, space) if space == pltpu.HBM else a
        for a, space in zip(operands, spaces)
    ]
    return pl.pallas_call(
        body,
        out_shape=[jax.ShapeDtypeStruct((rows, 128), jnp.float32) for rows in outs],
        in_specs=[pl.BlockSpec(memory_space=space) for space in spaces],
        out_specs=[pl.BlockSpec(memory_space=pltpu.HBM if far_out else pltpu.VMEM)] * len(outs),
        scratch_shapes=[
            pltpu.VMEM((rows, 128), jnp.float32) if isinstance(rows, int) else rows
            for rows in scratch
        ],
        compiler_params=pltpu.CompilerParams(vmem_limit_bytes=LIM),
    )(*operands)


def pair_swap(values, axis, start):
    pairs = []
    for i in range(start, lax.axis_size(axis) - 1, 2):
        pairs += [(i, i + 1), (i + 1, i)]
    if not pairs:
        return jnp.zeros_like(values)
    return lax.ppermute(values, axis, pairs)


def tracer_swap(values):
    return lax.ppermute(values, "tracer", [(0, 1), (1, 0)])


def all_prey(values):
    if lax.axis_size("tracer") == 2:
        return [values, tracer_swap(values)]
    return [lax.psum(values, "tracer")]


def neighbours(x_ev, x_od, y):
    y_ev, y_od = pair_swap(y, "gy", 0), pair_swap(y, "gy", 1)
    return pair_swap(x_ev, "gx", 0), pair_swap(x_od, "gx", 1), y_ev, y_od


def on_device(tracers, fluxes, diff_east, diff_north, column_depth, grazers, groups, preference):
    tr_dev, levels, rows, cols = tracers.shape
    parts = lax.axis_size("tracer")
    if not (cols == 128 and rows == SUB and levels == 2 * SUB and tr_dev % 2 == 0):
        return plain(
            tracers, fluxes, diff_east, diff_north, column_depth, grazers, groups, preference
        )
    g = Geo(tr_dev, levels, rows, cols)
    total = float(tr_dev * parts)
    flat = tracers.reshape(-1, cols)
    grazers = grazers.reshape(-1, cols)
    cells = g.T * g.tile
    copies = pltpu.SemaphoreType.DMA((g.T,))

    if parts == 2:
        mine = fluxes.reshape(-1, cols)
        other = tracer_swap(mine)
    else:
        gathered = lax.all_gather(fluxes, "tracer", axis=1, tiled=True)
        mine, other = (gathered[:, i : i + SUB].reshape(-1, cols) for i in (0, SUB))
    field, strips, prey, taste = call(
        functools.partial(load_kernel, g),
        [cells, g.T * g.SR, g.T * 2 * g.L + g.L + 3 * SUB, g.T * SUB],
        [flat, groups, preference],
        far=3,
        scratch=[cells, copies, pltpu.SMEM(groups.shape, groups.dtype),
                 pltpu.SMEM(preference.shape, preference.dtype), pltpu.SemaphoreType.DMA((2,))],
    )
    prey = all_prey(prey)
    x_rows = g.T * 2 * g.L
    x_more = x_rows + g.L + 2 * SUB
    *messages, extra = call(
        functools.partial(first_messages_kernel, g),
        [x_more, x_more, g.my1 * SUB, 3 * g.SR],
        [field, strips, mine, other, column_depth, diff_east, diff_north],
    )
    messages = neighbours(*messages)
    part, inner = call(
        functools.partial(inside_kernel, g, INSIDE),
        [cells, g.inner.rows],
        [field, mine, other, column_depth, diff_east, diff_north],
    )
    field, next_strips, next_prey, outer = call(
        functools.partial(border_kernel, g, total, FINISH),
        [cells, g.T * g.SR, g.tile, g.outer.rows],
        [field, part, *messages[:2], inner, mine, other, column_depth, diff_east, grazers, taste,
         *prey],
        scratch=[g.tile],
    )
    *messages, strips, prey, tend, ends = call(
        functools.partial(second_messages_kernel, g),
        [x_rows, x_rows, g.my2 * SUB, g.T * g.SR, g.tile, g.T * g.SR, g.ends.rows],
        [field, strips, next_strips, next_prey, extra, *messages[2:], taste],
        scratch=[g.SR],
    )
    prey = all_prey(prey)
    messages = neighbours(*messages)
    messages = messages[0], messages[1], messages[3], messages[2]
    (field,) = call(
        functools.partial(transport_two_kernel, g, total, BOTH),
        [cells],
        [field, tend, *messages[:2], inner, outer, grazers, taste, *prey],
        scratch=[cells, cells, g.tile],
    )
    (out,) = call(
        functools.partial(result_kernel, g, LAST),
        [cells],
        [field, strips, *messages[2:], ends],
        far_out=True,
        scratch=[g.T * g.SR, cells, copies],
    )
    return out.reshape(tracers.shape)


def solution(mesh):
    placed = (
        P("tracer", None, "gx", "gy"),
        P(None, "tracer", "gx", "gy"),
        P("gx", "gy"),
        P("gx", "gy"),
        P("gx", "gy"),
        P(None, "gx", "gy"),
        P("tracer"),
        P(),
    )
    return jax.shard_map(
        on_device,
        mesh=mesh,
        in_specs=placed,
        out_specs=P("tracer", None, "gx", "gy"),
        check_vma=False,
    )
```

```python
import functools

import jax
import jax.numpy as jnp
from jax import lax
from jax.experimental import pallas as pl
from jax.experimental.pallas import tpu as pltpu
from jax.sharding import PartitionSpec as P

STEPS = 2
SUB = 8
LIM = 48 * 1024 * 1024
INSIDE, FINISH, BOTH, LAST = 3, 3, 3, 6


def with_halo(cells, sides, width):
    for axis, dim in sides:
        count = lax.axis_size(axis)
        ends = count - 1
        head = lax.slice_in_dim(cells, 0, width, axis=dim)
        tail = lax.slice_in_dim(cells, cells.shape[dim] - width, cells.shape[dim], axis=dim)
        cells = jnp.concatenate(
            [
                lax.ppermute(tail, axis, [(i, (i + 1) % count) for i in range(ends)]),
                cells,
                lax.ppermute(head, axis, [((i + 1) % count, i) for i in range(ends)]),
            ],
            axis=dim,
        )
    return cells


def minmod(jump_low, jump_high):
    return jnp.maximum(0.0, jnp.minimum(jump_low, jump_high)) + jnp.minimum(
        0.0, jnp.maximum(jump_low, jump_high)
    )


def window(values, low_end, high_end, direction):
    return lax.slice_in_dim(values, low_end, high_end, axis=direction % values.ndim)


def face_terms(tracer_field, open_faces, face_flux, face_kappa, direction):
    length = tracer_field.shape[direction % tracer_field.ndim] - 4
    jump_face = open_faces * (
        window(tracer_field, 1, length + 4, direction)
        - window(tracer_field, 0, length + 3, direction)
    )
    slopes = minmod(
        window(jump_face, 0, length + 2, direction), window(jump_face, 1, length + 3, direction)
    )
    left_value = window(tracer_field, 1, length + 2, direction) + 0.5 * window(
        slopes, 0, length + 1, direction
    )
    right_value = window(tracer_field, 2, length + 3, direction) - 0.5 * window(
        slopes, 1, length + 2, direction
    )
    carried = face_flux * jnp.where(face_flux > 0.0, left_value, right_value)
    if face_kappa is not None:
        carried = carried - face_kappa * window(jump_face, 1, length + 2, direction)
    return window(carried, 0, length, direction) - window(carried, 1, length + 1, direction)


def plain(tracers, fluxes, diff_east, diff_north, column_depth, grazers, groups, preference):
    tr_dev, levels, rows_dev, cols_dev = tracers.shape
    total_tracers = tr_dev * lax.axis_size("tracer")
    level_index = lax.broadcasted_iota(jnp.int32, (levels, rows_dev, cols_dev), 0)
    wet_cells = (level_index < column_depth[None]).astype(jnp.float32)
    all_fluxes = lax.all_gather(fluxes, "tracer", axis=1, tiled=True)
    stacked = jnp.concatenate(
        [all_fluxes[0], all_fluxes[1], wet_cells, diff_east[None], diff_north[None]], 0
    )
    rimmed = with_halo(stacked, (("gx", 1), ("gy", 2)), 2)
    east_ext = rimmed[:levels]
    north_ext = rimmed[levels : 2 * levels]
    downward = all_fluxes[2]
    wet_ext = rimmed[-(levels + 2) : -2]
    kx_ext = rimmed[-2]
    ky_ext = rimmed[-1]
    open_x = wet_ext[:, :-1, 2:-2] * wet_ext[:, 1:, 2:-2]
    open_y = wet_ext[:, 2:-2, :-1] * wet_ext[:, 2:-2, 1:]
    flux_x = east_ext[:, 1 : rows_dev + 2, 2:-2] * open_x[:, 1 : rows_dev + 2]
    kappa_x = kx_ext[None, 1 : rows_dev + 2, 2:-2] * open_x[:, 1 : rows_dev + 2]
    flux_y = north_ext[:, 2:-2, 1 : cols_dev + 2] * open_y[:, :, 1 : cols_dev + 2]
    kappa_y = ky_ext[None, 2:-2, 1 : cols_dev + 2] * open_y[:, :, 1 : cols_dev + 2]
    wet_z = jnp.pad(wet_cells, ((2, 2), (0, 0), (0, 0)))
    open_z = wet_z[:-1] * wet_z[1:]
    flux_z = jnp.pad(downward, ((1, 0), (0, 0), (0, 0))) * open_z[1 : levels + 2]
    group_match = (
        groups[:, None] == lax.broadcasted_iota(jnp.int32, (1, preference.shape[0]), 1)
    ).astype(jnp.float32)
    grazing_pref = jnp.sum(group_match * preference[None, :], axis=1)
    tracer_field = tracers
    for step_index in range(STEPS):
        prey_local = jnp.sum(grazing_pref[:, None, None, None] * tracer_field, axis=0)
        prey_total = lax.psum(prey_local, "tracer")
        factor = grazers / (1.0 + 4.0 * prey_total / total_tracers)
        extended = with_halo(tracer_field, (("gx", 2), ("gy", 3)), 2)
        tendency = face_terms(extended[:, :, :, 2:-2], open_x, flux_x, kappa_x, -2)
        tendency = tendency + face_terms(extended[:, :, 2:-2, :], open_y, flux_y, kappa_y, -1)
        padded_z = jnp.pad(tracer_field, ((0, 0), (2, 2), (0, 0), (0, 0)))
        tendency = tendency + face_terms(padded_z, open_z, flux_z, None, -3)
        tracer_field = (
            tracer_field + tendency - grazing_pref[:, None, None, None] * factor * tracer_field
        )
    return tracer_field


WIDE = 16
EACH = 128 // WIDE
SLOTS = WIDE // 4


class Geo:
    def __init__(self, tr_dev, levels, rows, cols):
        self.T, self.L, self.R, self.C = tr_dev, levels, rows, cols
        self.LH = levels // SUB
        self.tile = rows * levels
        self.K = rows * self.LH
        self.NV = self.K // EACH
        self.SR = self.NV * SUB
        self.my1 = -(-(tr_dev + 3) * self.NV // SLOTS)
        self.my2 = -(-tr_dev * self.NV // SLOTS)
        self.inner = Table(
            hx=(rows + 1) * self.LH, px=(rows + 1) * self.LH, mx=(rows + 1) * self.LH,
            kx=rows + 1, hy=self.K, py=self.K, my=self.K, ky=rows,
            hz=self.K, pz=self.K, mz=self.K,
        )
        self.outer = Table(
            hx=4 * self.LH, px=2 * self.LH, mx=2 * self.LH, kx=1
        )
        self.ends = Table(
            hs=4 * self.NV, ps=2 * self.NV, ms=2 * self.NV, ks=2 * self.NV
        )


class Table:
    def __init__(self, **counts):
        self.at, self.rows = {}, 0
        for name, count in counts.items():
            self.at[name] = self.rows
            self.rows += count * SUB

    def get(self, ref, name, index):
        at = self.at[name] + index * SUB
        return ref[at : at + SUB, :]

    def set(self, ref, name, index, value):
        at = self.at[name] + index * SUB
        ref[at : at + SUB, :] = value

    def set_flux(self, ref, axis, index, opened, flux):
        flux = jnp.where(opened, flux, 0.0)
        self.set(ref, "p" + axis, index, jnp.maximum(flux, 0.0))
        self.set(ref, "m" + axis, index, jnp.minimum(flux, 0.0))

    def set_open(self, ref, axis, index, opened):
        self.set(ref, "h" + axis, index, jnp.where(opened, 0.5, 0.0))


def lanes():
    return lax.broadcasted_iota(jnp.int32, (SUB, 128), 1)


def sublanes():
    return lax.broadcasted_iota(jnp.int32, (SUB, 128), 0)


def roll(v, by, axis):
    by = by % v.shape[axis]
    return v if by == 0 else pltpu.roll(v, by, axis)


def registers(ref):
    return [ref[i : i + SUB, :] for i in range(0, ref.shape[0], SUB)]


def rows8(index):
    return pl.ds(pl.multiple_of(index * SUB, SUB), SUB)


def pack_strips(parts):
    lane = lanes()
    out = []
    for v in range(0, len(parts), EACH):
        packed = jnp.zeros((SUB, 128), jnp.float32)
        for k, part in enumerate(parts[v : v + EACH]):
            inside = (lane >= WIDE * k + 6) & (lane < WIDE * k + 14)
            packed = jnp.where(inside, roll(part, WIDE * k + 10, 1), packed)
        out.append(packed)
    return out


def put_messages(packed, out_ref):
    slot = (lanes() % WIDE) // 4
    for v in range(0, len(packed), SLOTS):
        out = jnp.zeros((SUB, 128), jnp.float32)
        for m, one in enumerate(packed[v : v + SLOTS]):
            out = jnp.where(slot == m, roll(one, 4 * m - 8, 1), out)
        out_ref[rows8(v // SLOTS), :] = out


def full_strips(own, from_lower, from_upper, m):
    place = lanes() % WIDE
    out = jnp.where(place < 2, roll(from_lower, -4 * m, 1), roll(own, -8, 1))
    out = jnp.where(place < 6, out, own)
    out = jnp.where(place < 10, out, roll(from_upper, 8 - 4 * m, 1))
    return jnp.where(place < 12, out, 0.0)


def spread(rows, r):
    return jnp.broadcast_to(rows[r : r + 1, :], (SUB, 128))


def spread_rows(g, rows):
    return [spread(rows, r) for r in range(g.R) for _ in range(g.LH)]


def taste_of(taste_ref, t):
    return taste_ref[rows8(t), :]


def is_even(axis):
    return lax.rem(lax.axis_index(axis), 2) == 0


def split_sides(even, ev, od):
    return jnp.where(even, od, ev), jnp.where(even, ev, od)


def limited(a, b):
    least, most = jnp.minimum(a, b), jnp.maximum(a, b)
    return jnp.maximum(least, jnp.minimum(most, 0.0))


def each_tracer(g, ahead, body):
    def some(i, carry):
        for more in range(ahead):
            body(i * ahead + more)
        return carry

    lax.fori_loop(0, g.T // ahead, some, 0)
    for t in range(g.T - g.T % ahead, g.T):
        body(t)


def level_rows(g, r, lh, base=0):
    return pl.ds(base + lh * g.R + r, SUB, stride=g.LH * g.R)


def flux_reader(g, fluxes_ref):
    def flux(dim, r, lh):
        return fluxes_ref[level_rows(g, r, lh, dim * g.tile), :]

    return flux


def join_fluxes(g, mine_ref, other_ref, out_ref):
    first = lax.axis_index("tracer") == 0
    single = lax.axis_size("tracer") != 2
    some = g.R * SUB
    for dim in range(3):
        a, b = (ref[dim * some : (dim + 1) * some, :] for ref in (mine_ref, other_ref))
        at = dim * g.tile
        out_ref[at : at + some, :] = a if single else jnp.where(first, a, b)
        out_ref[at + some : at + 2 * some, :] = b if single else jnp.where(first, b, a)


def load_kernel(
    g, tracers_ref, groups_far, pref_far, field_ref, strips_ref, prey_ref, taste_ref,
    landed, sems, groups_ref, pref_ref, small_sems,
):
    def arrival(t):
        at = pl.ds(pl.multiple_of(t * g.tile, g.tile), g.tile)
        return pltpu.make_async_copy(tracers_ref.at[at, :], landed.at[at, :], sems.at[t])

    small = [
        pltpu.make_async_copy(a, b, small_sems.at[i])
        for i, (a, b) in enumerate(((groups_far, groups_ref), (pref_far, pref_ref)))
    ]
    for copy in small:
        copy.start()
    for t in range(g.T):
        arrival(t).start()
    prey_ref[...] = jnp.zeros_like(prey_ref)

    for copy in small:
        copy.wait()
    for t in range(g.T):
        taste_ref[rows8(t), :] = jnp.full((SUB, 128), pref_ref[groups_ref[t]], jnp.float32)

    def one(t):
        arrival(t).wait()
        taste = taste_of(taste_ref, t)
        base = pl.multiple_of(t * g.tile, g.tile)
        parts = []
        for r in range(g.R):
            for lh in range(g.LH):
                at = (r * g.LH + lh) * SUB
                v = landed[level_rows(g, r, lh, base), :]
                field_ref[pl.ds(base + at, SUB), :] = v
                parts.append(v)
                prey_ref[at : at + SUB, :] += taste * v
        for i, packed in enumerate(pack_strips(parts)):
            strips_ref[rows8(t * g.NV + i), :] = packed

    each_tracer(g, 2, one)


def first_messages_kernel(
    g, field_ref, strips_ref, mine_ref, other_ref, depth_ref, east_ref, north_ref,
    xev_ref, xod_ref, y_ref, extra_ref, fluxes_ref,
):
    x_even = is_even("gx")
    join_fluxes(g, mine_ref, other_ref, fluxes_ref)
    flux = flux_reader(g, fluxes_ref)
    zero = jnp.zeros((SUB, 128), jnp.float32)

    def put(at, low, high):
        xev_ref[at, :] = jnp.where(x_even, high, low)
        xod_ref[at, :] = jnp.where(x_even, low, high)

    def one(t):
        base = pl.multiple_of(t * g.tile, g.tile)
        for i in range(2 * g.LH):
            low = field_ref[pl.ds(base + i * SUB, SUB), :]
            high = field_ref[pl.ds(base + g.tile - 2 * g.L + i * SUB, SUB), :]
            put(rows8(t * 2 * g.LH + i), low, high)

    each_tracer(g, 2, one)
    at = g.T * 2 * g.LH
    for lh in range(g.LH):
        put(rows8(at + lh), zero, flux(0, g.R - 1, lh))
    depth = depth_ref[...].astype(jnp.float32)
    put(rows8(at + g.LH), depth, roll(depth, 2, 0))
    put(rows8(at + g.LH + 1), zero, roll(east_ref[...], 1, 0))
    extras = pack_strips(spread_rows(g, depth))
    extras += pack_strips([flux(1, r, lh) for r in range(g.R) for lh in range(g.LH)])
    extras += pack_strips(spread_rows(g, north_ref[...]))
    for i, packed in enumerate(extras):
        extra_ref[rows8(i), :] = packed
    put_messages(registers(strips_ref) + extras, y_ref)


def wet_levels(g, depths):
    level = [(g.LH * sublanes() + lh).astype(jnp.float32) for lh in range(g.LH)]
    return [[level[lh] < d for lh in range(g.LH)] for d in depths]


def inner_coefficients(g, cf, flux, depth, east, north):
    tab, sub = g.inner, sublanes()
    depths = [spread(depth, r) for r in range(g.R)]
    wet = wet_levels(g, depths)
    wet_before = wet_levels(g, [roll(d, 1, 1) for d in depths])
    for r in range(g.R):
        tab.set(cf, "kx", r + 1, 2.0 * spread(east, r))
        tab.set(cf, "ky", r, 2.0 * roll(spread(north, r), 1, 1))
        flux_z = [flux(2, r, lh) for lh in range(g.LH)]
        for lh in range(g.LH):
            k, here = r * g.LH + lh, wet[r][lh]
            if r:
                opened = here & wet[r - 1][lh]
                tab.set_open(cf, "x", k, opened)
                tab.set_flux(cf, "x", k, opened, flux(0, r - 1, lh))
            opened = here & wet_before[r][lh]
            tab.set_open(cf, "y", k, opened)
            tab.set_flux(cf, "y", k, opened, roll(flux(1, r, lh), 1, 1))
            opened = here if lh else here & (sub > 0)
            above = flux_z[lh - 1] if lh else roll(flux_z[-1], 1, 0)
            tab.set_open(cf, "z", k, opened)
            tab.set_flux(cf, "z", k, opened, above)


def outer_coefficients(g, cf, extra_x, flux, depth, east):
    tab = g.outer
    depth_low, depth_high = extra_x(g.LH)
    depths = [spread(depth_low, 0), spread(depth_low, 1), spread(depth, 0), spread(depth, g.R - 1)]
    depths += [spread(depth_high, 0), spread(depth_high, 1)]
    wet = wet_levels(g, depths)
    tab.set(cf, "kx", 0, 2.0 * spread(extra_x(g.LH + 1)[0], 0))
    for lh in range(g.LH):
        for face, row in enumerate((0, 1, 3, 4)):
            tab.set_open(cf, "x", face * g.LH + lh, wet[row][lh] & wet[row + 1][lh])
        tab.set_flux(cf, "x", lh, wet[1][lh] & wet[2][lh], extra_x(lh)[0])
        tab.set_flux(cf, "x", g.LH + lh, wet[3][lh] & wet[4][lh], flux(0, g.R - 1, lh))


def strip_coefficients(g, cf, extra_y, extra_ref):
    tab, lane = g.ends, lanes()
    half = (lane // WIDE) % g.LH
    level = (g.LH * sublanes() + half).astype(jnp.float32)
    for i in range(g.NV):
        full = []
        for which in range(3):
            own = which * g.NV + i
            slot = g.T * g.NV + own
            full.append(full_strips(extra_ref[rows8(own), :], *extra_y(slot // SLOTS), slot % SLOTS))
        wet = [level < roll(full[0], -away, 1) for away in (-2, -1, 0, 1, 2)]
        opened = [a & b for a, b in zip(wet, wet[1:])]
        for face in range(4):
            tab.set_open(cf, "s", face * g.NV + i, opened[face])
        for face in range(2):
            flux, kappa = (roll(v, 1 - face, 1) for v in full[1:])
            tab.set_flux(cf, "s", face * g.NV + i, opened[1 + face], flux)
            tab.set(cf, "ks", face * g.NV + i, 2.0 * kappa)


def end_lanes():
    lane = lanes()
    return (lane < 2) | (lane >= 126)


def inside(g, cf, field_ref, part_ref, tend_ref=None, whole_ref=None):
    ends = end_lanes()

    def coef(name, index):
        return g.inner.get(cf, name, index)

    def shift_down(v):
        return [roll(v[-1], 1, 0), *v[:-1]]

    def shift_up(v):
        return [*v[1:], roll(v[0], -1, 0)]

    def one(t):
        base = pl.multiple_of(t * g.tile, g.tile)
        for r in range(g.R):
            index = [r * g.LH + lh for lh in range(g.LH)]
            at = [pl.ds(base + k * SUB, SUB) for k in index]
            cells = [field_ref[a, :] for a in at]
            if whole_ref is not None:
                cells = [c + end_columns(g, tend_ref, t, k) for k, c in zip(index, cells)]
                for a, c in zip(at, cells):
                    whole_ref[a, :] = c
            news = []
            for k, c in zip(index, cells):
                j = coef("hy", k) * (c - roll(c, 1, 1))
                s = limited(j, roll(j, -1, 1))
                flow = coef("py", k) * roll(c + s, 1, 1) + coef("my", k) * (c - s)
                flow = flow - coef("ky", r) * j
                news.append(c + jnp.where(ends, 0.0, flow - roll(flow, -1, 1)))
            j = [coef("hz", k) * (c - a) for k, c, a in zip(index, cells, shift_down(cells))]
            s = [limited(a, b) for a, b in zip(j, shift_up(j))]
            above = shift_down([c + v for c, v in zip(cells, s)])
            flow = [
                coef("pz", k) * a + coef("mz", k) * (c - v)
                for k, a, c, v in zip(index, above, cells, s)
            ]
            for a, new, high, low in zip(at, news, flow, shift_up(flow)):
                part_ref[a, :] = new + (high - low)

    return one


def inside_kernel(
    g, ahead, field_ref, fluxes_ref, depth_ref, east_ref, north_ref, part_ref, cf
):
    inner_coefficients(
        g, cf, flux_reader(g, fluxes_ref), depth_ref[...].astype(jnp.float32),
        east_ref[...], north_ref[...],
    )
    each_tracer(g, ahead, inside(g, cf, field_ref, part_ref))


def strip_tendency(g, cf, full, i):
    def coef(name, face):
        return g.ends.get(cf, name, face * g.NV + i)

    cell = [roll(full, -away, 1) for away in (-2, -1, 0, 1, 2)]
    j = [coef("hs", face) * (cell[face + 1] - cell[face]) for face in range(4)]
    s = [limited(a, b) for a, b in zip(j, j[1:])]
    flow = [
        coef("ps", f) * (cell[f + 1] + s[f])
        + coef("ms", f) * (cell[f + 2] - s[f + 1])
        - coef("ks", f) * j[f + 1]
        for f in range(2)
    ]
    tend = flow[0] - flow[1]
    place = lanes() % WIDE
    tend = jnp.where(place < 10, tend, roll(tend, 8, 1))
    return jnp.where((place >= 8) & (place < 12), tend, 0.0)


def all_strip_tendencies(g, cf, strips_ref, sides, tend_ref):
    for n in range(g.T * g.NV):
        full = full_strips(strips_ref[rows8(n), :], *sides(n // SLOTS), n % SLOTS)
        tend_ref[rows8(n), :] = strip_tendency(g, cf, full, n % g.NV)


def end_columns(g, tend_ref, t, k):
    v, n = divmod(k, EACH)
    return jnp.where(end_lanes(), roll(tend_ref[rows8(t * g.NV + v), :], -(WIDE * n + 10), 1), 0.0)


def set_factor(g, total, factor, grazers_ref, prey_refs):
    for r in range(g.R):
        for lh in range(g.LH):
            at = rows8(r * g.LH + lh)
            prey = sum(ref[at, :] for ref in prey_refs)
            grazers = grazers_ref[level_rows(g, r, lh), :]
            factor[at, :] = grazers / (1.0 + 4.0 * prey / total)


def finish(g, inner, outer, t, field_ref, part_ref, sides, emit):
    base = pl.multiple_of(t * g.tile, g.tile)

    def cell(r, lh):
        if 0 <= r < g.R:
            return field_ref[pl.ds(base + (r * g.LH + lh) * SUB, SUB), :]
        i = r + 2 if r < 0 else r - g.R
        return sides(t * 2 * g.LH + i * g.LH + lh)[0 if r < 0 else 1]

    def coef(name, f, lh):
        if 0 < f < g.R:
            return g.inner.get(inner, name, f * g.LH + lh)
        if name == "hx":
            return g.outer.get(outer, name, {-1: 0, 0: 1, g.R: 2, g.R + 1: 3}[f] * g.LH + lh)
        return g.outer.get(outer, name, (g.LH if f else 0) + lh)

    state = [None] * g.LH
    for f in range(-1, g.R + 2):
        for lh in range(g.LH):
            if f < 0:
                below = cell(-2, lh)
                here = cell(-1, lh)
                state[lh] = (here, coef("hx", f, lh) * (here - below), None, None)
                continue
            c, j, left, carried = state[lh]
            up = cell(f, lh)
            j_up = coef("hx", f, lh) * (up - c)
            s = limited(j, j_up)
            if f > 0:
                kap = g.inner.get(inner, "kx", f - 1) if f > 1 else g.outer.get(outer, "kx", 0)
                flow = coef("px", f - 1, lh) * left + coef("mx", f - 1, lh) * (c - s) - kap * j
                if f > 1:
                    r = f - 2
                    k = r * g.LH + lh
                    old = cell(r, lh)
                    new = part_ref[pl.ds(base + k * SUB, SUB), :] + (carried - flow)
                    emit(r, lh, old, new)
                carried = flow
            state[lh] = (up, j_up, c + s, carried)


def reader(even, ev_ref, od_ref):
    def sides(i):
        at = rows8(i)
        return split_sides(even, ev_ref[at, :], od_ref[at, :])

    return sides


def border_kernel(
    g, total, ahead,
    field_ref, part_ref, xev_ref, xod_ref, inner, fluxes_ref, depth_ref, east_ref,
    grazers_ref, taste_ref, *rest,
):
    prey_refs, (out_ref, strips_ref, prey_ref, outer, factor) = rest[:-5], rest[-5:]
    x_sides = reader(is_even("gx"), xev_ref, xod_ref)
    outer_coefficients(
        g, outer, lambda i: x_sides(g.T * 2 * g.LH + i), flux_reader(g, fluxes_ref),
        depth_ref[...].astype(jnp.float32), east_ref[...],
    )
    set_factor(g, total, factor, grazers_ref, prey_refs)
    prey_ref[...] = jnp.zeros_like(prey_ref)

    def one(t):
        taste = taste_of(taste_ref, t)
        base = pl.multiple_of(t * g.tile, g.tile)
        news = {}

        def emit(r, lh, old, new):
            at = (r * g.LH + lh) * SUB
            new = new - (taste * factor[at : at + SUB, :]) * old
            out_ref[pl.ds(base + at, SUB), :] = new
            prey_ref[at : at + SUB, :] += taste * new
            news[r, lh] = new

        finish(g, inner, outer, t, field_ref, part_ref, x_sides, emit)
        parts = [news[r, lh] for r in range(g.R) for lh in range(g.LH)]
        for i, packed in enumerate(pack_strips(parts)):
            strips_ref[rows8(t * g.NV + i), :] = packed

    each_tracer(g, ahead, one)


def second_messages_kernel(
    g, field_ref, strips_ref, next_ref, prey_ref, extra_ref, yev_ref, yod_ref, taste_ref,
    xev2_ref, xod2_ref, y2_ref, strips2_ref, prey2_ref, tend_ref, ends, grazed,
):
    x_even = is_even("gx")
    y_sides = reader(is_even("gy"), yev_ref, yod_ref)
    strip_coefficients(g, ends, y_sides, extra_ref)
    all_strip_tendencies(g, ends, strips_ref, y_sides, tend_ref)
    packed = [next_ref[rows8(n), :] + tend_ref[rows8(n), :] for n in range(g.T * g.NV)]
    for n, one_packed in enumerate(packed):
        strips2_ref[rows8(n), :] = one_packed
    put_messages(packed, y2_ref)
    for i in range(g.NV):
        grazed[rows8(i), :] = sum(
            taste_of(taste_ref, t) * tend_ref[rows8(t * g.NV + i), :] for t in range(g.T)
        )
    for k in range(g.K):
        prey2_ref[rows8(k), :] = prey_ref[rows8(k), :] + end_columns(g, grazed, 0, k)

    def one(t):
        for i in range(2 * g.LH):
            j = i + (g.R - 2) * g.LH
            low, high = (
                field_ref[rows8(t * g.K + k), :] + end_columns(g, tend_ref, t, k) for k in (i, j)
            )
            at = rows8(t * 2 * g.LH + i)
            xev2_ref[at, :] = jnp.where(x_even, high, low)
            xod2_ref[at, :] = jnp.where(x_even, low, high)

    each_tracer(g, 6, one)


def transport_two_kernel(
    g, total, ahead, field_ref, tend_ref, xev_ref, xod_ref, inner, outer, grazers_ref, taste_ref, *rest
):
    prey_refs, (out_ref, whole_ref, part_ref, factor) = rest[:-4], rest[-4:]
    set_factor(g, total, factor, grazers_ref, prey_refs)
    x_sides = reader(is_even("gx"), xev_ref, xod_ref)
    early = inside(g, inner, field_ref, part_ref, tend_ref, whole_ref)

    def late(t):
        taste = taste_of(taste_ref, t)

        def emit(r, lh, old, new):
            k = r * g.LH + lh
            out_ref[rows8(t * g.K + k), :] = new - (taste * factor[rows8(k), :]) * old

        finish(g, inner, outer, t, whole_ref, part_ref, x_sides, emit)

    def group(body, i):
        for more in range(ahead):
            body(i * ahead + more)

    def both(i, carry):
        group(late, i - 1)
        group(early, i)
        return carry

    groups = g.T // ahead
    group(early, 0)
    lax.fori_loop(1, groups, both, 0)
    group(late, groups - 1)
    for t in range(groups * ahead, g.T):
        early(t)
        late(t)


def result_kernel(
    g, ahead, field_ref, strips_ref, yod_ref, yev_ref, ends, out_ref, tend_ref, leaving, sems
):
    y_sides = reader(is_even("gy"), yev_ref, yod_ref)
    all_strip_tendencies(g, ends, strips_ref, y_sides, tend_ref)

    def departure(t):
        at = pl.ds(pl.multiple_of(t * g.tile, g.tile), g.tile)
        return pltpu.make_async_copy(leaving.at[at, :], out_ref.at[at, :], sems.at[t])

    def one(t):
        base = pl.multiple_of(t * g.tile, g.tile)
        for r in range(g.R):
            for lh in range(g.LH):
                k = r * g.LH + lh
                new = field_ref[rows8(t * g.K + k), :] + end_columns(g, tend_ref, t, k)
                leaving[level_rows(g, r, lh, base), :] = new
        departure(t).start()

    each_tracer(g, ahead, one)
    for t in range(g.T):
        departure(t).wait()


def call(body, outs, operands, far=0, far_out=False, scratch=()):
    spaces = [pltpu.HBM if i < far else pltpu.VMEM for i in range(len(operands))]
    operands = [
        pltpu.with_memory_space_constraint(a, space) if space == pltpu.HBM else a
        for a, space in zip(operands, spaces)
    ]
    return pl.pallas_call(
        body,
        out_shape=[jax.ShapeDtypeStruct((rows, 128), jnp.float32) for rows in outs],
        in_specs=[pl.BlockSpec(memory_space=space) for space in spaces],
        out_specs=[pl.BlockSpec(memory_space=pltpu.HBM if far_out else pltpu.VMEM)] * len(outs),
        scratch_shapes=[
            pltpu.VMEM((rows, 128), jnp.float32) if isinstance(rows, int) else rows
            for rows in scratch
        ],
        compiler_params=pltpu.CompilerParams(vmem_limit_bytes=LIM),
    )(*operands)


def pair_swap(values, axis, start):
    pairs = []
    for i in range(start, lax.axis_size(axis) - 1, 2):
        pairs += [(i, i + 1), (i + 1, i)]
    if not pairs:
        return jnp.zeros_like(values)
    return lax.ppermute(values, axis, pairs)


def tracer_swap(values):
    return lax.ppermute(values, "tracer", [(0, 1), (1, 0)])


def all_prey(values):
    if lax.axis_size("tracer") == 2:
        return [values, tracer_swap(values)]
    return [lax.psum(values, "tracer")]


def neighbours(x_ev, x_od, y):
    y_ev, y_od = pair_swap(y, "gy", 0), pair_swap(y, "gy", 1)
    return pair_swap(x_ev, "gx", 0), pair_swap(x_od, "gx", 1), y_ev, y_od


def on_device(tracers, fluxes, diff_east, diff_north, column_depth, grazers, groups, preference):
    tr_dev, levels, rows, cols = tracers.shape
    parts = lax.axis_size("tracer")
    if not (cols == 128 and rows == SUB and levels == 2 * SUB and tr_dev % 2 == 0):
        return plain(
            tracers, fluxes, diff_east, diff_north, column_depth, grazers, groups, preference
        )
    g = Geo(tr_dev, levels, rows, cols)
    total = float(tr_dev * parts)
    flat = tracers.reshape(-1, cols)
    grazers = grazers.reshape(-1, cols)
    cells = g.T * g.tile
    copies = pltpu.SemaphoreType.DMA((g.T,))

    if parts == 2:
        mine = fluxes.reshape(-1, cols)
        other = tracer_swap(mine)
    else:
        gathered = lax.all_gather(fluxes, "tracer", axis=1, tiled=True)
        mine, other = (gathered[:, i : i + SUB].reshape(-1, cols) for i in (0, SUB))
    field, strips, prey, taste = call(
        functools.partial(load_kernel, g),
        [cells, g.T * g.SR, g.T * 2 * g.L + g.L + 3 * SUB, g.T * SUB],
        [flat, groups, preference],
        far=3,
        scratch=[cells, copies, pltpu.SMEM(groups.shape, groups.dtype),
                 pltpu.SMEM(preference.shape, preference.dtype), pltpu.SemaphoreType.DMA((2,))],
    )
    prey = all_prey(prey)
    x_rows = g.T * 2 * g.L
    x_more = x_rows + g.L + 2 * SUB
    *messages, extra, fluxes = call(
        functools.partial(first_messages_kernel, g),
        [x_more, x_more, g.my1 * SUB, 3 * g.SR, 3 * g.tile],
        [field, strips, mine, other, column_depth, diff_east, diff_north],
    )
    messages = neighbours(*messages)
    part, inner = call(
        functools.partial(inside_kernel, g, INSIDE),
        [cells, g.inner.rows],
        [field, fluxes, column_depth, diff_east, diff_north],
    )
    field, next_strips, next_prey, outer = call(
        functools.partial(border_kernel, g, total, FINISH),
        [cells, g.T * g.SR, g.tile, g.outer.rows],
        [field, part, *messages[:2], inner, fluxes, column_depth, diff_east, grazers, taste,
         *prey],
        scratch=[g.tile],
    )
    *messages, strips, prey, tend, ends = call(
        functools.partial(second_messages_kernel, g),
        [x_rows, x_rows, g.my2 * SUB, g.T * g.SR, g.tile, g.T * g.SR, g.ends.rows],
        [field, strips, next_strips, next_prey, extra, *messages[2:], taste],
        scratch=[g.SR],
    )
    prey = all_prey(prey)
    messages = neighbours(*messages)
    messages = messages[0], messages[1], messages[3], messages[2]
    (field,) = call(
        functools.partial(transport_two_kernel, g, total, BOTH),
        [cells],
        [field, tend, *messages[:2], inner, outer, grazers, taste, *prey],
        scratch=[cells, cells, g.tile],
    )
    (out,) = call(
        functools.partial(result_kernel, g, LAST),
        [cells],
        [field, strips, *messages[2:], ends],
        far_out=True,
        scratch=[g.T * g.SR, cells, copies],
    )
    return out.reshape(tracers.shape)


def solution(mesh):
    placed = (
        P("tracer", None, "gx", "gy"),
        P(None, "tracer", "gx", "gy"),
        P("gx", "gy"),
        P("gx", "gy"),
        P("gx", "gy"),
        P(None, "gx", "gy"),
        P("tracer"),
        P(),
    )
    return jax.shard_map(
        on_device,
        mesh=mesh,
        in_specs=placed,
        out_specs=P("tracer", None, "gx", "gy"),
        check_vma=False,
    )
```

```python
import functools

import jax
import jax.numpy as jnp
from jax import lax
from jax.experimental import pallas as pl
from jax.experimental.pallas import tpu as pltpu
from jax.sharding import PartitionSpec as P

STEPS = 2
SUB = 8
LIM = 48 * 1024 * 1024
INSIDE, FINISH, BOTH, LAST = 3, 3, 2, 6


def with_halo(cells, sides, width):
    for axis, dim in sides:
        count = lax.axis_size(axis)
        ends = count - 1
        head = lax.slice_in_dim(cells, 0, width, axis=dim)
        tail = lax.slice_in_dim(cells, cells.shape[dim] - width, cells.shape[dim], axis=dim)
        cells = jnp.concatenate(
            [
                lax.ppermute(tail, axis, [(i, (i + 1) % count) for i in range(ends)]),
                cells,
                lax.ppermute(head, axis, [((i + 1) % count, i) for i in range(ends)]),
            ],
            axis=dim,
        )
    return cells


def minmod(jump_low, jump_high):
    return jnp.maximum(0.0, jnp.minimum(jump_low, jump_high)) + jnp.minimum(
        0.0, jnp.maximum(jump_low, jump_high)
    )


def window(values, low_end, high_end, direction):
    return lax.slice_in_dim(values, low_end, high_end, axis=direction % values.ndim)


def face_terms(tracer_field, open_faces, face_flux, face_kappa, direction):
    length = tracer_field.shape[direction % tracer_field.ndim] - 4
    jump_face = open_faces * (
        window(tracer_field, 1, length + 4, direction)
        - window(tracer_field, 0, length + 3, direction)
    )
    slopes = minmod(
        window(jump_face, 0, length + 2, direction), window(jump_face, 1, length + 3, direction)
    )
    left_value = window(tracer_field, 1, length + 2, direction) + 0.5 * window(
        slopes, 0, length + 1, direction
    )
    right_value = window(tracer_field, 2, length + 3, direction) - 0.5 * window(
        slopes, 1, length + 2, direction
    )
    carried = face_flux * jnp.where(face_flux > 0.0, left_value, right_value)
    if face_kappa is not None:
        carried = carried - face_kappa * window(jump_face, 1, length + 2, direction)
    return window(carried, 0, length, direction) - window(carried, 1, length + 1, direction)


def plain(tracers, fluxes, diff_east, diff_north, column_depth, grazers, groups, preference):
    tr_dev, levels, rows_dev, cols_dev = tracers.shape
    total_tracers = tr_dev * lax.axis_size("tracer")
    level_index = lax.broadcasted_iota(jnp.int32, (levels, rows_dev, cols_dev), 0)
    wet_cells = (level_index < column_depth[None]).astype(jnp.float32)
    all_fluxes = lax.all_gather(fluxes, "tracer", axis=1, tiled=True)
    stacked = jnp.concatenate(
        [all_fluxes[0], all_fluxes[1], wet_cells, diff_east[None], diff_north[None]], 0
    )
    rimmed = with_halo(stacked, (("gx", 1), ("gy", 2)), 2)
    east_ext = rimmed[:levels]
    north_ext = rimmed[levels : 2 * levels]
    downward = all_fluxes[2]
    wet_ext = rimmed[-(levels + 2) : -2]
    kx_ext = rimmed[-2]
    ky_ext = rimmed[-1]
    open_x = wet_ext[:, :-1, 2:-2] * wet_ext[:, 1:, 2:-2]
    open_y = wet_ext[:, 2:-2, :-1] * wet_ext[:, 2:-2, 1:]
    flux_x = east_ext[:, 1 : rows_dev + 2, 2:-2] * open_x[:, 1 : rows_dev + 2]
    kappa_x = kx_ext[None, 1 : rows_dev + 2, 2:-2] * open_x[:, 1 : rows_dev + 2]
    flux_y = north_ext[:, 2:-2, 1 : cols_dev + 2] * open_y[:, :, 1 : cols_dev + 2]
    kappa_y = ky_ext[None, 2:-2, 1 : cols_dev + 2] * open_y[:, :, 1 : cols_dev + 2]
    wet_z = jnp.pad(wet_cells, ((2, 2), (0, 0), (0, 0)))
    open_z = wet_z[:-1] * wet_z[1:]
    flux_z = jnp.pad(downward, ((1, 0), (0, 0), (0, 0))) * open_z[1 : levels + 2]
    group_match = (
        groups[:, None] == lax.broadcasted_iota(jnp.int32, (1, preference.shape[0]), 1)
    ).astype(jnp.float32)
    grazing_pref = jnp.sum(group_match * preference[None, :], axis=1)
    tracer_field = tracers
    for step_index in range(STEPS):
        prey_local = jnp.sum(grazing_pref[:, None, None, None] * tracer_field, axis=0)
        prey_total = lax.psum(prey_local, "tracer")
        factor = grazers / (1.0 + 4.0 * prey_total / total_tracers)
        extended = with_halo(tracer_field, (("gx", 2), ("gy", 3)), 2)
        tendency = face_terms(extended[:, :, :, 2:-2], open_x, flux_x, kappa_x, -2)
        tendency = tendency + face_terms(extended[:, :, 2:-2, :], open_y, flux_y, kappa_y, -1)
        padded_z = jnp.pad(tracer_field, ((0, 0), (2, 2), (0, 0), (0, 0)))
        tendency = tendency + face_terms(padded_z, open_z, flux_z, None, -3)
        tracer_field = (
            tracer_field + tendency - grazing_pref[:, None, None, None] * factor * tracer_field
        )
    return tracer_field


WIDE = 16
EACH = 128 // WIDE
SLOTS = WIDE // 4


class Geo:
    def __init__(self, tr_dev, levels, rows, cols):
        self.T, self.L, self.R, self.C = tr_dev, levels, rows, cols
        self.LH = levels // SUB
        self.tile = rows * levels
        self.K = rows * self.LH
        self.NV = self.K // EACH
        self.SR = self.NV * SUB
        self.my1 = -(-(tr_dev + 3) * self.NV // SLOTS)
        self.my2 = -(-tr_dev * self.NV // SLOTS)
        self.inner = Table(
            hx=(rows + 1) * self.LH, px=(rows + 1) * self.LH, mx=(rows + 1) * self.LH,
            kx=rows + 1, hy=self.K, py=self.K, my=self.K, ky=rows,
            hz=self.K, pz=self.K, mz=self.K,
            hyu=self.K, pyu=self.K, myu=self.K, kyu=rows,
        )
        self.outer = Table(
            hx=4 * self.LH, px=2 * self.LH, mx=2 * self.LH, kx=1
        )
        self.ends = Table(
            hs=4 * self.NV, ps=2 * self.NV, ms=2 * self.NV, ks=2 * self.NV
        )


class Table:
    def __init__(self, **counts):
        self.at, self.rows = {}, 0
        for name, count in counts.items():
            self.at[name] = self.rows
            self.rows += count * SUB

    def get(self, ref, name, index):
        at = self.at[name] + index * SUB
        return ref[at : at + SUB, :]

    def set(self, ref, name, index, value):
        at = self.at[name] + index * SUB
        ref[at : at + SUB, :] = value

    def set_flux(self, ref, axis, index, opened, flux):
        flux = jnp.where(opened, flux, 0.0)
        self.set(ref, "p" + axis, index, jnp.maximum(flux, 0.0))
        self.set(ref, "m" + axis, index, jnp.minimum(flux, 0.0))

    def set_open(self, ref, axis, index, opened):
        self.set(ref, "h" + axis, index, jnp.where(opened, 0.5, 0.0))


def lanes():
    return lax.broadcasted_iota(jnp.int32, (SUB, 128), 1)


def sublanes():
    return lax.broadcasted_iota(jnp.int32, (SUB, 128), 0)


def roll(v, by, axis):
    by = by % v.shape[axis]
    return v if by == 0 else pltpu.roll(v, by, axis)


def registers(ref):
    return [ref[i : i + SUB, :] for i in range(0, ref.shape[0], SUB)]


def rows8(index):
    return pl.ds(pl.multiple_of(index * SUB, SUB), SUB)


def pack_strips(parts):
    lane = lanes()
    out = []
    for v in range(0, len(parts), EACH):
        packed = jnp.zeros((SUB, 128), jnp.float32)
        for k, part in enumerate(parts[v : v + EACH]):
            inside = (lane >= WIDE * k + 6) & (lane < WIDE * k + 14)
            packed = jnp.where(inside, roll(part, WIDE * k + 10, 1), packed)
        out.append(packed)
    return out


def put_messages(packed, out_ref):
    slot = (lanes() % WIDE) // 4
    for v in range(0, len(packed), SLOTS):
        out = jnp.zeros((SUB, 128), jnp.float32)
        for m, one in enumerate(packed[v : v + SLOTS]):
            out = jnp.where(slot == m, roll(one, 4 * m - 8, 1), out)
        out_ref[rows8(v // SLOTS), :] = out


def full_strips(own, from_lower, from_upper, m):
    place = lanes() % WIDE
    out = jnp.where(place < 2, roll(from_lower, -4 * m, 1), roll(own, -8, 1))
    out = jnp.where(place < 6, out, own)
    out = jnp.where(place < 10, out, roll(from_upper, 8 - 4 * m, 1))
    return jnp.where(place < 12, out, 0.0)


def spread(rows, r):
    return jnp.broadcast_to(rows[r : r + 1, :], (SUB, 128))


def spread_rows(g, rows):
    return [spread(rows, r) for r in range(g.R) for _ in range(g.LH)]


def taste_of(taste_ref, t):
    return taste_ref[rows8(t), :]


def is_even(axis):
    return lax.rem(lax.axis_index(axis), 2) == 0


def split_sides(even, ev, od):
    return jnp.where(even, od, ev), jnp.where(even, ev, od)


def limited(a, b):
    least, most = jnp.minimum(a, b), jnp.maximum(a, b)
    return jnp.maximum(least, jnp.minimum(most, 0.0))


def each_tracer(g, ahead, body):
    def some(i, carry):
        for more in range(ahead):
            body(i * ahead + more)
        return carry

    lax.fori_loop(0, g.T // ahead, some, 0)
    for t in range(g.T - g.T % ahead, g.T):
        body(t)


def level_rows(g, r, lh, base=0):
    return pl.ds(base + lh * g.R + r, SUB, stride=g.LH * g.R)


def flux_reader(g, fluxes_ref):
    def flux(dim, r, lh):
        return fluxes_ref[level_rows(g, r, lh, dim * g.tile), :]

    return flux


def join_fluxes(g, mine_ref, other_ref, out_ref):
    first = lax.axis_index("tracer") == 0
    single = lax.axis_size("tracer") != 2
    some = g.R * SUB
    for dim in range(3):
        a, b = (ref[dim * some : (dim + 1) * some, :] for ref in (mine_ref, other_ref))
        at = dim * g.tile
        out_ref[at : at + some, :] = a if single else jnp.where(first, a, b)
        out_ref[at + some : at + 2 * some, :] = b if single else jnp.where(first, b, a)


def load_kernel(
    g, tracers_ref, groups_far, pref_far, field_ref, strips_ref, prey_ref, taste_ref,
    landed, sems, groups_ref, pref_ref, small_sems,
):
    def arrival(t):
        at = pl.ds(pl.multiple_of(t * g.tile, g.tile), g.tile)
        return pltpu.make_async_copy(tracers_ref.at[at, :], landed.at[at, :], sems.at[t])

    small = [
        pltpu.make_async_copy(a, b, small_sems.at[i])
        for i, (a, b) in enumerate(((groups_far, groups_ref), (pref_far, pref_ref)))
    ]
    for copy in small:
        copy.start()
    for t in range(g.T):
        arrival(t).start()
    prey_ref[...] = jnp.zeros_like(prey_ref)

    for copy in small:
        copy.wait()
    for t in range(g.T):
        taste_ref[rows8(t), :] = jnp.full((SUB, 128), pref_ref[groups_ref[t]], jnp.float32)

    def one(t):
        arrival(t).wait()
        taste = taste_of(taste_ref, t)
        base = pl.multiple_of(t * g.tile, g.tile)
        parts = []
        for r in range(g.R):
            for lh in range(g.LH):
                at = (r * g.LH + lh) * SUB
                v = landed[level_rows(g, r, lh, base), :]
                field_ref[pl.ds(base + at, SUB), :] = v
                parts.append(v)
                prey_ref[at : at + SUB, :] += taste * v
        for i, packed in enumerate(pack_strips(parts)):
            strips_ref[rows8(t * g.NV + i), :] = packed

    each_tracer(g, 2, one)


def first_messages_kernel(
    g, field_ref, strips_ref, mine_ref, other_ref, depth_ref, east_ref, north_ref,
    xev_ref, xod_ref, y_ref, extra_ref, fluxes_ref,
):
    x_even = is_even("gx")
    join_fluxes(g, mine_ref, other_ref, fluxes_ref)
    flux = flux_reader(g, fluxes_ref)
    zero = jnp.zeros((SUB, 128), jnp.float32)

    def put(at, low, high):
        xev_ref[at, :] = jnp.where(x_even, high, low)
        xod_ref[at, :] = jnp.where(x_even, low, high)

    def one(t):
        base = pl.multiple_of(t * g.tile, g.tile)
        for i in range(2 * g.LH):
            low = field_ref[pl.ds(base + i * SUB, SUB), :]
            high = field_ref[pl.ds(base + g.tile - 2 * g.L + i * SUB, SUB), :]
            put(rows8(t * 2 * g.LH + i), low, high)

    each_tracer(g, 2, one)
    at = g.T * 2 * g.LH
    for lh in range(g.LH):
        put(rows8(at + lh), zero, flux(0, g.R - 1, lh))
    depth = depth_ref[...].astype(jnp.float32)
    put(rows8(at + g.LH), depth, roll(depth, 2, 0))
    put(rows8(at + g.LH + 1), zero, roll(east_ref[...], 1, 0))
    extras = pack_strips(spread_rows(g, depth))
    extras += pack_strips([flux(1, r, lh) for r in range(g.R) for lh in range(g.LH)])
    extras += pack_strips(spread_rows(g, north_ref[...]))
    for i, packed in enumerate(extras):
        extra_ref[rows8(i), :] = packed
    put_messages(registers(strips_ref) + extras, y_ref)


def wet_levels(g, depths):
    level = [(g.LH * sublanes() + lh).astype(jnp.float32) for lh in range(g.LH)]
    return [[level[lh] < d for lh in range(g.LH)] for d in depths]


def inner_coefficients(g, cf, flux, depth, east, north):
    tab, sub = g.inner, sublanes()
    depths = [spread(depth, r) for r in range(g.R)]
    wet = wet_levels(g, depths)
    wet_before, wet_after = (wet_levels(g, [roll(d, by, 1) for d in depths]) for by in (1, -1))
    for r in range(g.R):
        tab.set(cf, "kx", r + 1, 2.0 * spread(east, r))
        tab.set(cf, "ky", r, 2.0 * roll(spread(north, r), 1, 1))
        tab.set(cf, "kyu", r, 2.0 * spread(north, r))
        flux_z = [flux(2, r, lh) for lh in range(g.LH)]
        for lh in range(g.LH):
            k, here = r * g.LH + lh, wet[r][lh]
            if r:
                opened = here & wet[r - 1][lh]
                tab.set_open(cf, "x", k, opened)
                tab.set_flux(cf, "x", k, opened, flux(0, r - 1, lh))
            opened = here & wet_before[r][lh]
            tab.set_open(cf, "y", k, opened)
            tab.set_flux(cf, "y", k, opened, roll(flux(1, r, lh), 1, 1))
            opened = here & wet_after[r][lh]
            tab.set_open(cf, "yu", k, opened)
            tab.set_flux(cf, "yu", k, opened, flux(1, r, lh))
            opened = here if lh else here & (sub > 0)
            above = flux_z[lh - 1] if lh else roll(flux_z[-1], 1, 0)
            tab.set_open(cf, "z", k, opened)
            tab.set_flux(cf, "z", k, opened, above)


def outer_coefficients(g, cf, extra_x, flux, depth, east):
    tab = g.outer
    depth_low, depth_high = extra_x(g.LH)
    depths = [spread(depth_low, 0), spread(depth_low, 1), spread(depth, 0), spread(depth, g.R - 1)]
    depths += [spread(depth_high, 0), spread(depth_high, 1)]
    wet = wet_levels(g, depths)
    tab.set(cf, "kx", 0, 2.0 * spread(extra_x(g.LH + 1)[0], 0))
    for lh in range(g.LH):
        for face, row in enumerate((0, 1, 3, 4)):
            tab.set_open(cf, "x", face * g.LH + lh, wet[row][lh] & wet[row + 1][lh])
        tab.set_flux(cf, "x", lh, wet[1][lh] & wet[2][lh], extra_x(lh)[0])
        tab.set_flux(cf, "x", g.LH + lh, wet[3][lh] & wet[4][lh], flux(0, g.R - 1, lh))


def strip_coefficients(g, cf, extra_y, extra_ref):
    tab, lane = g.ends, lanes()
    half = (lane // WIDE) % g.LH
    level = (g.LH * sublanes() + half).astype(jnp.float32)
    for i in range(g.NV):
        full = []
        for which in range(3):
            own = which * g.NV + i
            slot = g.T * g.NV + own
            full.append(full_strips(extra_ref[rows8(own), :], *extra_y(slot // SLOTS), slot % SLOTS))
        wet = [level < roll(full[0], -away, 1) for away in (-2, -1, 0, 1, 2)]
        opened = [a & b for a, b in zip(wet, wet[1:])]
        for face in range(4):
            tab.set_open(cf, "s", face * g.NV + i, opened[face])
        for face in range(2):
            flux, kappa = (roll(v, 1 - face, 1) for v in full[1:])
            tab.set_flux(cf, "s", face * g.NV + i, opened[1 + face], flux)
            tab.set(cf, "ks", face * g.NV + i, 2.0 * kappa)


def end_lanes():
    lane = lanes()
    return (lane < 2) | (lane >= 126)


def inside(g, cf, field_ref, part_ref, tend_ref=None, whole_ref=None):
    ends = end_lanes()

    def coef(name, index):
        return g.inner.get(cf, name, index)

    def shift_down(v):
        return [roll(v[-1], 1, 0), *v[:-1]]

    def shift_up(v):
        return [*v[1:], roll(v[0], -1, 0)]

    def one(t):
        base = pl.multiple_of(t * g.tile, g.tile)
        for r in range(g.R):
            index = [r * g.LH + lh for lh in range(g.LH)]
            at = [pl.ds(base + k * SUB, SUB) for k in index]
            cells = [field_ref[a, :] for a in at]
            if whole_ref is not None:
                cells = [c + end_columns(g, tend_ref, t, k) for k, c in zip(index, cells)]
                for a, c in zip(at, cells):
                    whole_ref[a, :] = c
            news = []
            for k, c in zip(index, cells):
                j = coef("hy", k) * (c - roll(c, 1, 1))
                if whole_ref is None:
                    j_up = roll(j, -1, 1)
                else:
                    j_up = coef("hyu", k) * (roll(c, -1, 1) - c)
                s = limited(j, j_up)
                left, right = c + s, c - s
                flow = coef("py", k) * roll(left, 1, 1) + coef("my", k) * right
                flow = flow - coef("ky", r) * j
                if whole_ref is None:
                    flow_up = roll(flow, -1, 1)
                else:
                    flow_up = coef("pyu", k) * left + coef("myu", k) * roll(right, -1, 1)
                    flow_up = flow_up - coef("kyu", r) * j_up
                news.append(c + jnp.where(ends, 0.0, flow - flow_up))
            j = [coef("hz", k) * (c - a) for k, c, a in zip(index, cells, shift_down(cells))]
            s = [limited(a, b) for a, b in zip(j, shift_up(j))]
            above = shift_down([c + v for c, v in zip(cells, s)])
            flow = [
                coef("pz", k) * a + coef("mz", k) * (c - v)
                for k, a, c, v in zip(index, above, cells, s)
            ]
            for a, new, high, low in zip(at, news, flow, shift_up(flow)):
                part_ref[a, :] = new + (high - low)

    return one


def inside_kernel(
    g, ahead, field_ref, fluxes_ref, depth_ref, east_ref, north_ref, part_ref, cf
):
    inner_coefficients(
        g, cf, flux_reader(g, fluxes_ref), depth_ref[...].astype(jnp.float32),
        east_ref[...], north_ref[...],
    )
    each_tracer(g, ahead, inside(g, cf, field_ref, part_ref))


def strip_tendency(g, cf, full, i):
    def coef(name, face):
        return g.ends.get(cf, name, face * g.NV + i)

    cell = [roll(full, -away, 1) for away in (-2, -1, 0, 1, 2)]
    j = [coef("hs", face) * (cell[face + 1] - cell[face]) for face in range(4)]
    s = [limited(a, b) for a, b in zip(j, j[1:])]
    flow = [
        coef("ps", f) * (cell[f + 1] + s[f])
        + coef("ms", f) * (cell[f + 2] - s[f + 1])
        - coef("ks", f) * j[f + 1]
        for f in range(2)
    ]
    tend = flow[0] - flow[1]
    place = lanes() % WIDE
    tend = jnp.where(place < 10, tend, roll(tend, 8, 1))
    return jnp.where((place >= 8) & (place < 12), tend, 0.0)


def all_strip_tendencies(g, cf, strips_ref, sides, tend_ref):
    for n in range(g.T * g.NV):
        full = full_strips(strips_ref[rows8(n), :], *sides(n // SLOTS), n % SLOTS)
        tend_ref[rows8(n), :] = strip_tendency(g, cf, full, n % g.NV)


def end_columns(g, tend_ref, t, k):
    v, n = divmod(k, EACH)
    return jnp.where(end_lanes(), roll(tend_ref[rows8(t * g.NV + v), :], -(WIDE * n + 10), 1), 0.0)


def set_factor(g, total, factor, grazers_ref, prey_refs):
    for r in range(g.R):
        for lh in range(g.LH):
            at = rows8(r * g.LH + lh)
            prey = sum(ref[at, :] for ref in prey_refs)
            grazers = grazers_ref[level_rows(g, r, lh), :]
            factor[at, :] = grazers / (1.0 + 4.0 * prey / total)


def finish(g, inner, outer, t, field_ref, part_ref, sides, emit):
    base = pl.multiple_of(t * g.tile, g.tile)

    def cell(r, lh):
        if 0 <= r < g.R:
            return field_ref[pl.ds(base + (r * g.LH + lh) * SUB, SUB), :]
        i = r + 2 if r < 0 else r - g.R
        return sides(t * 2 * g.LH + i * g.LH + lh)[0 if r < 0 else 1]

    def coef(name, f, lh):
        if 0 < f < g.R:
            return g.inner.get(inner, name, f * g.LH + lh)
        if name == "hx":
            return g.outer.get(outer, name, {-1: 0, 0: 1, g.R: 2, g.R + 1: 3}[f] * g.LH + lh)
        return g.outer.get(outer, name, (g.LH if f else 0) + lh)

    state = [None] * g.LH
    for f in range(-1, g.R + 2):
        for lh in range(g.LH):
            if f < 0:
                below = cell(-2, lh)
                here = cell(-1, lh)
                state[lh] = (here, coef("hx", f, lh) * (here - below), None, None)
                continue
            c, j, left, carried = state[lh]
            up = cell(f, lh)
            j_up = coef("hx", f, lh) * (up - c)
            s = limited(j, j_up)
            if f > 0:
                kap = g.inner.get(inner, "kx", f - 1) if f > 1 else g.outer.get(outer, "kx", 0)
                flow = coef("px", f - 1, lh) * left + coef("mx", f - 1, lh) * (c - s) - kap * j
                if f > 1:
                    r = f - 2
                    k = r * g.LH + lh
                    old = cell(r, lh)
                    new = part_ref[pl.ds(base + k * SUB, SUB), :] + (carried - flow)
                    emit(r, lh, old, new)
                carried = flow
            state[lh] = (up, j_up, c + s, carried)


def reader(even, ev_ref, od_ref):
    def sides(i):
        at = rows8(i)
        return split_sides(even, ev_ref[at, :], od_ref[at, :])

    return sides


def border_kernel(
    g, total, ahead,
    field_ref, part_ref, xev_ref, xod_ref, inner, fluxes_ref, depth_ref, east_ref,
    grazers_ref, taste_ref, *rest,
):
    prey_refs, (out_ref, strips_ref, prey_ref, outer, factor) = rest[:-5], rest[-5:]
    x_sides = reader(is_even("gx"), xev_ref, xod_ref)
    outer_coefficients(
        g, outer, lambda i: x_sides(g.T * 2 * g.LH + i), flux_reader(g, fluxes_ref),
        depth_ref[...].astype(jnp.float32), east_ref[...],
    )
    set_factor(g, total, factor, grazers_ref, prey_refs)
    prey_ref[...] = jnp.zeros_like(prey_ref)

    def one(t):
        taste = taste_of(taste_ref, t)
        base = pl.multiple_of(t * g.tile, g.tile)
        news = {}

        def emit(r, lh, old, new):
            at = (r * g.LH + lh) * SUB
            new = new - (taste * factor[at : at + SUB, :]) * old
            out_ref[pl.ds(base + at, SUB), :] = new
            prey_ref[at : at + SUB, :] += taste * new
            news[r, lh] = new

        finish(g, inner, outer, t, field_ref, part_ref, x_sides, emit)
        parts = [news[r, lh] for r in range(g.R) for lh in range(g.LH)]
        for i, packed in enumerate(pack_strips(parts)):
            strips_ref[rows8(t * g.NV + i), :] = packed

    each_tracer(g, ahead, one)


def second_messages_kernel(
    g, field_ref, strips_ref, next_ref, prey_ref, extra_ref, yev_ref, yod_ref, taste_ref,
    xev2_ref, xod2_ref, y2_ref, strips2_ref, prey2_ref, tend_ref, ends, grazed,
):
    x_even = is_even("gx")
    y_sides = reader(is_even("gy"), yev_ref, yod_ref)
    strip_coefficients(g, ends, y_sides, extra_ref)
    all_strip_tendencies(g, ends, strips_ref, y_sides, tend_ref)
    packed = [next_ref[rows8(n), :] + tend_ref[rows8(n), :] for n in range(g.T * g.NV)]
    for n, one_packed in enumerate(packed):
        strips2_ref[rows8(n), :] = one_packed
    put_messages(packed, y2_ref)
    for i in range(g.NV):
        grazed[rows8(i), :] = sum(
            taste_of(taste_ref, t) * tend_ref[rows8(t * g.NV + i), :] for t in range(g.T)
        )
    for k in range(g.K):
        prey2_ref[rows8(k), :] = prey_ref[rows8(k), :] + end_columns(g, grazed, 0, k)

    def one(t):
        for i in range(2 * g.LH):
            j = i + (g.R - 2) * g.LH
            low, high = (
                field_ref[rows8(t * g.K + k), :] + end_columns(g, tend_ref, t, k) for k in (i, j)
            )
            at = rows8(t * 2 * g.LH + i)
            xev2_ref[at, :] = jnp.where(x_even, high, low)
            xod2_ref[at, :] = jnp.where(x_even, low, high)

    each_tracer(g, 6, one)


def transport_two_kernel(
    g, total, ahead, field_ref, tend_ref, xev_ref, xod_ref, inner, outer, grazers_ref, taste_ref, *rest
):
    prey_refs, (out_ref, whole_ref, part_ref, factor) = rest[:-4], rest[-4:]
    set_factor(g, total, factor, grazers_ref, prey_refs)
    x_sides = reader(is_even("gx"), xev_ref, xod_ref)
    early = inside(g, inner, field_ref, part_ref, tend_ref, whole_ref)

    def late(t):
        taste = taste_of(taste_ref, t)

        def emit(r, lh, old, new):
            k = r * g.LH + lh
            out_ref[rows8(t * g.K + k), :] = new - (taste * factor[rows8(k), :]) * old

        finish(g, inner, outer, t, whole_ref, part_ref, x_sides, emit)

    def group(body, i):
        for more in range(ahead):
            body(i * ahead + more)

    def both(i, carry):
        group(late, i - 1)
        group(early, i)
        return carry

    groups = g.T // ahead
    group(early, 0)
    lax.fori_loop(1, groups, both, 0)
    group(late, groups - 1)
    for t in range(groups * ahead, g.T):
        early(t)
        late(t)


def result_kernel(
    g, ahead, field_ref, strips_ref, yod_ref, yev_ref, ends, out_ref, tend_ref, leaving, sems
):
    y_sides = reader(is_even("gy"), yev_ref, yod_ref)
    all_strip_tendencies(g, ends, strips_ref, y_sides, tend_ref)

    def departure(t):
        at = pl.ds(pl.multiple_of(t * g.tile, g.tile), g.tile)
        return pltpu.make_async_copy(leaving.at[at, :], out_ref.at[at, :], sems.at[t])

    def one(t):
        base = pl.multiple_of(t * g.tile, g.tile)
        for r in range(g.R):
            for lh in range(g.LH):
                k = r * g.LH + lh
                new = field_ref[rows8(t * g.K + k), :] + end_columns(g, tend_ref, t, k)
                leaving[level_rows(g, r, lh, base), :] = new
        departure(t).start()

    each_tracer(g, ahead, one)
    for t in range(g.T):
        departure(t).wait()


def call(body, outs, operands, far=0, far_out=False, scratch=()):
    spaces = [pltpu.HBM if i < far else pltpu.VMEM for i in range(len(operands))]
    operands = [
        pltpu.with_memory_space_constraint(a, space) if space == pltpu.HBM else a
        for a, space in zip(operands, spaces)
    ]
    return pl.pallas_call(
        body,
        out_shape=[jax.ShapeDtypeStruct((rows, 128), jnp.float32) for rows in outs],
        in_specs=[pl.BlockSpec(memory_space=space) for space in spaces],
        out_specs=[pl.BlockSpec(memory_space=pltpu.HBM if far_out else pltpu.VMEM)] * len(outs),
        scratch_shapes=[
            pltpu.VMEM((rows, 128), jnp.float32) if isinstance(rows, int) else rows
            for rows in scratch
        ],
        compiler_params=pltpu.CompilerParams(vmem_limit_bytes=LIM),
    )(*operands)


def pair_swap(values, axis, start):
    pairs = []
    for i in range(start, lax.axis_size(axis) - 1, 2):
        pairs += [(i, i + 1), (i + 1, i)]
    if not pairs:
        return jnp.zeros_like(values)
    return lax.ppermute(values, axis, pairs)


def tracer_swap(values):
    return lax.ppermute(values, "tracer", [(0, 1), (1, 0)])


def all_prey(values):
    if lax.axis_size("tracer") == 2:
        return [values, tracer_swap(values)]
    return [lax.psum(values, "tracer")]


def neighbours(x_ev, x_od, y):
    y_ev, y_od = pair_swap(y, "gy", 0), pair_swap(y, "gy", 1)
    return pair_swap(x_ev, "gx", 0), pair_swap(x_od, "gx", 1), y_ev, y_od


def on_device(tracers, fluxes, diff_east, diff_north, column_depth, grazers, groups, preference):
    tr_dev, levels, rows, cols = tracers.shape
    parts = lax.axis_size("tracer")
    if not (cols == 128 and rows == SUB and levels == 2 * SUB and tr_dev % 2 == 0):
        return plain(
            tracers, fluxes, diff_east, diff_north, column_depth, grazers, groups, preference
        )
    g = Geo(tr_dev, levels, rows, cols)
    total = float(tr_dev * parts)
    flat = tracers.reshape(-1, cols)
    grazers = grazers.reshape(-1, cols)
    cells = g.T * g.tile
    copies = pltpu.SemaphoreType.DMA((g.T,))

    if parts == 2:
        mine = fluxes.reshape(-1, cols)
        other = tracer_swap(mine)
    else:
        gathered = lax.all_gather(fluxes, "tracer", axis=1, tiled=True)
        mine, other = (gathered[:, i : i + SUB].reshape(-1, cols) for i in (0, SUB))
    field, strips, prey, taste = call(
        functools.partial(load_kernel, g),
        [cells, g.T * g.SR, g.T * 2 * g.L + g.L + 3 * SUB, g.T * SUB],
        [flat, groups, preference],
        far=3,
        scratch=[cells, copies, pltpu.SMEM(groups.shape, groups.dtype),
                 pltpu.SMEM(preference.shape, preference.dtype), pltpu.SemaphoreType.DMA((2,))],
    )
    prey = all_prey(prey)
    x_rows = g.T * 2 * g.L
    x_more = x_rows + g.L + 2 * SUB
    *messages, extra, fluxes = call(
        functools.partial(first_messages_kernel, g),
        [x_more, x_more, g.my1 * SUB, 3 * g.SR, 3 * g.tile],
        [field, strips, mine, other, column_depth, diff_east, diff_north],
    )
    messages = neighbours(*messages)
    part, inner = call(
        functools.partial(inside_kernel, g, INSIDE),
        [cells, g.inner.rows],
        [field, fluxes, column_depth, diff_east, diff_north],
    )
    field, next_strips, next_prey, outer = call(
        functools.partial(border_kernel, g, total, FINISH),
        [cells, g.T * g.SR, g.tile, g.outer.rows],
        [field, part, *messages[:2], inner, fluxes, column_depth, diff_east, grazers, taste,
         *prey],
        scratch=[g.tile],
    )
    *messages, strips, prey, tend, ends = call(
        functools.partial(second_messages_kernel, g),
        [x_rows, x_rows, g.my2 * SUB, g.T * g.SR, g.tile, g.T * g.SR, g.ends.rows],
        [field, strips, next_strips, next_prey, extra, *messages[2:], taste],
        scratch=[g.SR],
    )
    prey = all_prey(prey)
    messages = neighbours(*messages)
    messages = messages[0], messages[1], messages[3], messages[2]
    (field,) = call(
        functools.partial(transport_two_kernel, g, total, BOTH),
        [cells],
        [field, tend, *messages[:2], inner, outer, grazers, taste, *prey],
        scratch=[cells, cells, g.tile],
    )
    (out,) = call(
        functools.partial(result_kernel, g, LAST),
        [cells],
        [field, strips, *messages[2:], ends],
        far_out=True,
        scratch=[g.T * g.SR, cells, copies],
    )
    return out.reshape(tracers.shape)


def solution(mesh):
    placed = (
        P("tracer", None, "gx", "gy"),
        P(None, "tracer", "gx", "gy"),
        P("gx", "gy"),
        P("gx", "gy"),
        P("gx", "gy"),
        P(None, "gx", "gy"),
        P("tracer"),
        P(),
    )
    return jax.shard_map(
        on_device,
        mesh=mesh,
        in_specs=placed,
        out_specs=P("tracer", None, "gx", "gy"),
        check_vma=False,
    )
```
